32 devices in a mesh: frame: 4 (over z), space: 4 (over y, core), tensor: 2 (over x).
Axes of the slice: x: 2, y: 2, z: 4, core: 2. Of those that a mesh axis runs over, the one named last changes fastest.
Arguments:
- inputs: bfloat16 [2, 8, 576, 2048], P(None, 'frame', 'space'), may hold values from -6 to 6
- upstream: bfloat16 [2, 8, 576, 2048], P(None, 'frame', 'space'), may hold values from -6 to 6
- action_ids: int32 [2, 8], P(None, 'frame'), may hold values from 0 to 7
- frame_time: int32 [2, 8], replicated, may hold values from 0 to 7, each once within a row
- action_table: float32 [8, 2048], replicated, may hold values from -3 to 3
- gain: float32 [2048], replicated, may hold values from 0.5 to 1.5
- w_qkv: bfloat16 [2048, 3, 2048], P(('frame', 'space'), None, 'tensor'), may hold values from -1 to 1
- w_out: bfloat16 [2048, 2048], P(('frame', 'space'), 'tensor'), may hold values from -0.125 to 0.125
Outputs:
- grad_inputs: bfloat16 [2, 8, 576, 2048], P(None, 'frame', 'space')
- grad_qkv: float32 [2048, 3, 2048], P(('frame', 'space'), None, 'tensor')
- grad_out_proj: float32 [2048, 2048], P(('frame', 'space'), 'tensor')
- grad_gain: float32 [2048], replicated
- grad_actions: float32 [8, 2048], replicated
The draws below stay inside these ranges and needn't reach their ends.
All inputs are finite; a program needn't handle non-finite values.
Results may differ from the reference program's by a relative error of at most 0.018.
The reference program's roundings to bfloat16 on the way (of `normed`, `merged_qkv`, `grad_heads`, `rounded`, `mixed_out` and `grad_merged`) count: a program that leaves them out, or rounds other values in their place, can miss the bound.
Values may be sent and summed in bfloat16 or wider, within the bound.
No kernel may reach another device: no remote copies, remote signals or barrier semaphores. Data moves between devices by JAX's collectives and lax.ppermute only.
A program may use at most 128 MiB of HBM per device.

```python
import math
import jax
import jax.numpy as jnp
from jax import lax

D = 2048
HEADS = 16
HEAD = 128
ACTIONS = 8
BATCH = 2
FRAMES = 8
SPATIAL = 576


def draw_w_qkv(key, part):
    key = jax.random.fold_in(key, 7)
    base_key = jax.random.fold_in(key, 0)
    bound = 6.0 * D ** (-0.5)
    base = jax.random.normal(base_key, (D, 3, HEADS * HEAD), jnp.float32) * D ** (-0.5)
    base = jnp.clip(base, -bound, bound)
    base = jnp.clip(base, -1.0, 1.0)
    return base.astype(jnp.bfloat16)


def place_ends(entries, stream_key, low, top_value):
    longest = entries.shape.index(max(entries.shape))
    spots = []
    for shift in (0, 1):
        where = [jax.random.randint(jax.random.fold_in(stream_key, axis), (), 0, length) for axis, length in enumerate(entries.shape)]
        where[longest] = (where[longest] + shift) % entries.shape[longest]
        spots.append(tuple(where))
    return entries.at[spots[0]].set(low).at[spots[1]].set(top_value)


def spiked(drawn, own_key, source, target, parts, factor):
    owner, partner = [(jnp.arange(drawn.shape[axis_at]) // (drawn.shape[axis_at] // parts)).reshape([-1 if axis == axis_at else 1 for axis in range(drawn.ndim)]) for axis_at in (source, target)]
    chosen = jax.random.permutation(own_key, parts)[partner]
    strong = (owner == chosen) | (owner == (partner + parts // 2) % parts)
    return jnp.where(strong, factor * drawn, drawn)


def levels(own_key, extent, pieces, low, largest):
    def one(position, blocks):
        draws = jax.random.uniform(jax.random.fold_in(jax.random.fold_in(own_key, 6), position), (blocks,), jnp.float32, low / len(pieces), largest / len(pieces))
        return jnp.repeat(jnp.exp(draws), extent[position] // blocks).reshape((-1,) + (1,) * (len(extent) - position - 1))

    level = one(*pieces[0])
    for cut in pieces[1:]:
        level = level * one(*cut)
    return level


def centred(key, shape, spread, most, shards=(), kind=jnp.bfloat16):
    result = jax.random.normal(key, shape, jnp.float32) * spread
    if len(shards) > 0:
        result = levels(key, shape, shards, -0.22, 0.18) * result
    return jnp.clip(result, min=-most, max=most).astype(kind)


def gaussian_with(own_key, dims, spread, reach, cuts, heavy, kind=jnp.bfloat16):
    drawn = spread * jax.random.normal(own_key, dims, jnp.float32)
    if cuts:
        drawn = drawn * levels(own_key, dims, cuts, -0.22, 0.18)
    return jnp.clip(spiked(drawn, jax.random.fold_in(own_key, 3), *heavy), -reach, reach).astype(kind)


def setup_inputs(seed: int = 0) -> dict:
    arg_keys = jax.random.split(jax.random.key(seed), 9)
    inputs = gaussian_with(arg_keys[0], (BATCH, FRAMES, SPATIAL, D), 1.0, 6.0, ((1, 4), (2, 4)), (2, 3, 4, 2.0))
    upstream = gaussian_with(arg_keys[1], (BATCH, FRAMES, SPATIAL, D), 1.0, 6.0, ((1, 4), (2, 4)), (1, 3, 4, 2.0))
    action_ids = place_ends(jax.random.randint(arg_keys[2], (BATCH, FRAMES), 0, ACTIONS), jax.random.fold_in(arg_keys[2], 1), 0, ACTIONS - 1).astype(jnp.int32)
    frame_time = jax.vmap(lambda own: jax.random.permutation(own, FRAMES))(jax.random.split(arg_keys[3], BATCH)).reshape((BATCH, FRAMES)).astype(jnp.int32)
    action_table = centred(arg_keys[4], (ACTIONS, D), 0.5, 3.0, (), jnp.float32)
    gain = jnp.clip(1.0 + 0.1 * jax.random.normal(arg_keys[5], (D,), jnp.float32), 0.5, 1.5)
    w_qkv = draw_w_qkv(jax.random.fold_in(arg_keys[8], 71), 0)
    w_out = centred(arg_keys[7], (D, HEADS * HEAD), (HEADS * HEAD) ** -0.5, 0.125, ((0, 16), (1, 2)))
    return {"inputs": inputs, "upstream": upstream, "action_ids": action_ids, "frame_time": frame_time, "action_table": action_table, "gain": gain, "w_qkv": w_qkv, "w_out": w_out}


NORM_EPSILON = 1e-06

def normalize(inputs, action_ids, action_table, gain):
    action_count = action_table.shape[0]
    onehot = (action_ids[..., None] == jnp.arange(action_count, dtype=jnp.int32)).astype(jnp.float32)
    embedded = jnp.einsum('bfa,ad->bfd', onehot, action_table, precision=lax.Precision.HIGHEST)
    hidden = inputs.astype(jnp.float32) + embedded[:, :, None, :]
    inverse = lax.rsqrt(lax.optimization_barrier(jnp.mean(hidden * hidden, -1, keepdims=True)) + NORM_EPSILON)
    unit_rows = hidden * inverse
    normed = (unit_rows * gain).astype(jnp.bfloat16)
    return (onehot, inverse, unit_rows, normed)

def temporal_attention(merged_qkv, grad_heads, frame_time, head_size):
    batch_count, frame_count, space_count, channel_count = merged_qkv.shape
    head_width = channel_count // 3
    head_count = head_width // head_size
    split_parts = merged_qkv.reshape(batch_count, frame_count, space_count, 3, head_count, head_size).astype(jnp.float32)
    queries = split_parts[:, :, :, 0]
    key_rows = split_parts[:, :, :, 1]
    value_rows = split_parts[:, :, :, 2]
    score_scale = 1.0 / math.sqrt(head_size)
    scores = jnp.einsum('bqshd,bkshd->bshqk', queries, key_rows) * score_scale
    allowed = frame_time[:, None, None, None, :] <= frame_time[:, None, None, :, None]
    scores = jnp.where(allowed, scores, -1e+30)
    row_maxima = lax.optimization_barrier(jnp.max(scores, -1, keepdims=True))
    exponent = jnp.exp(scores - row_maxima)
    probabilities = exponent / lax.optimization_barrier(jnp.sum(exponent, -1, keepdims=True))
    rounded = lax.optimization_barrier(probabilities.astype(jnp.bfloat16)).astype(jnp.float32)
    mixed_out = jnp.einsum('bshqk,bkshd->bqshd', rounded, value_rows)
    mixed_out = mixed_out.reshape(batch_count, frame_count, space_count, head_width).astype(jnp.bfloat16)
    grad_rows = grad_heads.reshape(batch_count, frame_count, space_count, head_count, head_size).astype(jnp.float32)
    grad_probs = jnp.einsum('bqshd,bkshd->bshqk', grad_rows, value_rows)
    grad_values = jnp.einsum('bshqk,bqshd->bkshd', rounded, grad_rows)
    grad_scores = probabilities * (grad_probs - lax.optimization_barrier(jnp.sum(grad_probs * probabilities, -1, keepdims=True)))
    grad_queries = jnp.einsum('bshqk,bkshd->bqshd', grad_scores, key_rows) * score_scale
    grad_keys = jnp.einsum('bshqk,bqshd->bkshd', grad_scores, queries) * score_scale
    grad_merged = jnp.stack([grad_queries, grad_keys, grad_values], 3)
    grad_merged = grad_merged.reshape(batch_count, frame_count, space_count, channel_count).astype(jnp.bfloat16)
    return (mixed_out, grad_merged)

def norm_backward(grad_norm, unit_rows, inverse, upstream_rows, row_onehot, gain):
    scaled = grad_norm * gain
    grad_hidden = upstream_rows.astype(jnp.float32) + inverse * (scaled - unit_rows * lax.optimization_barrier(jnp.mean(scaled * unit_rows, -1, keepdims=True)))
    gain_term = lax.optimization_barrier(jnp.sum(grad_norm * unit_rows, 0))
    action_term = jnp.einsum('ra,rd->ad', row_onehot, grad_hidden, precision=lax.Precision.HIGHEST)
    return (grad_hidden, gain_term, action_term)

def reference(inputs, upstream, action_ids, frame_time, action_table, gain, w_qkv, w_out):
    batch_count, frame_count, space_count, feature_count = inputs.shape
    row_count = batch_count * frame_count * space_count
    channel_count = w_out.shape[1]
    onehot, inverse, unit_rows, normed = normalize(inputs, action_ids, action_table, gain)
    flat_norm = normed.reshape(row_count, feature_count)
    flat_up = upstream.reshape(row_count, feature_count)
    weight_flat = w_qkv.reshape(feature_count, 3 * channel_count)
    merged_qkv = jnp.dot(flat_norm, weight_flat, preferred_element_type=jnp.float32).astype(jnp.bfloat16)
    merged_qkv = merged_qkv.reshape(batch_count, frame_count, space_count, 3 * channel_count)
    grad_heads = jnp.dot(flat_up, w_out, preferred_element_type=jnp.float32).astype(jnp.bfloat16)
    grad_heads = grad_heads.reshape(batch_count, frame_count, space_count, channel_count)
    mixed_out, grad_merged = temporal_attention(merged_qkv, grad_heads, frame_time, HEAD)
    flat_mixed = mixed_out.reshape(row_count, channel_count)
    flat_grads = grad_merged.reshape(row_count, 3 * channel_count)
    grad_out_proj = jnp.dot(flat_up.T, flat_mixed, preferred_element_type=jnp.float32)
    grad_qkv = jnp.dot(flat_norm.T, flat_grads, preferred_element_type=jnp.float32).reshape(feature_count, 3, channel_count)
    grad_norm = jnp.dot(flat_grads, weight_flat.T, preferred_element_type=jnp.float32)
    row_onehot = jnp.broadcast_to(onehot[:, :, None, :], (batch_count, frame_count, space_count, onehot.shape[2])).reshape(row_count, onehot.shape[2])
    grad_hidden, grad_gain, grad_actions = norm_backward(grad_norm, unit_rows.reshape(row_count, feature_count), inverse.reshape(row_count, 1), flat_up, row_onehot, gain)
    grad_inputs = grad_hidden.astype(jnp.bfloat16).reshape(inputs.shape)
    return (grad_inputs, grad_qkv, grad_out_proj, grad_gain, grad_actions)
```

```python
import functools
import math

import jax
import jax.numpy as jnp
from jax import lax
from jax.experimental import pallas as pl
from jax.experimental.pallas import tpu as pltpu
from jax.sharding import PartitionSpec as P

HEAD = 128
NORM_EPSILON = 1e-06
UPSTREAM_TOP = 6.0
WIRE = jnp.float16
WIRE_TOP = 32768.0


def dot_nt(a, b):
    return lax.dot_general(a, b, (((1,), (1,)), ((), ())), preferred_element_type=jnp.float32)


def dot_nn(a, b):
    return lax.dot_general(a, b, (((1,), (0,)), ((), ())), preferred_element_type=jnp.float32)


def dot_tn(a, b):
    return lax.dot_general(a, b, (((0,), (0,)), ((), ())), preferred_element_type=jnp.float32)


def attention_kernel(
    late_ref, early_ref, qkv_ref, grad_ref, mixed_ref, merged_ref, peak_qkv_ref, peak_out_ref
):
    frames, group, width = grad_ref.shape
    rows = frames * group
    scale = 1.0 / math.sqrt(HEAD)

    def load(ref, start):
        block = ref[:, :, start : start + HEAD]
        if group % 16:
            return block.astype(jnp.float32).reshape(rows, HEAD).astype(jnp.bfloat16)
        return block.reshape(rows, HEAD)

    def store(ref, start, value):
        if group % 16:
            ref[:, :, start : start + HEAD] = value.reshape(frames, group, HEAD).astype(
                jnp.bfloat16
            )
        else:
            ref[:, :, start : start + HEAD] = value.astype(jnp.bfloat16).reshape(
                frames, group, HEAD
            )

    def peak(value):
        return jnp.max(jnp.abs(value).reshape(rows // 8, 8, HEAD), axis=0)

    @pl.when(pl.program_id(0) == 0)
    def _():
        peak_qkv_ref[...] = jnp.zeros_like(peak_qkv_ref)
        peak_out_ref[...] = jnp.zeros_like(peak_out_ref)

    row_id = lax.broadcasted_iota(jnp.int32, (rows, rows), 0)
    col_id = lax.broadcasted_iota(jnp.int32, (rows, rows), 1)
    allowed = (row_id % group == col_id % group) & (early_ref[...] <= late_ref[...])
    for start in range(0, width, HEAD):
        query = load(qkv_ref, start)
        key = load(qkv_ref, width + start)
        value = load(qkv_ref, 2 * width + start)
        grad = load(grad_ref, start)
        scores = jnp.where(allowed, dot_nt(query, key) * scale, -1e30)
        exponent = jnp.exp(scores - jnp.max(scores, -1, keepdims=True))
        probabilities = exponent / jnp.sum(exponent, -1, keepdims=True)
        rounded = probabilities.astype(jnp.bfloat16)
        mixed = dot_nn(rounded, value)
        grad_probs = dot_nt(grad, value)
        grad_value = dot_tn(rounded, grad)
        grad_scores = probabilities * (
            grad_probs - jnp.sum(grad_probs * probabilities, -1, keepdims=True)
        )
        high = grad_scores.astype(jnp.bfloat16)
        low = (grad_scores - high.astype(jnp.float32)).astype(jnp.bfloat16)
        grad_query = (dot_nn(high, key) + dot_nn(low, key)) * scale
        grad_key = (dot_tn(high, query) + dot_tn(low, query)) * scale
        store(mixed_ref, start, mixed)
        store(merged_ref, start, grad_query)
        store(merged_ref, width + start, grad_key)
        store(merged_ref, 2 * width + start, grad_value)
        peak_out_ref[...] = jnp.maximum(peak_out_ref[...], peak(mixed))
        top = jnp.maximum(jnp.maximum(peak(grad_query), peak(grad_key)), peak(grad_value))
        peak_qkv_ref[...] = jnp.maximum(peak_qkv_ref[...], top)


def temporal_attention(qkv, grad_heads, times):
    frames, pairs, width = grad_heads.shape
    group = 16 if pairs % 16 == 0 else 8
    rows = frames * group
    per_row = jnp.repeat(times.astype(jnp.float32), group)
    work = pairs // group * rows * rows * (width // HEAD)
    fixed = lambda i: (0, 0)
    moving = lambda i: (0, i, 0)
    return pl.pallas_call(
        attention_kernel,
        grid=(pairs // group,),
        in_specs=[
            pl.BlockSpec((rows, 1), fixed),
            pl.BlockSpec((1, rows), fixed),
            pl.BlockSpec((frames, group, 3 * width), moving),
            pl.BlockSpec((frames, group, width), moving),
        ],
        out_specs=[
            pl.BlockSpec((frames, group, width), moving),
            pl.BlockSpec((frames, group, 3 * width), moving),
            pl.BlockSpec((8, HEAD), fixed),
            pl.BlockSpec((8, HEAD), fixed),
        ],
        out_shape=[
            jax.ShapeDtypeStruct((frames, pairs, width), jnp.bfloat16),
            jax.ShapeDtypeStruct((frames, pairs, 3 * width), jnp.bfloat16),
            jax.ShapeDtypeStruct((8, HEAD), jnp.float32),
            jax.ShapeDtypeStruct((8, HEAD), jnp.float32),
        ],
        compiler_params=pltpu.CompilerParams(vmem_limit_bytes=40 * 1024 * 1024),
        cost_estimate=pl.CostEstimate(
            flops=16 * work * HEAD,
            bytes_accessed=16 * frames * pairs * width,
            transcendentals=work,
        ),
        name="temporal_attention",
    )(per_row[:, None], per_row[None, :], qkv, grad_heads)


def on_device(
    depth, spaces, tensors, inputs, upstream, action_ids, frame_time, action_table, gain, w_qkv, w_out
):
    batch, local_frames, local_space, features = inputs.shape
    actions = action_table.shape[0]
    shard_rows, _, channels = w_qkv.shape
    z = lax.axis_index("frame")
    s = lax.axis_index("space")
    x = lax.axis_index("tensor")
    y, core = s // 2, s % 2
    frames = depth * local_frames
    pairs = batch * local_space // depth
    slots = depth // batch
    slice_width = features // tensors
    head_width = channels // 2
    width = 4 * head_width
    tokens = frames * 2 * pairs

    def ring(value, shift):
        return lax.ppermute(value, "frame", [(i, (i + shift) % depth) for i in range(depth)])

    def swap_z(value, bit):
        return lax.ppermute(value, "frame", [(i, i ^ bit) for i in range(depth)])

    def swap_core(value):
        return lax.ppermute(value, "space", [(i, i ^ 1) for i in range(spaces)])

    def swap_y(value):
        return lax.ppermute(value, "space", [(i, i ^ 2) for i in range(spaces)])

    def swap_x(value):
        return lax.ppermute(value, "tensor", [(0, 1), (1, 0)])

    def join_x(own):
        if tensors == 2:
            other = swap_x(own)
            first = jnp.where(x == 0, own, other)
            second = jnp.where(x == 0, other, own)
            return jnp.concatenate([first, second], -1)
        return lax.all_gather(own, "tensor", axis=own.ndim - 1, tiled=True)

    def cut_x(value, which=None):
        which = x if which is None else which
        return lax.dynamic_slice_in_dim(value, which * slice_width, slice_width, value.ndim - 1)

    def place(j):
        return j // slots, (j % slots) * pairs

    stacked = jnp.concatenate([w_qkv, w_out[:, None, :]], 1)
    halves = stacked.reshape(shard_rows, 4, 2, head_width)

    def core_half(which):
        return lax.dynamic_index_in_dim(halves, which, 2, keepdims=False).reshape(
            shard_rows, width
        )

    mine, other = core_half(core), swap_core(core_half(1 - core))
    block = jnp.concatenate(
        [jnp.where(core == 0, mine, other), jnp.where(core == 0, other, mine)], 0
    )
    block_rows = 2 * shard_rows
    weights = jnp.zeros((features, width), jnp.bfloat16)
    for k in range(depth):
        if k:
            block = ring(block, 1)
        start = (z - k) % depth * (2 * block_rows)
        weights = lax.dynamic_update_slice(weights, block, (start + y * block_rows, 0))
        weights = lax.dynamic_update_slice(
            weights, swap_y(block), (start + (1 - y) * block_rows, 0)
        )
    weight_qkv, weight_out = weights[:, : 3 * head_width], weights[:, 3 * head_width :]

    def collect(rows):
        parts = []
        for k in range(depth):
            rollout, first = place((z + k) % depth)
            if k == 0:
                parts.append(
                    lax.dynamic_slice(
                        rows, (rollout, 0, first, 0), (1, local_frames, pairs, features)
                    )[0]
                )
            else:
                piece = lax.dynamic_slice(
                    rows,
                    (rollout, 0, first, x * slice_width),
                    (1, local_frames, pairs, slice_width),
                )[0]
                parts.append(join_x(ring(piece, k)))
        return jnp.concatenate(parts, 0)

    own_inputs = collect(inputs)
    own_upstream = collect(upstream)
    rollout, _ = place(z)
    ids = jnp.concatenate(
        [
            lax.dynamic_index_in_dim(
                ring(action_ids, k) if k else action_ids, rollout, 0, keepdims=False
            )
            for k in range(depth)
        ]
    )
    order = (
        (z - jnp.arange(depth, dtype=jnp.int32)[:, None]) % depth * local_frames
        + jnp.arange(local_frames, dtype=jnp.int32)[None, :]
    ).reshape(frames)
    own_time = lax.dynamic_index_in_dim(frame_time, rollout, 0, keepdims=False)
    times = jnp.sum(
        jnp.where(
            order[:, None] == jnp.arange(frames, dtype=jnp.int32)[None, :], own_time[None, :], 0
        ),
        1,
    )
    onehot = (ids[:, None] == jnp.arange(actions, dtype=jnp.int32)[None, :]).astype(jnp.float32)
    embedded = jnp.dot(onehot, action_table, precision=lax.Precision.HIGHEST)
    hidden = own_inputs.astype(jnp.float32) + embedded[:, None, :]
    inverse = lax.rsqrt(jnp.mean(hidden * hidden, -1, keepdims=True) + NORM_EPSILON)
    normed = (hidden * inverse * gain).astype(jnp.bfloat16)

    def both(own):
        return jnp.concatenate([own, swap_core(own)], 1).reshape(tokens, features)

    all_upstream = both(own_upstream)
    all_normed = both(normed)
    qkv = dot_nn(all_normed, weight_qkv).astype(jnp.bfloat16)
    grad_heads = dot_nn(all_upstream, weight_out).astype(jnp.bfloat16)
    mixed, merged, peak_qkv, peak_out = temporal_attention(
        qkv.reshape(frames, 2 * pairs, 3 * head_width),
        grad_heads.reshape(frames, 2 * pairs, head_width),
        times,
    )
    flat_mixed = mixed.reshape(tokens, head_width)
    flat_merged = merged.reshape(tokens, 3 * head_width)

    def norm_part(rows):
        flat = rows.reshape(frames * pairs, 3 * head_width)
        return dot_nt(flat, weight_qkv).reshape(frames, pairs, features)

    sent = swap_core(norm_part(merged[:, pairs:]))
    partial_norm = norm_part(merged[:, :pairs]) + sent
    row_dot = jnp.sum(partial_norm * gain * (hidden * inverse), -1, keepdims=True)
    if tensors == 2:
        row_dot = row_dot + swap_x(row_dot)
        grad_norm = cut_x(partial_norm) + swap_x(cut_x(partial_norm, 1 - x))
    else:
        row_dot = lax.psum(row_dot, "tensor")
        grad_norm = lax.psum_scatter(partial_norm, "tensor", scatter_dimension=2, tiled=True)
    unit_rows = (cut_x(own_inputs).astype(jnp.float32) + cut_x(embedded)[:, None, :]) * inverse
    grad_hidden = cut_x(own_upstream).astype(jnp.float32) + inverse * (
        grad_norm * cut_x(gain) - unit_rows * (row_dot / features)
    )
    grad_rows = grad_hidden.astype(jnp.bfloat16)
    home = jnp.zeros((batch, local_frames, local_space, slice_width), jnp.bfloat16)
    for k in range(depth):
        piece = grad_rows[k * local_frames : (k + 1) * local_frames]
        if k:
            piece = ring(piece, depth - k)
        target, first = place((z + k) % depth)
        home = lax.dynamic_update_slice(home, piece[None], (target, 0, first, 0))
    grad_inputs = join_x(home)

    gain_term = jnp.sum(grad_norm * unit_rows, (0, 1))
    action_term = jnp.dot(
        onehot.T, jnp.sum(grad_hidden, 1), precision=lax.Precision.HIGHEST
    )
    small = jnp.concatenate([action_term, gain_term[None, :]], 0)
    small = small + swap_core(small)
    small = small + swap_y(small)
    bit = 1
    while bit < depth:
        small = small + swap_z(small, bit)
        bit *= 2
    small = join_x(small)

    bounds = tokens * jnp.stack(
        [
            math.sqrt(features) * jnp.max(jnp.abs(gain)) * jnp.max(peak_qkv),
            UPSTREAM_TOP * jnp.max(peak_out),
        ]
    )
    bounds = jnp.maximum(bounds, 1e-30)
    y_bounds = swap_y(bounds)
    chip_bounds = bounds + y_bounds
    is_out = lax.broadcasted_iota(jnp.int32, (1, width), 1) >= 3 * head_width

    def encode(value, bound):
        return (value * jnp.where(is_out, WIRE_TOP / bound[1], WIRE_TOP / bound[0])).astype(WIRE)

    def decode(value, bound):
        return value.astype(jnp.float32) * jnp.where(
            is_out, bound[1] / WIRE_TOP, bound[0] / WIRE_TOP
        )

    def weight_part(start):
        normed_cut = lax.dynamic_slice_in_dim(all_normed, start, block_rows, 1)
        upstream_cut = lax.dynamic_slice_in_dim(all_upstream, start, block_rows, 1)
        return jnp.concatenate(
            [dot_tn(normed_cut, flat_merged), dot_tn(upstream_cut, flat_mixed)], 1
        )

    total = None
    ring_bounds = chip_bounds
    for k in range(depth):
        start = (z - 1 - k) % depth * (2 * block_rows)
        away = swap_y(encode(weight_part(start + (1 - y) * block_rows), bounds))
        here = weight_part(start + y * block_rows) + decode(away, y_bounds)
        if k:
            here = here + decode(ring(total, 1), arriving)
        if k < depth - 1:
            total = encode(here, ring_bounds)
            arriving = ring(ring_bounds, 1)
            ring_bounds = arriving + chip_bounds
    mine = lax.dynamic_slice_in_dim(here, core * shard_rows, shard_rows, 0)
    other = swap_core(lax.dynamic_slice_in_dim(here, (1 - core) * shard_rows, shard_rows, 0))
    first = jnp.where(core == 0, mine, other).reshape(shard_rows, 4, head_width)
    second = jnp.where(core == 0, other, mine).reshape(shard_rows, 4, head_width)
    joined = jnp.concatenate([first, second], 2)
    return (grad_inputs, joined[:, :3], joined[:, 3], small[actions], small[:actions])


def solution(mesh):
    sizes = mesh.shape
    return jax.shard_map(
        functools.partial(on_device, sizes["frame"], sizes["space"], sizes["tensor"]),
        mesh=mesh,
        in_specs=(
            P(None, "frame", "space", None),
            P(None, "frame", "space", None),
            P(None, "frame"),
            P(),
            P(),
            P(),
            P(("frame", "space"), None, "tensor"),
            P(("frame", "space"), "tensor"),
        ),
        out_specs=(
            P(None, "frame", "space", None),
            P(("frame", "space"), None, "tensor"),
            P(("frame", "space"), "tensor"),
            P(),
            P(),
        ),
        check_vma=False,
    )
```

```python
import functools
import math

import jax
import jax.numpy as jnp
from jax import lax
from jax.experimental import pallas as pl
from jax.experimental.pallas import tpu as pltpu
from jax.sharding import PartitionSpec as P

HEAD = 128
NORM_EPSILON = 1e-06
UPSTREAM_TOP = 6.0
WIRE = jnp.float16
WIRE_TOP = 32768.0


def after(value, *earlier):
    return lax.optimization_barrier((value, *earlier))[0]


def dot_nt(a, b):
    return lax.dot_general(a, b, (((1,), (1,)), ((), ())), preferred_element_type=jnp.float32)


def dot_nn(a, b):
    return lax.dot_general(a, b, (((1,), (0,)), ((), ())), preferred_element_type=jnp.float32)


def dot_tn(a, b):
    return lax.dot_general(a, b, (((0,), (0,)), ((), ())), preferred_element_type=jnp.float32)


def attention_kernel(
    late_ref, early_ref, qkv_ref, grad_ref, mixed_ref, merged_ref, peak_qkv_ref, peak_out_ref
):
    frames, group, width = grad_ref.shape
    rows = frames * group
    scale = 1.0 / math.sqrt(HEAD)

    def load(ref, start):
        block = ref[:, :, start : start + HEAD]
        if group % 16:
            return block.astype(jnp.float32).reshape(rows, HEAD).astype(jnp.bfloat16)
        return block.reshape(rows, HEAD)

    def store(ref, start, value):
        if group % 16:
            ref[:, :, start : start + HEAD] = value.reshape(frames, group, HEAD).astype(
                jnp.bfloat16
            )
        else:
            ref[:, :, start : start + HEAD] = value.astype(jnp.bfloat16).reshape(
                frames, group, HEAD
            )

    def peak(value):
        return jnp.max(jnp.abs(value).reshape(rows // 8, 8, HEAD), axis=0)

    @pl.when(pl.program_id(0) == 0)
    def _():
        peak_qkv_ref[...] = jnp.zeros_like(peak_qkv_ref)
        peak_out_ref[...] = jnp.zeros_like(peak_out_ref)

    row_id = lax.broadcasted_iota(jnp.int32, (rows, rows), 0)
    col_id = lax.broadcasted_iota(jnp.int32, (rows, rows), 1)
    allowed = (row_id % group == col_id % group) & (early_ref[...] <= late_ref[...])
    starts = range(0, width, HEAD)
    query = [load(qkv_ref, i) for i in starts]
    key = [load(qkv_ref, width + i) for i in starts]
    value = [load(qkv_ref, 2 * width + i) for i in starts]
    grad = [load(grad_ref, i) for i in starts]
    heads = range(len(query))
    scores = [jnp.where(allowed, dot_nt(query[h], key[h]) * scale, -1e30) for h in heads]
    grad_probs = [dot_nt(grad[h], value[h]) for h in heads]
    exponent = [jnp.exp(scores[h] - jnp.max(scores[h], -1, keepdims=True)) for h in heads]
    probabilities = [exponent[h] / jnp.sum(exponent[h], -1, keepdims=True) for h in heads]
    rounded = [probabilities[h].astype(jnp.bfloat16) for h in heads]
    mean_grad = [jnp.sum(grad_probs[h] * probabilities[h], -1, keepdims=True) for h in heads]
    mixed = [dot_nn(rounded[h], value[h]) for h in heads]
    grad_value = [dot_tn(rounded[h], grad[h]) for h in heads]
    grad_scores = [probabilities[h] * (grad_probs[h] - mean_grad[h]) for h in heads]
    high = [grad_scores[h].astype(jnp.bfloat16) for h in heads]
    low = [(grad_scores[h] - high[h].astype(jnp.float32)).astype(jnp.bfloat16) for h in heads]
    grad_query = [(dot_nn(high[h], key[h]) + dot_nn(low[h], key[h])) * scale for h in heads]
    grad_key = [(dot_tn(high[h], query[h]) + dot_tn(low[h], query[h])) * scale for h in heads]
    top_out, top_qkv = peak_out_ref[...], peak_qkv_ref[...]
    for h, start in enumerate(starts):
        store(mixed_ref, start, mixed[h])
        store(merged_ref, start, grad_query[h])
        store(merged_ref, width + start, grad_key[h])
        store(merged_ref, 2 * width + start, grad_value[h])
        top_out = jnp.maximum(top_out, peak(mixed[h]))
        for term in (grad_query[h], grad_key[h], grad_value[h]):
            top_qkv = jnp.maximum(top_qkv, peak(term))
    peak_out_ref[...] = top_out
    peak_qkv_ref[...] = top_qkv


def temporal_attention(qkv, grad_heads, times):
    frames, pairs, width = grad_heads.shape
    group = 16 if pairs % 16 == 0 else 8
    rows = frames * group
    per_row = jnp.repeat(times.astype(jnp.float32), group)
    work = pairs // group * rows * rows * (width // HEAD)
    fixed = lambda i: (0, 0)
    moving = lambda i: (0, i, 0)
    return pl.pallas_call(
        attention_kernel,
        grid=(pairs // group,),
        in_specs=[
            pl.BlockSpec((rows, 1), fixed),
            pl.BlockSpec((1, rows), fixed),
            pl.BlockSpec((frames, group, 3 * width), moving),
            pl.BlockSpec((frames, group, width), moving),
        ],
        out_specs=[
            pl.BlockSpec((frames, group, width), moving),
            pl.BlockSpec((frames, group, 3 * width), moving),
            pl.BlockSpec((8, HEAD), fixed),
            pl.BlockSpec((8, HEAD), fixed),
        ],
        out_shape=[
            jax.ShapeDtypeStruct((frames, pairs, width), jnp.bfloat16),
            jax.ShapeDtypeStruct((frames, pairs, 3 * width), jnp.bfloat16),
            jax.ShapeDtypeStruct((8, HEAD), jnp.float32),
            jax.ShapeDtypeStruct((8, HEAD), jnp.float32),
        ],
        compiler_params=pltpu.CompilerParams(vmem_limit_bytes=40 * 1024 * 1024),
        cost_estimate=pl.CostEstimate(
            flops=16 * work * HEAD,
            bytes_accessed=16 * frames * pairs * width,
            transcendentals=work,
        ),
        name="temporal_attention",
    )(per_row[:, None], per_row[None, :], qkv, grad_heads)


def on_device(
    depth, spaces, tensors, inputs, upstream, action_ids, frame_time, action_table, gain, w_qkv, w_out
):
    batch, local_frames, local_space, features = inputs.shape
    actions = action_table.shape[0]
    shard_rows, _, channels = w_qkv.shape
    z = lax.axis_index("frame")
    s = lax.axis_index("space")
    x = lax.axis_index("tensor")
    y, core = s // 2, s % 2
    frames = depth * local_frames
    pairs = batch * local_space // depth
    slots = depth // batch
    slice_width = features // tensors
    head_width = channels // 2
    width = 4 * head_width
    tokens = frames * 2 * pairs

    def ring(value, shift):
        return lax.ppermute(value, "frame", [(i, (i + shift) % depth) for i in range(depth)])

    def swap_z(value, bit):
        return lax.ppermute(value, "frame", [(i, i ^ bit) for i in range(depth)])

    def swap_core(value):
        return lax.ppermute(value, "space", [(i, i ^ 1) for i in range(spaces)])

    def swap_y(value):
        return lax.ppermute(value, "space", [(i, i ^ 2) for i in range(spaces)])

    def swap_x(value):
        return lax.ppermute(value, "tensor", [(0, 1), (1, 0)])

    def join_x(own):
        if tensors == 2:
            other = swap_x(own)
            first = jnp.where(x == 0, own, other)
            second = jnp.where(x == 0, other, own)
            return jnp.concatenate([first, second], -1)
        return lax.all_gather(own, "tensor", axis=own.ndim - 1, tiled=True)

    def cut_x(value, which=None):
        which = x if which is None else which
        return lax.dynamic_slice_in_dim(value, which * slice_width, slice_width, value.ndim - 1)

    def place(j):
        return j // slots, (j % slots) * pairs

    shards = [w_qkv[:, 0], w_qkv[:, 1], w_qkv[:, 2], w_out]

    def core_half(which):
        return jnp.concatenate(
            [jnp.where(which == 0, t[:, :head_width], t[:, head_width:]) for t in shards], 1
        )

    mine, sent = core_half(core), core_half(1 - core)
    other = swap_core(sent)
    block = jnp.concatenate(
        [jnp.where(core == 0, mine, other), jnp.where(core == 0, other, mine)], 0
    )

    def pieces(rows, k, start, size):
        rollout, first = place((z + k) % depth)
        return lax.dynamic_slice(
            rows, (rollout, 0, first, start), (1, local_frames, pairs, size)
        )[0]

    collected = []
    for k in range(depth):
        if k == 0:
            collected.append([pieces(rows, k, 0, features) for rows in (inputs, upstream)])
            continue
        start = x * slice_width
        if k > 1:
            start = after(start, sent)
        piece = jnp.stack([pieces(rows, k, start, slice_width) for rows in (inputs, upstream)])
        piece = join_x(ring(piece, k))
        collected.append([piece[0], piece[1]])
    own_inputs = jnp.concatenate([both_rows[0] for both_rows in collected], 0)
    own_upstream = jnp.concatenate([both_rows[1] for both_rows in collected], 0)

    block_rows = 2 * shard_rows
    weights = jnp.zeros((features, width), jnp.bfloat16)
    for k in range(depth):
        if k:
            block = ring(block, 1)
        start = (z - k) % depth * (2 * block_rows)
        weights = lax.dynamic_update_slice(weights, block, (start + y * block_rows, 0))
        weights = lax.dynamic_update_slice(
            weights, swap_y(block), (start + (1 - y) * block_rows, 0)
        )
    weight_qkv, weight_out = weights[:, : 3 * head_width], weights[:, 3 * head_width :]
    rollout, _ = place(z)
    ids = jnp.concatenate(
        [
            lax.dynamic_index_in_dim(
                ring(action_ids, k) if k else action_ids, rollout, 0, keepdims=False
            )
            for k in range(depth)
        ]
    )
    order = (
        (z - jnp.arange(depth, dtype=jnp.int32)[:, None]) % depth * local_frames
        + jnp.arange(local_frames, dtype=jnp.int32)[None, :]
    ).reshape(frames)
    own_time = lax.dynamic_index_in_dim(frame_time, rollout, 0, keepdims=False)
    times = jnp.sum(
        jnp.where(
            order[:, None] == jnp.arange(frames, dtype=jnp.int32)[None, :], own_time[None, :], 0
        ),
        1,
    )
    onehot = (ids[:, None] == jnp.arange(actions, dtype=jnp.int32)[None, :]).astype(jnp.float32)
    embedded = jnp.dot(onehot, action_table, precision=lax.Precision.HIGHEST)
    hidden = own_inputs.astype(jnp.float32) + embedded[:, None, :]
    inverse = lax.rsqrt(jnp.mean(hidden * hidden, -1, keepdims=True) + NORM_EPSILON)
    normed = (hidden * inverse * gain).astype(jnp.bfloat16)

    def both(own):
        return jnp.concatenate([own, swap_core(own)], 1).reshape(tokens, features)

    all_upstream = both(own_upstream)
    all_normed = both(normed)
    qkv = dot_nn(all_normed, weight_qkv).astype(jnp.bfloat16)
    grad_heads = dot_nn(all_upstream, weight_out).astype(jnp.bfloat16)
    mixed, merged, peak_qkv, peak_out = temporal_attention(
        qkv.reshape(frames, 2 * pairs, 3 * head_width),
        grad_heads.reshape(frames, 2 * pairs, head_width),
        times,
    )
    flat_mixed = mixed.reshape(tokens, head_width)
    flat_merged = merged.reshape(tokens, 3 * head_width)

    peaks = jnp.stack([jnp.max(peak_qkv), jnp.max(peak_out)])
    peaks = jnp.maximum(peaks, swap_core(peaks))
    if tensors == 2:
        peaks = jnp.maximum(peaks, swap_x(peaks))
    peaks = jnp.maximum(peaks, swap_y(peaks))
    bit = 1
    while bit < depth:
        peaks = jnp.maximum(peaks, swap_z(peaks, bit))
        bit *= 2
    peaks = jnp.maximum(peaks, 1e-25)
    all_tokens = tokens * depth * (spaces // 2)
    qkv_bound = all_tokens * math.sqrt(features) * jnp.max(jnp.abs(gain)) * peaks[0]
    out_bound = all_tokens * UPSTREAM_TOP * peaks[1]
    norm_bound = 6 * head_width * peaks[0]
    is_out = lax.broadcasted_iota(jnp.int32, (1, width), 1) >= 3 * head_width
    encoding = jnp.where(is_out, WIRE_TOP / out_bound, WIRE_TOP / qkv_bound)
    decoding = jnp.where(is_out, out_bound / WIRE_TOP, qkv_bound / WIRE_TOP)

    def weight_part(k, row, earlier):
        start = after((z - 1 - k) % depth * (2 * block_rows) + row * block_rows, earlier)
        normed_cut = lax.dynamic_slice_in_dim(all_normed, start, block_rows, 1)
        upstream_cut = lax.dynamic_slice_in_dim(all_upstream, start, block_rows, 1)
        return jnp.concatenate(
            [dot_tn(normed_cut, flat_merged), dot_tn(upstream_cut, flat_mixed)], 1
        )

    def away_part(k, earlier):
        return (weight_part(k, 1 - y, earlier) * encoding).astype(WIRE)

    def norm_part(rows):
        flat = rows.reshape(frames * pairs, 3 * head_width)
        return dot_nt(flat, weight_qkv).reshape(frames, pairs, features)

    norm_away = norm_part(merged[:, pairs:])
    away = [away_part(0, norm_away)]
    norm_here = norm_part(after(merged[:, :pairs], away[0]))
    away.append(away_part(1, norm_here))
    here = [weight_part(0, y, away[1])]
    for k in range(2, depth):
        away.append(away_part(k, here[-1]))
        here.append(weight_part(k - 1, y, away[-1]))
    here.append(weight_part(depth - 1, y, here[-1]))
    partial_norm = norm_here + swap_core(norm_away)
    row_dot = jnp.sum(partial_norm * gain * (hidden * inverse), -1, keepdims=True)
    if tensors == 2:
        row_dot = row_dot + swap_x(row_dot)
        sent = (cut_x(partial_norm, 1 - x) * (WIRE_TOP / norm_bound)).astype(WIRE)
        grad_norm = cut_x(partial_norm) + swap_x(sent).astype(jnp.float32) * (
            norm_bound / WIRE_TOP
        )
    else:
        row_dot = lax.psum(row_dot, "tensor")
        grad_norm = lax.psum_scatter(partial_norm, "tensor", scatter_dimension=2, tiled=True)
    unit_rows = (cut_x(own_inputs).astype(jnp.float32) + cut_x(embedded)[:, None, :]) * inverse
    grad_hidden = cut_x(own_upstream).astype(jnp.float32) + inverse * (
        grad_norm * cut_x(gain) - unit_rows * (row_dot / features)
    )
    grad_rows = grad_hidden.astype(jnp.bfloat16)
    grad_inputs = jnp.zeros(inputs.shape, jnp.bfloat16)
    for k in range(depth):
        piece = grad_rows[k * local_frames : (k + 1) * local_frames]
        if k:
            piece = ring(piece, depth - k)
        target, first = place((z + k) % depth)
        grad_inputs = lax.dynamic_update_slice(
            grad_inputs, join_x(piece)[None], (target, 0, first, 0)
        )

    gain_term = jnp.sum(grad_norm * unit_rows, (0, 1))
    action_term = jnp.dot(
        onehot.T, jnp.sum(grad_hidden, 1), precision=lax.Precision.HIGHEST
    )
    small = jnp.concatenate([action_term, gain_term[None, :]], 0)
    small = small + swap_core(small)
    small = small + swap_y(small)
    bit = 1
    while bit < depth:
        small = small + swap_z(small, bit)
        bit *= 2
    small = join_x(small)

    for k in range(depth):
        total = here[k] + swap_y(away[k]).astype(jnp.float32) * decoding
        if k:
            total = total + arriving.astype(jnp.float32) * decoding
        if k < depth - 1:
            arriving = ring((total * encoding).astype(WIRE), 1)
    mine = lax.dynamic_slice_in_dim(total, core * shard_rows, shard_rows, 0)
    other = swap_core(lax.dynamic_slice_in_dim(total, (1 - core) * shard_rows, shard_rows, 0))
    first = jnp.where(core == 0, mine, other).reshape(shard_rows, 4, head_width)
    second = jnp.where(core == 0, other, mine).reshape(shard_rows, 4, head_width)
    joined = jnp.concatenate([first, second], 2)
    return (grad_inputs, joined[:, :3], joined[:, 3], small[actions], small[:actions])


def solution(mesh):
    sizes = mesh.shape
    return jax.shard_map(
        functools.partial(on_device, sizes["frame"], sizes["space"], sizes["tensor"]),
        mesh=mesh,
        in_specs=(
            P(None, "frame", "space", None),
            P(None, "frame", "space", None),
            P(None, "frame"),
            P(),
            P(),
            P(),
            P(("frame", "space"), None, "tensor"),
            P(("frame", "space"), "tensor"),
        ),
        out_specs=(
            P(None, "frame", "space", None),
            P(("frame", "space"), None, "tensor"),
            P(("frame", "space"), "tensor"),
            P(),
            P(),
        ),
        check_vma=False,
    )
```

```python
import functools
import math

import jax
import jax.numpy as jnp
from jax import lax
from jax.experimental import pallas as pl
from jax.experimental.pallas import tpu as pltpu
from jax.sharding import PartitionSpec as P

HEAD = 128
NORM_EPSILON = 1e-06
UPSTREAM_TOP = 6.0
WIRE = jnp.float16
WIRE_TOP = 32768.0


def after(value, *earlier):
    return lax.optimization_barrier((value, earlier))[0]


def dot_nt(a, b):
    return lax.dot_general(a, b, (((1,), (1,)), ((), ())), preferred_element_type=jnp.float32)


def dot_nn(a, b):
    return lax.dot_general(a, b, (((1,), (0,)), ((), ())), preferred_element_type=jnp.float32)


def dot_tn(a, b):
    return lax.dot_general(a, b, (((0,), (0,)), ((), ())), preferred_element_type=jnp.float32)


def attention_kernel(
    late_ref, early_ref, qkv_ref, grad_ref, mixed_ref, merged_ref, peak_qkv_ref, peak_out_ref
):
    frames, group, width = grad_ref.shape
    rows = frames * group
    scale = 1.0 / math.sqrt(HEAD)

    def load(ref, start):
        block = ref[:, :, start : start + HEAD]
        if group % 16:
            return block.astype(jnp.float32).reshape(rows, HEAD).astype(jnp.bfloat16)
        return block.reshape(rows, HEAD)

    def store(ref, start, value):
        if group % 16:
            ref[:, :, start : start + HEAD] = value.reshape(frames, group, HEAD).astype(
                jnp.bfloat16
            )
        else:
            ref[:, :, start : start + HEAD] = value.astype(jnp.bfloat16).reshape(
                frames, group, HEAD
            )

    def peak(value):
        return jnp.max(jnp.abs(value).reshape(rows // 8, 8, HEAD), axis=0)

    @pl.when(pl.program_id(0) == 0)
    def _():
        peak_qkv_ref[...] = jnp.zeros_like(peak_qkv_ref)
        peak_out_ref[...] = jnp.zeros_like(peak_out_ref)

    row_id = lax.broadcasted_iota(jnp.int32, (rows, rows), 0)
    col_id = lax.broadcasted_iota(jnp.int32, (rows, rows), 1)
    allowed = (row_id % group == col_id % group) & (early_ref[...] <= late_ref[...])
    starts = range(0, width, HEAD)
    query = [load(qkv_ref, i) for i in starts]
    key = [load(qkv_ref, width + i) for i in starts]
    value = [load(qkv_ref, 2 * width + i) for i in starts]
    grad = [load(grad_ref, i) for i in starts]
    heads = range(len(query))
    scores = [jnp.where(allowed, dot_nt(query[h], key[h]) * scale, -1e30) for h in heads]
    grad_probs = [dot_nt(grad[h], value[h]) for h in heads]
    exponent = [jnp.exp(scores[h] - jnp.max(scores[h], -1, keepdims=True)) for h in heads]
    probabilities = [exponent[h] / jnp.sum(exponent[h], -1, keepdims=True) for h in heads]
    rounded = [probabilities[h].astype(jnp.bfloat16) for h in heads]
    mean_grad = [jnp.sum(grad_probs[h] * probabilities[h], -1, keepdims=True) for h in heads]
    mixed = [dot_nn(rounded[h], value[h]) for h in heads]
    grad_value = [dot_tn(rounded[h], grad[h]) for h in heads]
    grad_scores = [probabilities[h] * (grad_probs[h] - mean_grad[h]) for h in heads]
    high = [grad_scores[h].astype(jnp.bfloat16) for h in heads]
    low = [(grad_scores[h] - high[h].astype(jnp.float32)).astype(jnp.bfloat16) for h in heads]
    grad_query = [(dot_nn(high[h], key[h]) + dot_nn(low[h], key[h])) * scale for h in heads]
    grad_key = [(dot_tn(high[h], query[h]) + dot_tn(low[h], query[h])) * scale for h in heads]
    top_out, top_qkv = peak_out_ref[...], peak_qkv_ref[...]
    for h, start in enumerate(starts):
        store(mixed_ref, start, mixed[h])
        store(merged_ref, start, grad_query[h])
        store(merged_ref, width + start, grad_key[h])
        store(merged_ref, 2 * width + start, grad_value[h])
        top_out = jnp.maximum(top_out, peak(mixed[h]))
        for term in (grad_query[h], grad_key[h], grad_value[h]):
            top_qkv = jnp.maximum(top_qkv, peak(term))
    peak_out_ref[...] = top_out
    peak_qkv_ref[...] = top_qkv


def temporal_attention(qkv, grad_heads, times):
    frames, pairs, width = grad_heads.shape
    group = 16 if pairs % 16 == 0 else 8
    rows = frames * group
    per_row = jnp.repeat(times.astype(jnp.float32), group)
    work = pairs // group * rows * rows * (width // HEAD)
    fixed = lambda i: (0, 0)
    moving = lambda i: (0, i, 0)
    return pl.pallas_call(
        attention_kernel,
        grid=(pairs // group,),
        in_specs=[
            pl.BlockSpec((rows, 1), fixed),
            pl.BlockSpec((1, rows), fixed),
            pl.BlockSpec((frames, group, 3 * width), moving),
            pl.BlockSpec((frames, group, width), moving),
        ],
        out_specs=[
            pl.BlockSpec((frames, group, width), moving),
            pl.BlockSpec((frames, group, 3 * width), moving),
            pl.BlockSpec((8, HEAD), fixed),
            pl.BlockSpec((8, HEAD), fixed),
        ],
        out_shape=[
            jax.ShapeDtypeStruct((frames, pairs, width), jnp.bfloat16),
            jax.ShapeDtypeStruct((frames, pairs, 3 * width), jnp.bfloat16),
            jax.ShapeDtypeStruct((8, HEAD), jnp.float32),
            jax.ShapeDtypeStruct((8, HEAD), jnp.float32),
        ],
        compiler_params=pltpu.CompilerParams(vmem_limit_bytes=40 * 1024 * 1024),
        cost_estimate=pl.CostEstimate(
            flops=16 * work * HEAD,
            bytes_accessed=16 * frames * pairs * width,
            transcendentals=work,
        ),
        name="temporal_attention",
    )(per_row[:, None], per_row[None, :], qkv, grad_heads)


def on_device(
    depth, spaces, tensors, inputs, upstream, action_ids, frame_time, action_table, gain, w_qkv, w_out
):
    batch, local_frames, local_space, features = inputs.shape
    actions = action_table.shape[0]
    shard_rows, _, channels = w_qkv.shape
    z = lax.axis_index("frame")
    s = lax.axis_index("space")
    x = lax.axis_index("tensor")
    y, core = s // 2, s % 2
    frames = depth * local_frames
    pairs = batch * local_space // depth
    slots = depth // batch
    slice_width = features // tensors
    head_width = channels // 2
    width = 4 * head_width
    tokens = frames * 2 * pairs

    def ring(value, shift):
        return lax.ppermute(value, "frame", [(i, (i + shift) % depth) for i in range(depth)])

    def swap_z(value, bit):
        return lax.ppermute(value, "frame", [(i, i ^ bit) for i in range(depth)])

    def swap_core(value):
        return lax.ppermute(value, "space", [(i, i ^ 1) for i in range(spaces)])

    def swap_y(value):
        return lax.ppermute(value, "space", [(i, i ^ 2) for i in range(spaces)])

    def swap_x(value):
        return lax.ppermute(value, "tensor", [(0, 1), (1, 0)])

    def join_x(own, other=None):
        if tensors == 2:
            other = swap_x(own) if other is None else other
            first = jnp.where(x == 0, own, other)
            second = jnp.where(x == 0, other, own)
            return jnp.concatenate([first, second], -1)
        return lax.all_gather(own, "tensor", axis=own.ndim - 1, tiled=True)

    def cut_x(value, which=None):
        which = x if which is None else which
        return lax.dynamic_slice_in_dim(value, which * slice_width, slice_width, value.ndim - 1)

    def place(j):
        return j // slots, (j % slots) * pairs

    shards = [w_qkv[:, 0], w_qkv[:, 1], w_qkv[:, 2], w_out]

    def core_half(which):
        return jnp.concatenate(
            [jnp.where(which == 0, t[:, :head_width], t[:, head_width:]) for t in shards], 1
        )

    mine, sent = core_half(core), core_half(1 - core)
    other = swap_core(sent)
    block = jnp.concatenate(
        [jnp.where(core == 0, mine, other), jnp.where(core == 0, other, mine)], 0
    )

    def pieces(rows, k, start, size):
        rollout, first = place((z + k) % depth)
        return lax.dynamic_slice(
            rows, (rollout, 0, first, start), (1, local_frames, pairs, size)
        )[0]

    def collect(k, start):
        piece = jnp.stack([pieces(rows, k, start, slice_width) for rows in (inputs, upstream)])
        return ring(piece, k)

    block_rows = 2 * shard_rows
    arrived = collect(1, x * slice_width)
    block = after(block, arrived)
    blocks, across, joined, all_ids = [], [], [], [action_ids]
    for k in range(1, depth):
        blocks.append(block)
        across.append(swap_y(block))
        crossed = swap_x(arrived) if tensors == 2 else None
        joined.append(join_x(arrived, crossed))
        following = ring(block, 1)
        earlier = [across[-1], joined[-1] if crossed is None else crossed]
        if k + 1 < depth:
            arrived = collect(k + 1, after(x * slice_width, block))
            earlier.append(arrived)
            all_ids.append(ring(after(action_ids, block), k))
            earlier.append(all_ids[-1])
            following, arrived = lax.optimization_barrier((following, arrived, earlier))[:2]
        block = following
    all_ids.append(ring(after(action_ids, blocks[-1]), depth - 1))
    blocks.append(block)
    across.append(swap_y(block))
    weights = jnp.zeros((features, width), jnp.bfloat16)

    def settle(weights, k, arrived, row):
        start = (z - k) % depth * (2 * block_rows) + row * block_rows
        return lax.dynamic_update_slice(weights, arrived, (start, 0))

    for k in range(depth - 1):
        weights = settle(weights, k, blocks[k], y)
        if k + 2 < depth:
            weights = settle(weights, k, across[k], 1 - y)
    joined[-1], weights, block, all_ids, across[-2] = lax.optimization_barrier(
        (joined[-1], weights, blocks[-1], all_ids, across[-2])
    )
    locals_ = [pieces(rows, 0, 0, features) for rows in (inputs, upstream)]
    own_inputs = jnp.concatenate([locals_[0]] + [both_rows[0] for both_rows in joined], 0)
    own_upstream = jnp.concatenate([locals_[1]] + [both_rows[1] for both_rows in joined], 0)
    rollout, _ = place(z)
    ids = jnp.concatenate(
        [
            lax.dynamic_index_in_dim(each, rollout, 0, keepdims=False) for each in all_ids
        ]
    )
    order = (
        (z - jnp.arange(depth, dtype=jnp.int32)[:, None]) % depth * local_frames
        + jnp.arange(local_frames, dtype=jnp.int32)[None, :]
    ).reshape(frames)
    own_time = lax.dynamic_index_in_dim(frame_time, rollout, 0, keepdims=False)
    times = jnp.sum(
        jnp.where(
            order[:, None] == jnp.arange(frames, dtype=jnp.int32)[None, :], own_time[None, :], 0
        ),
        1,
    )
    onehot = (ids[:, None] == jnp.arange(actions, dtype=jnp.int32)[None, :]).astype(jnp.float32)
    embedded = jnp.dot(onehot, action_table, precision=lax.Precision.HIGHEST)
    hidden = own_inputs.astype(jnp.float32) + embedded[:, None, :]
    inverse = lax.rsqrt(jnp.mean(hidden * hidden, -1, keepdims=True) + NORM_EPSILON)
    normed = (hidden * inverse * gain).astype(jnp.bfloat16)

    def both(own):
        return jnp.concatenate([own, swap_core(own)], 1).reshape(tokens, features)

    all_upstream = both(own_upstream)
    all_normed = both(normed)
    normed_t, upstream_t = lax.optimization_barrier((all_normed.T, all_upstream.T))

    weights = settle(weights, depth - 2, across[-2], 1 - y)
    weights = settle(weights, depth - 1, block, y)
    weights = settle(weights, depth - 1, after(across[-1], normed_t, upstream_t), 1 - y)
    weight_qkv, weight_out = weights[:, : 3 * head_width], weights[:, 3 * head_width :]
    qkv = dot_nn(all_normed, weight_qkv).astype(jnp.bfloat16)
    grad_heads = dot_nn(all_upstream, weight_out).astype(jnp.bfloat16)
    mixed, merged, peak_qkv, peak_out = temporal_attention(
        qkv.reshape(frames, 2 * pairs, 3 * head_width),
        grad_heads.reshape(frames, 2 * pairs, head_width),
        times,
    )
    flat_mixed = mixed.reshape(tokens, head_width)
    flat_merged = merged.reshape(tokens, 3 * head_width)

    own_bound = tokens * jnp.where(
        lax.broadcasted_iota(jnp.int32, (1, width), 1) < 3 * head_width,
        math.sqrt(features) * jnp.max(jnp.abs(gain)) * jnp.max(peak_qkv),
        UPSTREAM_TOP * jnp.max(peak_out),
    )
    own_bound = jnp.maximum(own_bound, 1e-20)

    def pack(value, bound):
        exponent = jnp.ceil(jnp.log2(bound / WIRE_TOP))
        return jnp.concatenate(
            [value * jnp.exp2(-exponent), jnp.broadcast_to(exponent, (8, width))], 0
        ).astype(WIRE)

    def unpack(sent):
        scale = jnp.exp2(sent[block_rows : block_rows + 1].astype(jnp.float32))
        return sent[:block_rows].astype(jnp.float32) * scale, scale * WIRE_TOP

    def weight_part(k, earlier):
        start = after((z - 1 - k) % depth * (2 * block_rows), earlier)
        cuts = [
            lax.dynamic_slice_in_dim(rows, start, 2 * block_rows, 0)
            for rows in (normed_t, upstream_t)
        ]
        part = jnp.concatenate([dot_nn(cuts[0], flat_merged), dot_nn(cuts[1], flat_mixed)], 1)
        return (
            lax.dynamic_slice_in_dim(part, y * block_rows, block_rows, 0),
            pack(
                lax.dynamic_slice_in_dim(part, (1 - y) * block_rows, block_rows, 0), own_bound
            ),
        )

    def norm_part(rows):
        flat = rows.reshape(frames * pairs, 3 * head_width)
        return dot_nt(flat, weight_qkv).reshape(frames, pairs, features)

    norm_away = norm_part(merged[:, pairs:])
    weight_parts = [weight_part(0, norm_away)]
    norm_here = norm_part(after(merged[:, :pairs], weight_parts[0][1]))
    partial_norm = norm_here + swap_core(norm_away)
    row_dot = jnp.sum(partial_norm * gain * (hidden * inverse), -1, keepdims=True)
    if tensors == 2:
        x_away = cut_x(partial_norm, 1 - x)
        row_scale = jnp.max(jnp.abs(partial_norm), -1, keepdims=True)
        row_scale = jnp.maximum(row_scale, 1e-20) / WIRE_TOP
        sent = (x_away / row_scale).astype(WIRE)
        row_terms = swap_x(jnp.concatenate([row_dot, row_scale], -1))
        x_terms = swap_x(sent)
    else:
        row_dot = lax.psum(row_dot, "tensor")
        grad_norm = lax.psum_scatter(partial_norm, "tensor", scatter_dimension=2, tiled=True)
        sent = partial_norm

    def chip_sum(k, earlier):
        term, bound = unpack(after(swap_y(weight_parts[k][1]), earlier))
        return weight_parts[k][0] + term, bound + own_bound

    def ring_sum(k, arriving, earlier):
        total, bound = chip_sum(k, earlier)
        term, ring_bound = unpack(arriving)
        return total + term, bound + ring_bound

    weight_parts.append(weight_part(1, sent))
    payload = pack(*chip_sum(0, weight_parts[1][1]))
    weight_parts.append(weight_part(2, payload))
    if tensors == 2:
        x_terms, row_terms = after((x_terms, row_terms), weight_parts[2][1])
        row_dot = row_dot + row_terms[..., :1]
        grad_norm = cut_x(partial_norm) + x_terms.astype(jnp.float32) * row_terms[..., 1:]
    unit_rows = (cut_x(own_inputs).astype(jnp.float32) + cut_x(embedded)[:, None, :]) * inverse
    grad_hidden = cut_x(own_upstream).astype(jnp.float32) + inverse * (
        grad_norm * cut_x(gain) - unit_rows * (row_dot / features)
    )
    grad_rows = grad_hidden.astype(jnp.bfloat16)
    returned = [grad_rows[:local_frames]]
    for k in range(1, depth):
        returned.append(
            ring(grad_rows[k * local_frames : (k + 1) * local_frames], depth - k)
        )
    for k in range(1, depth - 1):
        if k + 2 < depth:
            weight_parts.append(weight_part(k + 2, (payload, grad_rows)))
        payload = pack(*ring_sum(k, ring(payload, 1), weight_parts[-1][1]))
    grad_inputs = jnp.zeros(inputs.shape, jnp.bfloat16)
    for k in range(depth):
        piece = after(returned[k], payload) if k else returned[k]
        target, first = place((z + k) % depth)
        grad_inputs = lax.dynamic_update_slice(
            grad_inputs, join_x(piece)[None], (target, 0, first, 0)
        )

    gain_term = jnp.sum(grad_norm * unit_rows, (0, 1))
    action_term = jnp.dot(
        onehot.T, jnp.sum(grad_hidden, 1), precision=lax.Precision.HIGHEST
    )
    small = jnp.concatenate([action_term, gain_term[None, :]], 0)
    last_sum, last_bound = chip_sum(depth - 1, payload)
    small = after(small, last_sum)
    small = small + swap_core(small)
    small = join_x(small + swap_y(small))
    bit = 1
    while bit < depth:
        small = small + swap_z(small, bit)
        bit *= 2

    total = last_sum + unpack(ring(payload, 1))[0]
    mine = lax.dynamic_slice_in_dim(total, core * shard_rows, shard_rows, 0)
    other = swap_core(lax.dynamic_slice_in_dim(total, (1 - core) * shard_rows, shard_rows, 0))
    first = jnp.where(core == 0, mine, other).reshape(shard_rows, 4, head_width)
    second = jnp.where(core == 0, other, mine).reshape(shard_rows, 4, head_width)
    joined = jnp.concatenate([first, second], 2)
    return (grad_inputs, joined[:, :3], joined[:, 3], small[actions], small[:actions])


def solution(mesh):
    sizes = mesh.shape
    return jax.shard_map(
        functools.partial(on_device, sizes["frame"], sizes["space"], sizes["tensor"]),
        mesh=mesh,
        in_specs=(
            P(None, "frame", "space", None),
            P(None, "frame", "space", None),
            P(None, "frame"),
            P(),
            P(),
            P(),
            P(("frame", "space"), None, "tensor"),
            P(("frame", "space"), "tensor"),
        ),
        out_specs=(
            P(None, "frame", "space", None),
            P(("frame", "space"), None, "tensor"),
            P(("frame", "space"), "tensor"),
            P(),
            P(),
        ),
        check_vma=False,
    )
```

```python
import functools
import math

import jax
import jax.numpy as jnp
from jax import lax
from jax.experimental import pallas as pl
from jax.experimental.pallas import tpu as pltpu
from jax.sharding import PartitionSpec as P

HEAD = 128
NORM_EPSILON = 1e-06
UPSTREAM_TOP = 6.0
WIRE = jnp.float16
WIRE_TOP = 32768.0


def after(value, *earlier):
    return lax.optimization_barrier((value, earlier))[0]


def dot_nt(a, b):
    return lax.dot_general(a, b, (((1,), (1,)), ((), ())), preferred_element_type=jnp.float32)


def dot_nn(a, b):
    return lax.dot_general(a, b, (((1,), (0,)), ((), ())), preferred_element_type=jnp.float32)


def dot_tn(a, b):
    return lax.dot_general(a, b, (((0,), (0,)), ((), ())), preferred_element_type=jnp.float32)


def attention_kernel(
    late_ref, early_ref, qkv_ref, grad_ref, mixed_ref, merged_ref, peak_qkv_ref, peak_out_ref
):
    frames, group, width = grad_ref.shape
    rows = frames * group
    scale = 1.0 / math.sqrt(HEAD)

    def load(ref, start):
        block = ref[:, :, start : start + HEAD]
        if group % 16:
            return block.astype(jnp.float32).reshape(rows, HEAD).astype(jnp.bfloat16)
        return block.reshape(rows, HEAD)

    def store(ref, start, value):
        if group % 16:
            ref[:, :, start : start + HEAD] = value.reshape(frames, group, HEAD).astype(
                jnp.bfloat16
            )
        else:
            ref[:, :, start : start + HEAD] = value.astype(jnp.bfloat16).reshape(
                frames, group, HEAD
            )

    def peak(value):
        return jnp.max(jnp.abs(value).reshape(rows // 8, 8, HEAD), axis=0)

    @pl.when(pl.program_id(0) == 0)
    def _():
        peak_qkv_ref[...] = jnp.zeros_like(peak_qkv_ref)
        peak_out_ref[...] = jnp.zeros_like(peak_out_ref)

    row_id = lax.broadcasted_iota(jnp.int32, (rows, rows), 0)
    col_id = lax.broadcasted_iota(jnp.int32, (rows, rows), 1)
    allowed = (row_id % group == col_id % group) & (early_ref[...] <= late_ref[...])
    starts = range(0, width, HEAD)
    query = [load(qkv_ref, i) for i in starts]
    key = [load(qkv_ref, width + i) for i in starts]
    value = [load(qkv_ref, 2 * width + i) for i in starts]
    grad = [load(grad_ref, i) for i in starts]
    heads = range(len(query))
    scores = [jnp.where(allowed, dot_nt(query[h], key[h]) * scale, -1e30) for h in heads]
    grad_probs = [dot_nt(grad[h], value[h]) for h in heads]
    exponent = [jnp.exp(scores[h] - jnp.max(scores[h], -1, keepdims=True)) for h in heads]
    probabilities = [exponent[h] / jnp.sum(exponent[h], -1, keepdims=True) for h in heads]
    rounded = [probabilities[h].astype(jnp.bfloat16) for h in heads]
    mean_grad = [jnp.sum(grad_probs[h] * probabilities[h], -1, keepdims=True) for h in heads]
    mixed = [dot_nn(rounded[h], value[h]) for h in heads]
    grad_value = [dot_tn(rounded[h], grad[h]) for h in heads]
    grad_scores = [probabilities[h] * (grad_probs[h] - mean_grad[h]) for h in heads]
    high = [grad_scores[h].astype(jnp.bfloat16) for h in heads]
    low = [(grad_scores[h] - high[h].astype(jnp.float32)).astype(jnp.bfloat16) for h in heads]
    grad_query = [(dot_nn(high[h], key[h]) + dot_nn(low[h], key[h])) * scale for h in heads]
    grad_key = [(dot_tn(high[h], query[h]) + dot_tn(low[h], query[h])) * scale for h in heads]
    top_out, top_qkv = peak_out_ref[...], peak_qkv_ref[...]
    for h, start in enumerate(starts):
        store(mixed_ref, start, mixed[h])
        store(merged_ref, start, grad_query[h])
        store(merged_ref, width + start, grad_key[h])
        store(merged_ref, 2 * width + start, grad_value[h])
        top_out = jnp.maximum(top_out, peak(mixed[h]))
        for term in (grad_query[h], grad_key[h], grad_value[h]):
            top_qkv = jnp.maximum(top_qkv, peak(term))
    peak_out_ref[...] = top_out
    peak_qkv_ref[...] = top_qkv


def temporal_attention(qkv, grad_heads, times):
    frames, pairs, width = grad_heads.shape
    group = 16 if pairs % 16 == 0 else 8
    rows = frames * group
    per_row = jnp.repeat(times.astype(jnp.float32), group)
    work = pairs // group * rows * rows * (width // HEAD)
    fixed = lambda i: (0, 0)
    moving = lambda i: (0, i, 0)
    return pl.pallas_call(
        attention_kernel,
        grid=(pairs // group,),
        in_specs=[
            pl.BlockSpec((rows, 1), fixed),
            pl.BlockSpec((1, rows), fixed),
            pl.BlockSpec((frames, group, 3 * width), moving),
            pl.BlockSpec((frames, group, width), moving),
        ],
        out_specs=[
            pl.BlockSpec((frames, group, width), moving),
            pl.BlockSpec((frames, group, 3 * width), moving),
            pl.BlockSpec((8, HEAD), fixed),
            pl.BlockSpec((8, HEAD), fixed),
        ],
        out_shape=[
            jax.ShapeDtypeStruct((frames, pairs, width), jnp.bfloat16),
            jax.ShapeDtypeStruct((frames, pairs, 3 * width), jnp.bfloat16),
            jax.ShapeDtypeStruct((8, HEAD), jnp.float32),
            jax.ShapeDtypeStruct((8, HEAD), jnp.float32),
        ],
        compiler_params=pltpu.CompilerParams(vmem_limit_bytes=40 * 1024 * 1024),
        cost_estimate=pl.CostEstimate(
            flops=16 * work * HEAD,
            bytes_accessed=16 * frames * pairs * width,
            transcendentals=work,
        ),
        name="temporal_attention",
    )(per_row[:, None], per_row[None, :], qkv, grad_heads)


def weight_kernel(
    place_ref, norm_near, norm_far, up_near, up_far, merged_ref, mixed_ref, near_ref, far_ref, turned
):
    step = pl.program_id(0)
    rows = near_ref.shape[0]

    @pl.when(step == 0)
    def _():
        turned[:rows] = norm_near[...].T
        turned[rows:] = norm_far[...].T

    @pl.when(step < 3)
    def _():
        near_ref[...] = dot_nn(turned[:rows], merged_ref[...])
        far_ref[...] = dot_nn(turned[rows:], merged_ref[...])

    @pl.when(step == 3)
    def _():
        near_ref[...] = dot_tn(up_near[...], mixed_ref[...])
        far_ref[...] = dot_tn(up_far[...], mixed_ref[...])


def weight_product(places, rows, normed, upstream, merged, mixed):
    tokens, width = mixed.shape
    near = pl.BlockSpec((tokens, rows), lambda i, at: (0, at[0]))
    far = pl.BlockSpec((tokens, rows), lambda i, at: (0, at[1]))
    out = pl.BlockSpec((rows, width), lambda i, at: (0, i))
    return pl.pallas_call(
        weight_kernel,
        grid_spec=pltpu.PrefetchScalarGridSpec(
            num_scalar_prefetch=1,
            grid=(4,),
            in_specs=[
                near,
                far,
                near,
                far,
                pl.BlockSpec((tokens, width), lambda i, at: (0, jnp.minimum(i, 2))),
                pl.BlockSpec((tokens, width), lambda i, at: (0, 0)),
            ],
            out_specs=[out, out],
            scratch_shapes=[pltpu.VMEM((2 * rows, tokens), jnp.bfloat16)],
        ),
        out_shape=[jax.ShapeDtypeStruct((rows, 4 * width), jnp.float32)] * 2,
        compiler_params=pltpu.CompilerParams(vmem_limit_bytes=40 * 1024 * 1024),
        cost_estimate=pl.CostEstimate(flops=1, bytes_accessed=1, transcendentals=0),
        name="weight_product",
    )(places, normed, normed, upstream, upstream, merged, mixed)


def project_kernel(normed_ref, up_ref, weight_ref, qkv_ref, grad_ref):
    @pl.when(pl.program_id(0) < 3)
    def _():
        qkv_ref[...] = dot_nn(normed_ref[...], weight_ref[...]).astype(jnp.bfloat16)

    @pl.when(pl.program_id(0) == 3)
    def _():
        grad_ref[...] = dot_nn(up_ref[...], weight_ref[...]).astype(jnp.bfloat16)


def project(normed, upstream, weights):
    tokens, features = normed.shape
    width = weights.shape[1] // 4
    rows = tokens // 2
    return pl.pallas_call(
        project_kernel,
        grid=(4, 2),
        in_specs=[
            pl.BlockSpec((rows, features), lambda i, j: (jnp.where(i < 3, j, 1), 0)),
            pl.BlockSpec((rows, features), lambda i, j: (jnp.where(i < 3, 0, j), 0)),
            pl.BlockSpec((features, width), lambda i, j: (0, i)),
        ],
        out_specs=[
            pl.BlockSpec(
                (rows, width), lambda i, j: (jnp.where(i < 3, j, 1), jnp.minimum(i, 2))
            ),
            pl.BlockSpec((rows, width), lambda i, j: (jnp.where(i < 3, 0, j), 0)),
        ],
        out_shape=[
            jax.ShapeDtypeStruct((tokens, 3 * width), jnp.bfloat16),
            jax.ShapeDtypeStruct((tokens, width), jnp.bfloat16),
        ],
        compiler_params=pltpu.CompilerParams(vmem_limit_bytes=40 * 1024 * 1024),
        cost_estimate=pl.CostEstimate(
            flops=2 * tokens * features * 4 * width,
            bytes_accessed=8 * tokens * features,
            transcendentals=0,
        ),
        name="project",
    )(normed, upstream, weights)


def norm_kernel(merged_ref, weight_ref, out_ref):
    out_ref[...] = dot_nt(merged_ref[...], weight_ref[...])


def norm_product(merged, weights):
    rows, depth = merged.shape
    features = weights.shape[0]
    tile = features // 4
    return pl.pallas_call(
        norm_kernel,
        grid=(4,),
        in_specs=[
            pl.BlockSpec((rows, depth), lambda i: (0, 0)),
            pl.BlockSpec((tile, depth), lambda i: (i, 0)),
        ],
        out_specs=pl.BlockSpec((rows, tile), lambda i: (0, i)),
        out_shape=jax.ShapeDtypeStruct((rows, features), jnp.float32),
        compiler_params=pltpu.CompilerParams(vmem_limit_bytes=40 * 1024 * 1024),
        cost_estimate=pl.CostEstimate(flops=1, bytes_accessed=1, transcendentals=0),
        name="norm_product",
    )(merged, weights)


def on_device(
    depth, spaces, tensors, inputs, upstream, action_ids, frame_time, action_table, gain, w_qkv, w_out
):
    batch, local_frames, local_space, features = inputs.shape
    actions = action_table.shape[0]
    shard_rows, _, channels = w_qkv.shape
    z = lax.axis_index("frame")
    s = lax.axis_index("space")
    x = lax.axis_index("tensor")
    y, core = s // 2, s % 2
    frames = depth * local_frames
    pairs = batch * local_space // depth
    slots = depth // batch
    slice_width = features // tensors
    head_width = channels // 2
    width = 4 * head_width
    tokens = frames * 2 * pairs

    def ring(value, shift):
        return lax.ppermute(value, "frame", [(i, (i + shift) % depth) for i in range(depth)])

    def swap_z(value, bit):
        return lax.ppermute(value, "frame", [(i, i ^ bit) for i in range(depth)])

    def swap_core(value):
        return lax.ppermute(value, "space", [(i, i ^ 1) for i in range(spaces)])

    def swap_y(value):
        return lax.ppermute(value, "space", [(i, i ^ 2) for i in range(spaces)])

    def swap_x(value):
        return lax.ppermute(value, "tensor", [(0, 1), (1, 0)])

    def join_x(own, other=None):
        if tensors == 2:
            other = swap_x(own) if other is None else other
            first = jnp.where(x == 0, own, other)
            second = jnp.where(x == 0, other, own)
            return jnp.concatenate([first, second], -1)
        return lax.all_gather(own, "tensor", axis=own.ndim - 1, tiled=True)

    def cut_x(value, which=None):
        which = x if which is None else which
        return lax.dynamic_slice_in_dim(value, which * slice_width, slice_width, value.ndim - 1)

    def place(j):
        return j // slots, (j % slots) * pairs

    shards = [w_qkv[:, 0], w_qkv[:, 1], w_qkv[:, 2], w_out]

    def core_half(which):
        return jnp.concatenate(
            [jnp.where(which == 0, t[:, :head_width], t[:, head_width:]) for t in shards], 1
        )

    mine, sent = core_half(core), core_half(1 - core)
    other = swap_core(sent)
    block = jnp.concatenate(
        [jnp.where(core == 0, mine, other), jnp.where(core == 0, other, mine)], 0
    )

    def pieces(rows, k, start, size):
        rollout, first = place((z + k) % depth)
        return lax.dynamic_slice(
            rows, (rollout, 0, first, start), (1, local_frames, pairs, size)
        )[0]

    def collect(k, start):
        piece = jnp.stack([pieces(rows, k, start, slice_width) for rows in (inputs, upstream)])
        return ring(piece, k)

    def settle(weights, k, arrived, row):
        start = (z - k) % depth * (2 * block_rows) + row * block_rows
        return lax.dynamic_update_slice(weights, arrived, (start, 0))

    block_rows = 2 * shard_rows
    arrived = collect(1, x * slice_width)
    block = after(block, arrived)
    blocks, across, joined, all_ids = [], [], [], [action_ids]
    weights = jnp.zeros((features, width), jnp.bfloat16)
    for k in range(1, depth):
        blocks.append(block)
        across.append(swap_y(block))
        crossed = swap_x(arrived) if tensors == 2 else None
        joined.append(join_x(arrived, crossed))
        following = ring(block, 1)
        weights = settle(weights, k - 1, block, y)
        if k > 1:
            weights = settle(weights, k - 2, across[k - 2], 1 - y)
        earlier = [across[-1], joined[-1] if crossed is None else crossed]
        if k + 1 < depth:
            arrived = collect(k + 1, after(x * slice_width, block))
            earlier.append(arrived)
            all_ids.append(ring(after(action_ids, block), k))
            earlier.append(all_ids[-1])
            following, arrived, weights = lax.optimization_barrier(
                (following, arrived, weights, earlier)
            )[:3]
        block = following
    all_ids.append(ring(after(action_ids, blocks[-1]), depth - 1))
    locals_ = [pieces(rows, 0, 0, features) for rows in (inputs, upstream)]
    own_inputs = jnp.concatenate([locals_[0]] + [both_rows[0] for both_rows in joined], 0)
    own_upstream = jnp.concatenate([locals_[1]] + [both_rows[1] for both_rows in joined], 0)
    rollout, _ = place(z)
    ids = jnp.concatenate(
        [
            lax.dynamic_index_in_dim(each, rollout, 0, keepdims=False) for each in all_ids
        ]
    )
    order = (
        (z - jnp.arange(depth, dtype=jnp.int32)[:, None]) % depth * local_frames
        + jnp.arange(local_frames, dtype=jnp.int32)[None, :]
    ).reshape(frames)
    own_time = lax.dynamic_index_in_dim(frame_time, rollout, 0, keepdims=False)
    times = jnp.sum(
        jnp.where(
            order[:, None] == jnp.arange(frames, dtype=jnp.int32)[None, :], own_time[None, :], 0
        ),
        1,
    )
    onehot = (ids[:, None] == jnp.arange(actions, dtype=jnp.int32)[None, :]).astype(jnp.float32)
    embedded = jnp.dot(onehot, action_table, precision=lax.Precision.HIGHEST)
    hidden = own_inputs.astype(jnp.float32) + embedded[:, None, :]
    inverse = lax.rsqrt(jnp.mean(hidden * hidden, -1, keepdims=True) + NORM_EPSILON)
    normed = (hidden * inverse * gain).astype(jnp.bfloat16)

    block, normed, own_upstream, weights, near = lax.optimization_barrier(
        (block, normed, own_upstream, weights, across[-1])
    )
    far = swap_y(block)

    def both(own):
        return jnp.concatenate([own, swap_core(own)], 1).reshape(tokens, features)

    all_upstream = both(own_upstream)
    all_normed = both(normed)
    weights = settle(weights, depth - 2, near, 1 - y)
    weights = settle(weights, depth - 1, block, y)
    weights = settle(weights, depth - 1, after(far, all_normed, all_upstream), 1 - y)
    qkv, grad_heads = project(all_normed, all_upstream, weights)
    mixed, merged, peak_qkv, peak_out = temporal_attention(
        qkv.reshape(frames, 2 * pairs, 3 * head_width),
        grad_heads.reshape(frames, 2 * pairs, head_width),
        times,
    )
    flat_mixed = mixed.reshape(tokens, head_width)
    flat_merged = merged.reshape(tokens, 3 * head_width)

    own_bound = tokens * jnp.where(
        lax.broadcasted_iota(jnp.int32, (1, width), 1) < 3 * head_width,
        math.sqrt(features) * jnp.max(jnp.abs(gain)) * jnp.max(peak_qkv),
        UPSTREAM_TOP * jnp.max(peak_out),
    )
    own_bound = jnp.maximum(own_bound, 1e-20)

    def pack(value, bound):
        exponent = jnp.ceil(jnp.log2(bound / WIRE_TOP))
        return jnp.concatenate(
            [value * jnp.exp2(-exponent), jnp.broadcast_to(exponent, (8, width))], 0
        ).astype(WIRE)

    def unpack(sent):
        scale = jnp.exp2(sent[block_rows : block_rows + 1].astype(jnp.float32))
        return sent[:block_rows].astype(jnp.float32) * scale, scale * WIRE_TOP

    def weight_part(k, earlier):
        block_at = after((z - 1 - k) % depth * 2, earlier)
        places = jnp.stack([block_at + y, block_at + 1 - y])
        near, far = weight_product(
            places, block_rows, all_normed, all_upstream, flat_merged, flat_mixed
        )
        return near, pack(far, own_bound)

    def norm_part(rows):
        flat = rows.reshape(frames * pairs, 3 * head_width)
        return norm_product(flat, weights).reshape(frames, pairs, features)

    def chip_sum(k, earlier):
        term, bound = unpack(after(swap_y(weight_parts[k][1]), earlier))
        return weight_parts[k][0] + term, bound + own_bound

    def ring_sum(k, arriving, earlier):
        total, bound = chip_sum(k, earlier)
        term, ring_bound = unpack(arriving)
        return total + term, bound + ring_bound

    weight_parts = [weight_part(0, flat_merged)]
    norm_away = norm_part(after(merged[:, pairs:], weight_parts[0][1]))
    weight_parts.append(weight_part(1, norm_away))
    payload = pack(*chip_sum(0, weight_parts[1][1]))
    norm_here = norm_part(after(merged[:, :pairs], payload))
    partial_norm = norm_here + swap_core(norm_away)
    row_dot = jnp.sum(partial_norm * gain * (hidden * inverse), -1, keepdims=True)
    if tensors == 2:
        x_away = cut_x(partial_norm, 1 - x)
        row_scale = jnp.max(jnp.abs(partial_norm), -1, keepdims=True)
        row_scale = jnp.maximum(row_scale, 1e-20) / WIRE_TOP
        sent = (x_away / row_scale).astype(WIRE)
        row_terms = swap_x(jnp.concatenate([row_dot, row_scale], -1))
        x_terms = swap_x(sent)
    else:
        row_dot = lax.psum(row_dot, "tensor")
        grad_norm = lax.psum_scatter(partial_norm, "tensor", scatter_dimension=2, tiled=True)
        sent = partial_norm
    weight_parts.append(weight_part(2, sent))
    payload = pack(*ring_sum(1, ring(payload, 1), weight_parts[2][1]))
    weight_parts.append(weight_part(3, payload))
    if tensors == 2:
        x_terms, row_terms = after((x_terms, row_terms), weight_parts[3][1])
        row_dot = row_dot + row_terms[..., :1]
        grad_norm = cut_x(partial_norm) + x_terms.astype(jnp.float32) * row_terms[..., 1:]
    unit_rows = (cut_x(own_inputs).astype(jnp.float32) + cut_x(embedded)[:, None, :]) * inverse
    grad_hidden = cut_x(own_upstream).astype(jnp.float32) + inverse * (
        grad_norm * cut_x(gain) - unit_rows * (row_dot / features)
    )
    grad_rows = grad_hidden.astype(jnp.bfloat16)
    returned = [grad_rows[:local_frames]]
    for k in range(1, depth):
        returned.append(
            ring(grad_rows[k * local_frames : (k + 1) * local_frames], depth - k)
        )

    gain_term = jnp.sum(grad_norm * unit_rows, (0, 1))
    action_term = jnp.dot(
        onehot.T, jnp.sum(grad_hidden, 1), precision=lax.Precision.HIGHEST
    )
    small = jnp.concatenate([action_term, gain_term[None, :]], 0)
    small = small + swap_core(small)
    bit = 1
    while bit < depth:
        small = small + swap_z(small, bit)
        bit *= 2

    for k in range(2, depth - 1):
        payload = pack(*ring_sum(k, ring(payload, 1), (small, weight_parts[k + 1][1])))
        if k + 2 < depth:
            weight_parts.append(weight_part(k + 2, payload))
    grad_inputs = jnp.zeros(inputs.shape, jnp.bfloat16)
    for k in range(depth):
        piece = after(returned[k], payload) if k else returned[k]
        target, first = place((z + k) % depth)
        grad_inputs = lax.dynamic_update_slice(
            grad_inputs, join_x(piece)[None], (target, 0, first, 0)
        )
    small = after(small, payload)
    small = join_x(small + swap_y(small))
    total = chip_sum(depth - 1, payload)[0] + unpack(after(ring(payload, 1), small))[0]
    mine = lax.dynamic_slice_in_dim(total, core * shard_rows, shard_rows, 0)
    other = swap_core(lax.dynamic_slice_in_dim(total, (1 - core) * shard_rows, shard_rows, 0))
    first = jnp.where(core == 0, mine, other).reshape(shard_rows, 4, head_width)
    second = jnp.where(core == 0, other, mine).reshape(shard_rows, 4, head_width)
    joined = jnp.concatenate([first, second], 2)
    return (grad_inputs, joined[:, :3], joined[:, 3], small[actions], small[:actions])


def solution(mesh):
    sizes = mesh.shape
    return jax.shard_map(
        functools.partial(on_device, sizes["frame"], sizes["space"], sizes["tensor"]),
        mesh=mesh,
        in_specs=(
            P(None, "frame", "space", None),
            P(None, "frame", "space", None),
            P(None, "frame"),
            P(),
            P(),
            P(),
            P(("frame", "space"), None, "tensor"),
            P(("frame", "space"), "tensor"),
        ),
        out_specs=(
            P(None, "frame", "space", None),
            P(("frame", "space"), None, "tensor"),
            P(("frame", "space"), "tensor"),
            P(),
            P(),
        ),
        check_vma=False,
    )
```

```python
import functools
import math

import jax
import jax.numpy as jnp
from jax import lax
from jax.experimental import pallas as pl
from jax.experimental.pallas import tpu as pltpu
from jax.sharding import PartitionSpec as P

HEAD = 128
NORM_EPSILON = 1e-06
UPSTREAM_TOP = 6.0
WIRE = jnp.float16
WIRE_TOP = 32768.0
VMEM = 58 * 1024 * 1024


def after(value, *earlier):
    return lax.optimization_barrier((value, earlier))[0]


def dot_nt(a, b):
    return lax.dot_general(a, b, (((1,), (1,)), ((), ())), preferred_element_type=jnp.float32)


def dot_nn(a, b):
    return lax.dot_general(a, b, (((1,), (0,)), ((), ())), preferred_element_type=jnp.float32)


def dot_tn(a, b):
    return lax.dot_general(a, b, (((0,), (0,)), ((), ())), preferred_element_type=jnp.float32)


def attention_kernel(
    late_ref, early_ref, qkv_ref, grad_ref, mixed_ref, merged_ref, peak_qkv_ref, peak_out_ref
):
    frames, group, width = grad_ref.shape
    rows = frames * group
    scale = 1.0 / math.sqrt(HEAD)

    def load(ref, start):
        block = ref[:, :, start : start + HEAD]
        if group % 16:
            return block.astype(jnp.float32).reshape(rows, HEAD).astype(jnp.bfloat16)
        return block.reshape(rows, HEAD)

    def store(ref, start, value):
        if group % 16:
            ref[:, :, start : start + HEAD] = value.reshape(frames, group, HEAD).astype(
                jnp.bfloat16
            )
        else:
            ref[:, :, start : start + HEAD] = value.astype(jnp.bfloat16).reshape(
                frames, group, HEAD
            )

    def peak(value):
        return jnp.max(jnp.abs(value).reshape(rows // 8, 8, HEAD), axis=0)

    @pl.when(pl.program_id(0) == 0)
    def _():
        peak_qkv_ref[...] = jnp.zeros_like(peak_qkv_ref)
        peak_out_ref[...] = jnp.zeros_like(peak_out_ref)

    row_id = lax.broadcasted_iota(jnp.int32, (rows, rows), 0)
    col_id = lax.broadcasted_iota(jnp.int32, (rows, rows), 1)
    allowed = (row_id % group == col_id % group) & (early_ref[...] <= late_ref[...])
    starts = range(0, width, HEAD)
    query = [load(qkv_ref, i) for i in starts]
    key = [load(qkv_ref, width + i) for i in starts]
    value = [load(qkv_ref, 2 * width + i) for i in starts]
    grad = [load(grad_ref, i) for i in starts]
    heads = range(len(query))
    scores = [jnp.where(allowed, dot_nt(query[h], key[h]) * scale, -1e30) for h in heads]
    grad_probs = [dot_nt(grad[h], value[h]) for h in heads]
    exponent = [jnp.exp(scores[h] - jnp.max(scores[h], -1, keepdims=True)) for h in heads]
    probabilities = [exponent[h] / jnp.sum(exponent[h], -1, keepdims=True) for h in heads]
    rounded = [probabilities[h].astype(jnp.bfloat16) for h in heads]
    mean_grad = [jnp.sum(grad_probs[h] * probabilities[h], -1, keepdims=True) for h in heads]
    mixed = [dot_nn(rounded[h], value[h]) for h in heads]
    grad_value = [dot_tn(rounded[h], grad[h]) for h in heads]
    grad_scores = [probabilities[h] * (grad_probs[h] - mean_grad[h]) for h in heads]
    high = [grad_scores[h].astype(jnp.bfloat16) for h in heads]
    low = [(grad_scores[h] - high[h].astype(jnp.float32)).astype(jnp.bfloat16) for h in heads]
    grad_query = [(dot_nn(high[h], key[h]) + dot_nn(low[h], key[h])) * scale for h in heads]
    grad_key = [(dot_tn(high[h], query[h]) + dot_tn(low[h], query[h])) * scale for h in heads]
    top_out, top_qkv = peak_out_ref[...], peak_qkv_ref[...]
    for h, start in enumerate(starts):
        store(mixed_ref, start, mixed[h])
        store(merged_ref, start, grad_query[h])
        store(merged_ref, width + start, grad_key[h])
        store(merged_ref, 2 * width + start, grad_value[h])
        top_out = jnp.maximum(top_out, peak(mixed[h]))
        for term in (grad_query[h], grad_key[h], grad_value[h]):
            top_qkv = jnp.maximum(top_qkv, peak(term))
    peak_out_ref[...] = top_out
    peak_qkv_ref[...] = top_qkv


def temporal_attention(qkv, grad_heads, times):
    frames, pairs, width = grad_heads.shape
    group = 16 if pairs % 16 == 0 else 8
    rows = frames * group
    per_row = jnp.repeat(times.astype(jnp.float32), group)
    work = pairs // group * rows * rows * (width // HEAD)
    fixed = lambda i: (0, 0)
    moving = lambda i: (0, i, 0)
    return pl.pallas_call(
        attention_kernel,
        grid=(pairs // group,),
        in_specs=[
            pl.BlockSpec((rows, 1), fixed),
            pl.BlockSpec((1, rows), fixed),
            pl.BlockSpec((frames, group, 3 * width), moving),
            pl.BlockSpec((frames, group, width), moving),
        ],
        out_specs=[
            pl.BlockSpec((frames, group, width), moving),
            pl.BlockSpec((frames, group, 3 * width), moving),
            pl.BlockSpec((8, HEAD), fixed),
            pl.BlockSpec((8, HEAD), fixed),
        ],
        out_shape=[
            jax.ShapeDtypeStruct((frames, pairs, width), jnp.bfloat16),
            jax.ShapeDtypeStruct((frames, pairs, 3 * width), jnp.bfloat16),
            jax.ShapeDtypeStruct((8, HEAD), jnp.float32),
            jax.ShapeDtypeStruct((8, HEAD), jnp.float32),
        ],
        compiler_params=pltpu.CompilerParams(vmem_limit_bytes=VMEM),
        cost_estimate=pl.CostEstimate(
            flops=16 * work * HEAD,
            bytes_accessed=16 * frames * pairs * width,
            transcendentals=work,
        ),
        name="temporal_attention",
    )(per_row[:, None], per_row[None, :], qkv, grad_heads)


def weight_kernel(
    place_ref, norm_near, norm_far, up_near, up_far, merged_ref, mixed_ref, near_ref, far_ref, turned
):
    step = pl.program_id(0)
    rows = near_ref.shape[0]

    @pl.when(step == 0)
    def _():
        turned[:rows] = norm_near[...].T
        turned[rows:] = norm_far[...].T

    @pl.when(step < 3)
    def _():
        near_ref[...] = dot_nn(turned[:rows], merged_ref[...])
        far_ref[...] = dot_nn(turned[rows:], merged_ref[...])

    @pl.when(step == 3)
    def _():
        near_ref[...] = dot_tn(up_near[...], mixed_ref[...])
        far_ref[...] = dot_tn(up_far[...], mixed_ref[...])


def weight_product(places, rows, normed, upstream, merged, mixed):
    tokens, width = mixed.shape
    near = pl.BlockSpec((tokens, rows), lambda i, at: (0, at[0]))
    far = pl.BlockSpec((tokens, rows), lambda i, at: (0, at[1]))
    out = pl.BlockSpec((rows, width), lambda i, at: (0, i))
    return pl.pallas_call(
        weight_kernel,
        grid_spec=pltpu.PrefetchScalarGridSpec(
            num_scalar_prefetch=1,
            grid=(4,),
            in_specs=[
                near,
                far,
                near,
                far,
                pl.BlockSpec((tokens, width), lambda i, at: (0, jnp.minimum(i, 2))),
                pl.BlockSpec((tokens, width), lambda i, at: (0, 0)),
            ],
            out_specs=[out, out],
            scratch_shapes=[pltpu.VMEM((2 * rows, tokens), jnp.bfloat16)],
        ),
        out_shape=[jax.ShapeDtypeStruct((rows, 4 * width), jnp.float32)] * 2,
        compiler_params=pltpu.CompilerParams(vmem_limit_bytes=VMEM),
        cost_estimate=pl.CostEstimate(flops=1, bytes_accessed=1, transcendentals=0),
        name="weight_product",
    )(places, normed, normed, upstream, upstream, merged, mixed)


def project_kernel(normed_ref, up_ref, weight_ref, qkv_ref, grad_ref):
    @pl.when(pl.program_id(0) < 3)
    def _():
        qkv_ref[...] = dot_nn(normed_ref[...], weight_ref[...]).astype(jnp.bfloat16)

    @pl.when(pl.program_id(0) == 3)
    def _():
        grad_ref[...] = dot_nn(up_ref[...], weight_ref[...]).astype(jnp.bfloat16)


def project(normed, upstream, weights):
    tokens, features = normed.shape
    width = weights.shape[1] // 4
    rows = tokens // 2
    return pl.pallas_call(
        project_kernel,
        grid=(4, 2),
        in_specs=[
            pl.BlockSpec((rows, features), lambda i, j: (jnp.where(i < 3, j, 1), 0)),
            pl.BlockSpec((rows, features), lambda i, j: (jnp.where(i < 3, 0, j), 0)),
            pl.BlockSpec((features, width), lambda i, j: (0, i)),
        ],
        out_specs=[
            pl.BlockSpec(
                (rows, width), lambda i, j: (jnp.where(i < 3, j, 1), jnp.minimum(i, 2))
            ),
            pl.BlockSpec((rows, width), lambda i, j: (jnp.where(i < 3, 0, j), 0)),
        ],
        out_shape=[
            jax.ShapeDtypeStruct((tokens, 3 * width), jnp.bfloat16),
            jax.ShapeDtypeStruct((tokens, width), jnp.bfloat16),
        ],
        compiler_params=pltpu.CompilerParams(vmem_limit_bytes=VMEM),
        cost_estimate=pl.CostEstimate(
            flops=2 * tokens * features * 4 * width,
            bytes_accessed=8 * tokens * features,
            transcendentals=0,
        ),
        name="project",
    )(normed, upstream, weights)


def norm_kernel(merged_ref, weight_ref, out_ref):
    out_ref[...] = dot_nt(merged_ref[...], weight_ref[...])


def norm_product(merged, weights):
    rows, depth = merged.shape
    features = weights.shape[0]
    tile = features // 4
    return pl.pallas_call(
        norm_kernel,
        grid=(4,),
        in_specs=[
            pl.BlockSpec((rows, depth), lambda i: (0, 0)),
            pl.BlockSpec((tile, depth), lambda i: (i, 0)),
        ],
        out_specs=pl.BlockSpec((rows, tile), lambda i: (0, i)),
        out_shape=jax.ShapeDtypeStruct((rows, features), jnp.float32),
        compiler_params=pltpu.CompilerParams(vmem_limit_bytes=VMEM),
        cost_estimate=pl.CostEstimate(flops=1, bytes_accessed=1, transcendentals=0),
        name="norm_product",
    )(merged, weights)


def on_device(
    depth, spaces, tensors, inputs, upstream, action_ids, frame_time, action_table, gain, w_qkv, w_out
):
    batch, local_frames, local_space, features = inputs.shape
    actions = action_table.shape[0]
    shard_rows, _, channels = w_qkv.shape
    z = lax.axis_index("frame")
    s = lax.axis_index("space")
    x = lax.axis_index("tensor")
    y, core = s // 2, s % 2
    frames = depth * local_frames
    pairs = batch * local_space // depth
    slots = depth // batch
    slice_width = features // tensors
    head_width = channels // 2
    width = 4 * head_width
    tokens = frames * 2 * pairs

    def ring(value, shift):
        return lax.ppermute(value, "frame", [(i, (i + shift) % depth) for i in range(depth)])

    def swap_z(value, bit):
        return lax.ppermute(value, "frame", [(i, i ^ bit) for i in range(depth)])

    def swap_core(value):
        return lax.ppermute(value, "space", [(i, i ^ 1) for i in range(spaces)])

    def swap_y(value):
        return lax.ppermute(value, "space", [(i, i ^ 2) for i in range(spaces)])

    def swap_x(value):
        return lax.ppermute(value, "tensor", [(0, 1), (1, 0)])

    def join_x(own, other=None):
        if tensors == 2:
            other = swap_x(own) if other is None else other
            first = jnp.where(x == 0, own, other)
            second = jnp.where(x == 0, other, own)
            return jnp.concatenate([first, second], -1)
        return lax.all_gather(own, "tensor", axis=own.ndim - 1, tiled=True)

    def cut_x(value, which=None):
        which = x if which is None else which
        return lax.dynamic_slice_in_dim(value, which * slice_width, slice_width, value.ndim - 1)

    def place(j):
        return j // slots, (j % slots) * pairs

    shards = [w_qkv[:, 0], w_qkv[:, 1], w_qkv[:, 2], w_out]

    def core_half(which):
        return jnp.concatenate(
            [jnp.where(which == 0, t[:, :head_width], t[:, head_width:]) for t in shards], 1
        )

    mine, sent = core_half(core), core_half(1 - core)
    other = swap_core(sent)
    block = jnp.concatenate(
        [jnp.where(core == 0, mine, other), jnp.where(core == 0, other, mine)], 0
    )

    def pieces(rows, k, start, size):
        rollout, first = place((z + k) % depth)
        return lax.dynamic_slice(
            rows, (rollout, 0, first, start), (1, local_frames, pairs, size)
        )[0]

    def collect(k, start):
        piece = jnp.stack([pieces(rows, k, start, slice_width) for rows in (inputs, upstream)])
        return ring(piece, k)

    def settle(weights, k, arrived, row, offset=0):
        start = (z - k) % depth * (2 * block_rows) + row * block_rows + offset
        return lax.dynamic_update_slice(weights, arrived, (start, 0))

    block_rows = 2 * shard_rows
    arrived = collect(1, x * slice_width)
    blocks, across, joined, all_ids = [], [], [], [action_ids]
    weights = jnp.zeros((features, width), jnp.bfloat16)
    for k in range(1, depth):
        blocks.append(block)
        across.append(swap_y(block))
        if k + 1 < depth:
            following = ring(block, 1)
            earlier = [across[-1]]
        else:
            following = [ring(block[:shard_rows], 1), ring(block[shard_rows:], 1)]
            earlier = [across[-1], swap_y(following[0])]
        weights = settle(weights, k - 1, block, y)
        if k > 1:
            crossed = swap_x(arrived) if tensors == 2 else None
            joined.append(join_x(arrived, crossed))
            earlier.append(joined[-1] if crossed is None else crossed)
            arrived = collect(k, after(x * slice_width, block))
            weights = settle(weights, k - 2, across[k - 2], 1 - y)
        all_ids.append(ring(after(action_ids, block), k))
        block, arrived, weights, all_ids[-1], earlier = lax.optimization_barrier(
            (following, arrived, weights, all_ids[-1], earlier)
        )
    joined.append(join_x(arrived))
    near = earlier[0]
    last = [*block, earlier[1], swap_y(block[1])]
    locals_ = [pieces(rows, 0, 0, features) for rows in (inputs, upstream)]
    own_inputs = jnp.concatenate([locals_[0]] + [both_rows[0] for both_rows in joined], 0)
    own_upstream = jnp.concatenate([locals_[1]] + [both_rows[1] for both_rows in joined], 0)
    rollout, _ = place(z)
    ids = jnp.concatenate(
        [
            lax.dynamic_index_in_dim(each, rollout, 0, keepdims=False) for each in all_ids
        ]
    )
    order = (
        (z - jnp.arange(depth, dtype=jnp.int32)[:, None]) % depth * local_frames
        + jnp.arange(local_frames, dtype=jnp.int32)[None, :]
    ).reshape(frames)
    own_time = lax.dynamic_index_in_dim(frame_time, rollout, 0, keepdims=False)
    times = jnp.sum(
        jnp.where(
            order[:, None] == jnp.arange(frames, dtype=jnp.int32)[None, :], own_time[None, :], 0
        ),
        1,
    )
    onehot = (ids[:, None] == jnp.arange(actions, dtype=jnp.int32)[None, :]).astype(jnp.float32)
    embedded = jnp.dot(onehot, action_table, precision=lax.Precision.HIGHEST)
    hidden = own_inputs.astype(jnp.float32) + embedded[:, None, :]
    inverse = lax.rsqrt(jnp.mean(hidden * hidden, -1, keepdims=True) + NORM_EPSILON)
    normed = (hidden * inverse * gain).astype(jnp.bfloat16)

    def both(own):
        return jnp.concatenate([own, swap_core(own)], 1).reshape(tokens, features)

    all_upstream = both(own_upstream)
    all_normed = both(normed)
    weights = settle(weights, depth - 2, near, 1 - y)
    last[3] = after(last[3], all_normed, all_upstream)
    for i, part in enumerate(last):
        weights = settle(
            weights, depth - 1, part, 1 - y if i >= 2 else y, offset=i % 2 * shard_rows
        )
    qkv, grad_heads = project(all_normed, all_upstream, weights)
    mixed, merged, peak_qkv, peak_out = temporal_attention(
        qkv.reshape(frames, 2 * pairs, 3 * head_width),
        grad_heads.reshape(frames, 2 * pairs, head_width),
        times,
    )
    flat_mixed = mixed.reshape(tokens, head_width)
    flat_merged = merged.reshape(tokens, 3 * head_width)

    own_bound = tokens * jnp.where(
        lax.broadcasted_iota(jnp.int32, (1, width), 1) < 3 * head_width,
        math.sqrt(features) * jnp.max(jnp.abs(gain)) * jnp.max(peak_qkv),
        UPSTREAM_TOP * jnp.max(peak_out),
    )
    own_bound = jnp.maximum(own_bound, 1e-20)

    def pack(value, bound):
        exponent = jnp.ceil(jnp.log2(bound / WIRE_TOP))
        return jnp.concatenate(
            [value * jnp.exp2(-exponent), jnp.broadcast_to(exponent, (8, width))], 0
        ).astype(WIRE)

    def unpack(sent):
        scale = jnp.exp2(sent[block_rows : block_rows + 1].astype(jnp.float32))
        return sent[:block_rows].astype(jnp.float32) * scale, scale * WIRE_TOP

    def weight_part(k, earlier):
        block_at = after((z - 1 - k) % depth * 2, earlier)
        places = jnp.stack([block_at + y, block_at + 1 - y])
        near, far = weight_product(
            places, block_rows, all_normed, all_upstream, flat_merged, flat_mixed
        )
        return near, pack(far, own_bound)

    def norm_part(rows):
        flat = rows.reshape(frames * pairs, 3 * head_width)
        return norm_product(flat, weights).reshape(frames, pairs, features)

    def chip_sum(k, earlier):
        term, bound = unpack(after(swap_y(weight_parts[k][1]), earlier))
        return weight_parts[k][0] + term, bound + own_bound

    def ring_sum(k, arriving, earlier):
        total, bound = chip_sum(k, earlier)
        term, ring_bound = unpack(arriving)
        return total + term, bound + ring_bound

    weight_parts = [weight_part(0, flat_merged)]
    norm_away = norm_part(after(merged[:, pairs:], weight_parts[0][1]))
    weight_parts.append(weight_part(1, norm_away))
    payload = pack(*chip_sum(0, weight_parts[1][1]))
    norm_here = norm_part(after(merged[:, :pairs], payload))
    partial_norm = norm_here + swap_core(after(norm_away, payload))
    row_dot = jnp.sum(partial_norm * gain * (hidden * inverse), -1, keepdims=True)
    if tensors == 2:
        x_away = cut_x(partial_norm, 1 - x)
        row_scale = jnp.max(jnp.abs(partial_norm), -1, keepdims=True)
        row_scale = jnp.maximum(row_scale, 1e-20) / WIRE_TOP
        sent = (x_away / row_scale).astype(WIRE)
        row_terms = swap_x(jnp.concatenate([row_dot, row_scale], -1))
        x_terms = swap_x(sent)
    else:
        row_dot = lax.psum(row_dot, "tensor")
        grad_norm = lax.psum_scatter(partial_norm, "tensor", scatter_dimension=2, tiled=True)
        sent = partial_norm
    weight_parts.append(weight_part(2, sent))
    payload = pack(*ring_sum(1, ring(payload, 1), weight_parts[2][1]))
    weight_parts.append(weight_part(3, payload))
    if tensors == 2:
        x_terms, row_terms = after((x_terms, row_terms), weight_parts[3][1])
        row_dot = row_dot + row_terms[..., :1]
        grad_norm = cut_x(partial_norm) + x_terms.astype(jnp.float32) * row_terms[..., 1:]
    unit_rows = (cut_x(own_inputs).astype(jnp.float32) + cut_x(embedded)[:, None, :]) * inverse
    grad_hidden = cut_x(own_upstream).astype(jnp.float32) + inverse * (
        grad_norm * cut_x(gain) - unit_rows * (row_dot / features)
    )
    grad_rows = grad_hidden.astype(jnp.bfloat16)
    returned = [grad_rows[:local_frames]]
    for k in range(1, depth):
        returned.append(
            ring(grad_rows[k * local_frames : (k + 1) * local_frames], depth - k)
        )

    gain_term = jnp.sum(grad_norm * unit_rows, (0, 1))
    action_term = jnp.dot(
        onehot.T, jnp.sum(grad_hidden, 1), precision=lax.Precision.HIGHEST
    )
    small = jnp.concatenate([action_term, gain_term[None, :]], 0)
    small = small + swap_core(small)
    for k in range(2, depth - 1):
        payload = pack(*ring_sum(k, ring(payload, 1), (small, returned[1:])))
        if k + 2 < depth:
            weight_parts.append(weight_part(k + 2, payload))
    grad_inputs = jnp.zeros(inputs.shape, jnp.bfloat16)
    for k in range(depth):
        piece = after(returned[k], payload)
        target, first = place((z + k) % depth)
        grad_inputs = lax.dynamic_update_slice(
            grad_inputs, join_x(piece)[None], (target, 0, first, 0)
        )
    total = chip_sum(depth - 1, payload)[0]
    small = after(small, total)
    small = join_x(small + swap_y(small))
    arriving, small = lax.optimization_barrier((ring(payload, 1), small))
    total = total + unpack(arriving)[0]
    bit = 1
    while bit < depth:
        small = small + swap_z(small, bit)
        bit *= 2
    mine = lax.dynamic_slice_in_dim(total, core * shard_rows, shard_rows, 0)
    other = swap_core(lax.dynamic_slice_in_dim(total, (1 - core) * shard_rows, shard_rows, 0))
    first = jnp.where(core == 0, mine, other).reshape(shard_rows, 4, head_width)
    second = jnp.where(core == 0, other, mine).reshape(shard_rows, 4, head_width)
    joined = jnp.concatenate([first, second], 2)
    return (grad_inputs, joined[:, :3], joined[:, 3], small[actions], small[:actions])


def solution(mesh):
    sizes = mesh.shape
    return jax.shard_map(
        functools.partial(on_device, sizes["frame"], sizes["space"], sizes["tensor"]),
        mesh=mesh,
        in_specs=(
            P(None, "frame", "space", None),
            P(None, "frame", "space", None),
            P(None, "frame"),
            P(),
            P(),
            P(),
            P(("frame", "space"), None, "tensor"),
            P(("frame", "space"), "tensor"),
        ),
        out_specs=(
            P(None, "frame", "space", None),
            P(("frame", "space"), None, "tensor"),
            P(("frame", "space"), "tensor"),
            P(),
            P(),
        ),
        check_vma=False,
    )
```

```python
import functools
import math

import jax
import jax.numpy as jnp
from jax import lax
from jax.experimental import pallas as pl
from jax.experimental.pallas import tpu as pltpu
from jax.sharding import PartitionSpec as P

HEAD = 128
NORM_EPSILON = 1e-06
UPSTREAM_TOP = 6.0
WIRE = jnp.float16
WIRE_TOP = 32768.0
MIB = 1024 * 1024


def after(value, *earlier):
    return lax.optimization_barrier((value, earlier))[0]


def dot_nt(a, b):
    return lax.dot_general(a, b, (((1,), (1,)), ((), ())), preferred_element_type=jnp.float32)


def dot_nn(a, b):
    return lax.dot_general(a, b, (((1,), (0,)), ((), ())), preferred_element_type=jnp.float32)


def dot_tn(a, b):
    return lax.dot_general(a, b, (((0,), (0,)), ((), ())), preferred_element_type=jnp.float32)


def attention_kernel(
    late_ref, early_ref, qkv_ref, grad_ref, mixed_ref, merged_ref, peak_ref
):
    frames, group, width = grad_ref.shape
    rows = frames * group
    scale = 1.0 / math.sqrt(HEAD)

    def load(ref, start):
        block = ref[:, :, start : start + HEAD]
        if group % 16:
            return block.astype(jnp.float32).reshape(rows, HEAD).astype(jnp.bfloat16)
        return block.reshape(rows, HEAD)

    def store(ref, start, value):
        if group % 16:
            ref[:, :, start : start + HEAD] = value.reshape(frames, group, HEAD).astype(
                jnp.bfloat16
            )
        else:
            ref[:, :, start : start + HEAD] = value.astype(jnp.bfloat16).reshape(
                frames, group, HEAD
            )

    def peak(value):
        return jnp.max(jnp.abs(value).reshape(rows // 8, 8, HEAD), axis=0)

    @pl.when(pl.program_id(0) == 0)
    def _():
        peak_ref[...] = jnp.zeros_like(peak_ref)

    row_id = lax.broadcasted_iota(jnp.int32, (rows, rows), 0)
    col_id = lax.broadcasted_iota(jnp.int32, (rows, rows), 1)
    allowed = (row_id % group == col_id % group) & (early_ref[...] <= late_ref[...])
    starts = range(0, width, HEAD)
    query = [load(qkv_ref, i) for i in starts]
    key = [load(qkv_ref, width + i) for i in starts]
    value = [load(qkv_ref, 2 * width + i) for i in starts]
    grad = [load(grad_ref, i) for i in starts]
    heads = range(len(query))
    scores = [jnp.where(allowed, dot_nt(query[h], key[h]) * scale, -1e30) for h in heads]
    grad_probs = [dot_nt(grad[h], value[h]) for h in heads]
    exponent = [jnp.exp(scores[h] - jnp.max(scores[h], -1, keepdims=True)) for h in heads]
    probabilities = [exponent[h] / jnp.sum(exponent[h], -1, keepdims=True) for h in heads]
    rounded = [probabilities[h].astype(jnp.bfloat16) for h in heads]
    mean_grad = [jnp.sum(grad_probs[h] * probabilities[h], -1, keepdims=True) for h in heads]
    mixed = [dot_nn(rounded[h], value[h]) for h in heads]
    grad_value = [dot_tn(rounded[h], grad[h]) for h in heads]
    grad_scores = [probabilities[h] * (grad_probs[h] - mean_grad[h]) for h in heads]
    high = [grad_scores[h].astype(jnp.bfloat16) for h in heads]
    low = [(grad_scores[h] - high[h].astype(jnp.float32)).astype(jnp.bfloat16) for h in heads]
    grad_query = [(dot_nn(high[h], key[h]) + dot_nn(low[h], key[h])) * scale for h in heads]
    grad_key = [(dot_tn(high[h], query[h]) + dot_tn(low[h], query[h])) * scale for h in heads]
    top_out, top_qkv = peak_ref[0], peak_ref[1]
    for h, start in enumerate(starts):
        store(mixed_ref, start, mixed[h])
        store(merged_ref, start, grad_query[h])
        store(merged_ref, width + start, grad_key[h])
        store(merged_ref, 2 * width + start, grad_value[h])
        top_out = jnp.maximum(top_out, peak(mixed[h]))
        for term in (grad_query[h], grad_key[h], grad_value[h]):
            top_qkv = jnp.maximum(top_qkv, peak(term))
    peak_ref[0] = top_out
    peak_ref[1] = top_qkv


def temporal_attention(qkv, grad_heads, times):
    frames, pairs, width = grad_heads.shape
    group = 16 if pairs % 16 == 0 else 8
    rows = frames * group
    per_row = jnp.repeat(times.astype(jnp.float32), group)
    work = pairs // group * rows * rows * (width // HEAD)
    fixed = lambda i: (0, 0)
    moving = lambda i: (0, i, 0)
    return pl.pallas_call(
        attention_kernel,
        grid=(pairs // group,),
        in_specs=[
            pl.BlockSpec((rows, 1), fixed),
            pl.BlockSpec((1, rows), fixed),
            pl.BlockSpec((frames, group, 3 * width), moving),
            pl.BlockSpec((frames, group, width), moving),
        ],
        out_specs=[
            pl.BlockSpec((frames, group, width), moving),
            pl.BlockSpec((frames, group, 3 * width), moving),
            pl.BlockSpec((2, 8, HEAD), lambda i: (0, 0, 0)),
        ],
        out_shape=[
            jax.ShapeDtypeStruct((frames, pairs, width), jnp.bfloat16),
            jax.ShapeDtypeStruct((frames, pairs, 3 * width), jnp.bfloat16),
            jax.ShapeDtypeStruct((2, 8, HEAD), jnp.float32),
        ],
        compiler_params=pltpu.CompilerParams(vmem_limit_bytes=16 * MIB),
        cost_estimate=pl.CostEstimate(
            flops=16 * work * HEAD,
            bytes_accessed=16 * frames * pairs * width,
            transcendentals=work,
        ),
        name="temporal_attention",
    )(per_row[:, None], per_row[None, :], qkv, grad_heads)


def turn_kernel(rows_ref, out_ref):
    out_ref[...] = rows_ref[...].T


def turn(rows):
    tokens, features = rows.shape
    tile = features // 8
    return pl.pallas_call(
        turn_kernel,
        grid=(8,),
        in_specs=[pl.BlockSpec((tokens, tile), lambda i: (0, i))],
        out_specs=pl.BlockSpec((tile, tokens), lambda i: (i, 0)),
        out_shape=jax.ShapeDtypeStruct((features, tokens), rows.dtype),
        compiler_params=pltpu.CompilerParams(vmem_limit_bytes=12 * MIB),
        cost_estimate=pl.CostEstimate(flops=1, bytes_accessed=1, transcendentals=0),
        name="turn",
    )(rows)


def weight_kernel(
    place_ref, norm_near, norm_far, up_near, up_far, merged_ref, mixed_ref, near_ref, far_ref
):
    step = pl.program_id(0)

    @pl.when(step < 3)
    def _():
        near_ref[...] = dot_nn(norm_near[...], merged_ref[...])
        far_ref[...] = dot_nn(norm_far[...], merged_ref[...])

    @pl.when(step == 3)
    def _():
        near_ref[...] = dot_nn(up_near[...], mixed_ref[...])
        far_ref[...] = dot_nn(up_far[...], mixed_ref[...])


def weight_product(places, rows, normed, upstream, merged, mixed):
    tokens, width = mixed.shape
    near = pl.BlockSpec((rows, tokens), lambda i, at: (at[0], 0))
    far = pl.BlockSpec((rows, tokens), lambda i, at: (at[1], 0))
    out = pl.BlockSpec((rows, width), lambda i, at: (0, i))
    return pl.pallas_call(
        weight_kernel,
        grid_spec=pltpu.PrefetchScalarGridSpec(
            num_scalar_prefetch=1,
            grid=(4,),
            in_specs=[
                near,
                far,
                near,
                far,
                pl.BlockSpec((tokens, width), lambda i, at: (0, jnp.minimum(i, 2))),
                pl.BlockSpec((tokens, width), lambda i, at: (0, 0)),
            ],
            out_specs=[out, out],
        ),
        out_shape=[jax.ShapeDtypeStruct((rows, 4 * width), jnp.float32)] * 2,
        compiler_params=pltpu.CompilerParams(vmem_limit_bytes=20 * MIB),
        cost_estimate=pl.CostEstimate(flops=1, bytes_accessed=1, transcendentals=0),
        name="weight_product",
    )(places, normed, normed, upstream, upstream, merged, mixed)


def project_kernel(normed_ref, up_ref, weight_ref, qkv_ref, grad_ref):
    @pl.when(pl.program_id(0) < 3)
    def _():
        qkv_ref[...] = dot_nn(normed_ref[...], weight_ref[...]).astype(jnp.bfloat16)

    @pl.when(pl.program_id(0) == 3)
    def _():
        grad_ref[...] = dot_nn(up_ref[...], weight_ref[...]).astype(jnp.bfloat16)


def project(normed, upstream, weights):
    tokens, features = normed.shape
    width = weights.shape[1] // 4
    rows = tokens // 2
    return pl.pallas_call(
        project_kernel,
        grid=(4, 2),
        in_specs=[
            pl.BlockSpec((rows, features), lambda i, j: (jnp.where(i < 3, j, 1), 0)),
            pl.BlockSpec((rows, features), lambda i, j: (jnp.where(i < 3, 0, j), 0)),
            pl.BlockSpec((features, width), lambda i, j: (0, i)),
        ],
        out_specs=[
            pl.BlockSpec(
                (rows, width), lambda i, j: (jnp.where(i < 3, j, 1), jnp.minimum(i, 2))
            ),
            pl.BlockSpec((rows, width), lambda i, j: (jnp.where(i < 3, 0, j), 0)),
        ],
        out_shape=[
            jax.ShapeDtypeStruct((tokens, 3 * width), jnp.bfloat16),
            jax.ShapeDtypeStruct((tokens, width), jnp.bfloat16),
        ],
        compiler_params=pltpu.CompilerParams(vmem_limit_bytes=26 * MIB),
        cost_estimate=pl.CostEstimate(
            flops=2 * tokens * features * 4 * width,
            bytes_accessed=8 * tokens * features,
            transcendentals=0,
        ),
        name="project",
    )(normed, upstream, weights)


def norm_kernel(merged_ref, weight_ref, out_ref):
    out_ref[...] = dot_nt(merged_ref[...], weight_ref[...])


def norm_product(merged, weights):
    rows, depth = merged.shape
    features = weights.shape[0]
    tile = features // 4
    return pl.pallas_call(
        norm_kernel,
        grid=(4,),
        in_specs=[
            pl.BlockSpec((rows, depth), lambda i: (0, 0)),
            pl.BlockSpec((tile, depth), lambda i: (i, 0)),
        ],
        out_specs=pl.BlockSpec((rows, tile), lambda i: (0, i)),
        out_shape=jax.ShapeDtypeStruct((rows, features), jnp.float32),
        compiler_params=pltpu.CompilerParams(vmem_limit_bytes=18 * MIB),
        cost_estimate=pl.CostEstimate(flops=1, bytes_accessed=1, transcendentals=0),
        name="norm_product",
    )(merged, weights)


def on_device(
    depth, spaces, tensors, inputs, upstream, action_ids, frame_time, action_table, gain, w_qkv, w_out
):
    batch, local_frames, local_space, features = inputs.shape
    actions = action_table.shape[0]
    shard_rows, _, channels = w_qkv.shape
    z = lax.axis_index("frame")
    s = lax.axis_index("space")
    x = lax.axis_index("tensor")
    y, core = s // 2, s % 2
    frames = depth * local_frames
    pairs = batch * local_space // depth
    slots = depth // batch
    slice_width = features // tensors
    head_width = channels // 2
    width = 4 * head_width
    tokens = frames * 2 * pairs

    def ring(value, shift):
        return lax.ppermute(value, "frame", [(i, (i + shift) % depth) for i in range(depth)])

    def swap_z(value, bit):
        return lax.ppermute(value, "frame", [(i, i ^ bit) for i in range(depth)])

    def swap_core(value):
        return lax.ppermute(value, "space", [(i, i ^ 1) for i in range(spaces)])

    def swap_y(value):
        return lax.ppermute(value, "space", [(i, i ^ 2) for i in range(spaces)])

    def swap_x(value):
        return lax.ppermute(value, "tensor", [(0, 1), (1, 0)])

    def join_x(own, other=None):
        if tensors == 2:
            other = swap_x(own) if other is None else other
            first = jnp.where(x == 0, own, other)
            second = jnp.where(x == 0, other, own)
            return jnp.concatenate([first, second], -1)
        return lax.all_gather(own, "tensor", axis=own.ndim - 1, tiled=True)

    def cut_x(value, which=None):
        which = x if which is None else which
        return lax.dynamic_slice_in_dim(value, which * slice_width, slice_width, value.ndim - 1)

    def place(j):
        return j // slots, (j % slots) * pairs

    shards = [w_qkv[:, 0], w_qkv[:, 1], w_qkv[:, 2], w_out]

    def core_half(which):
        return jnp.concatenate(
            [jnp.where(which == 0, t[:, :head_width], t[:, head_width:]) for t in shards], 1
        )

    mine, sent = core_half(core), core_half(1 - core)
    other = swap_core(sent)
    block = jnp.concatenate(
        [jnp.where(core == 0, mine, other), jnp.where(core == 0, other, mine)], 0
    )

    def pieces(rows, k, start, size):
        rollout, first = place((z + k) % depth)
        return lax.dynamic_slice(
            rows, (rollout, 0, first, start), (1, local_frames, pairs, size)
        )[0]

    def collect(k, start):
        piece = jnp.stack([pieces(rows, k, start, slice_width) for rows in (inputs, upstream)])
        return ring(piece, k)

    def settle(weights, k, arrived, row):
        start = (z - k) % depth * (2 * block_rows) + row * block_rows
        return lax.dynamic_update_slice(weights, arrived, (start, 0))

    block_rows = 2 * shard_rows
    arrived = collect(1, x * slice_width)
    blocks, across, joined = [], [], []
    all_ids = [action_ids] + [ring(after(action_ids, block), k) for k in range(1, depth)]
    weights = after(jnp.zeros((features, width), jnp.bfloat16), arrived)
    for k in range(1, depth):
        blocks.append(block)
        across.append(swap_y(block))
        crossed = swap_x(arrived) if tensors == 2 else None
        joined.append(join_x(arrived, crossed))
        following = ring(block, 1)
        weights = settle(weights, k - 1, block, y)
        if k > 1:
            weights = settle(weights, k - 2, across[k - 2], 1 - y)
        earlier = [across[-1], joined[-1] if crossed is None else crossed]
        if k + 1 < depth:
            arrived = collect(k + 1, after(x * slice_width, block))
            following, arrived, weights, all_ids, earlier = lax.optimization_barrier(
                (following, arrived, weights, all_ids, earlier)
            )
        block = following
    locals_ = [pieces(rows, 0, 0, features) for rows in (inputs, upstream)]
    own_inputs = jnp.concatenate([locals_[0]] + [both_rows[0] for both_rows in joined], 0)
    own_upstream = jnp.concatenate([locals_[1]] + [both_rows[1] for both_rows in joined], 0)
    rollout, _ = place(z)
    ids = jnp.concatenate(
        [
            lax.dynamic_index_in_dim(each, rollout, 0, keepdims=False) for each in all_ids
        ]
    )
    order = (
        (z - jnp.arange(depth, dtype=jnp.int32)[:, None]) % depth * local_frames
        + jnp.arange(local_frames, dtype=jnp.int32)[None, :]
    ).reshape(frames)
    own_time = lax.dynamic_index_in_dim(frame_time, rollout, 0, keepdims=False)
    times = jnp.sum(
        jnp.where(
            order[:, None] == jnp.arange(frames, dtype=jnp.int32)[None, :], own_time[None, :], 0
        ),
        1,
    )
    onehot = (ids[:, None] == jnp.arange(actions, dtype=jnp.int32)[None, :]).astype(jnp.float32)
    embedded = jnp.dot(onehot, action_table, precision=lax.Precision.HIGHEST)
    hidden = own_inputs.astype(jnp.float32) + embedded[:, None, :]
    inverse = lax.rsqrt(jnp.mean(hidden * hidden, -1, keepdims=True) + NORM_EPSILON)
    normed = (hidden * inverse * gain).astype(jnp.bfloat16)

    block, normed, own_upstream, weights, near = lax.optimization_barrier(
        (block, normed, own_upstream, weights, across[-1])
    )
    far = swap_y(block)

    def both(own):
        return jnp.concatenate([own, swap_core(own)], 1).reshape(tokens, features)

    all_upstream = both(own_upstream)
    all_normed = both(normed)
    normed_t, upstream_t = turn(all_normed), turn(all_upstream)
    weights = settle(weights, depth - 2, near, 1 - y)
    weights = settle(weights, depth - 1, block, y)
    weights = settle(weights, depth - 1, after(far, normed_t, upstream_t), 1 - y)
    qkv, grad_heads = project(all_normed, all_upstream, weights)
    mixed, merged, peaks = temporal_attention(
        qkv.reshape(frames, 2 * pairs, 3 * head_width),
        grad_heads.reshape(frames, 2 * pairs, head_width),
        times,
    )
    flat_mixed = mixed.reshape(tokens, head_width)
    flat_merged = merged.reshape(tokens, 3 * head_width)

    peaks = jnp.max(peaks, (1, 2))
    own_bound = tokens * jnp.where(
        lax.broadcasted_iota(jnp.int32, (1, width), 1) < 3 * head_width,
        math.sqrt(features) * jnp.max(jnp.abs(gain)) * peaks[1],
        UPSTREAM_TOP * peaks[0],
    )
    own_bound = jnp.maximum(own_bound, 1e-20)

    def pack(value, bound):
        exponent = jnp.ceil(jnp.log2(bound / WIRE_TOP))
        return jnp.concatenate(
            [value * jnp.exp2(-exponent), jnp.broadcast_to(exponent, (8, width))], 0
        ).astype(WIRE)

    def unpack(sent):
        scale = jnp.exp2(sent[block_rows : block_rows + 1].astype(jnp.float32))
        return sent[:block_rows].astype(jnp.float32) * scale, scale * WIRE_TOP

    def weight_part(k, earlier):
        block_at = after((z - 1 - k) % depth * 2, earlier)
        places = jnp.stack([block_at + y, block_at + 1 - y])
        near, far = weight_product(
            places, block_rows, normed_t, upstream_t, flat_merged, flat_mixed
        )
        return near, pack(far, own_bound)

    def norm_part(rows):
        flat = rows.reshape(frames * pairs, 3 * head_width)
        return norm_product(flat, weights).reshape(frames, pairs, features)

    def chip_sum(k, earlier):
        term, bound = unpack(after(swap_y(weight_parts[k][1]), earlier))
        return weight_parts[k][0] + term, bound + own_bound

    def ring_sum(k, arriving, earlier):
        total, bound = chip_sum(k, earlier)
        term, ring_bound = unpack(arriving)
        return total + term, bound + ring_bound

    weight_parts = [weight_part(0, flat_merged)]
    norm_away = norm_part(after(merged[:, pairs:], weight_parts[0][1]))
    weight_parts.append(weight_part(1, norm_away))
    payload = pack(*chip_sum(0, weight_parts[1][1]))
    norm_here = norm_part(after(merged[:, :pairs], payload))
    partial_norm = norm_here + swap_core(after(norm_away, payload))
    row_dot = jnp.sum(partial_norm * gain * (hidden * inverse), -1, keepdims=True)
    if tensors == 2:
        x_away = cut_x(partial_norm, 1 - x)
        row_scale = jnp.max(jnp.abs(partial_norm), -1, keepdims=True)
        row_scale = jnp.maximum(row_scale, 1e-20) / WIRE_TOP
        sent = (x_away / row_scale).astype(WIRE)
        row_terms = swap_x(jnp.concatenate([row_dot, row_scale], -1))
        x_terms = swap_x(sent)
    else:
        row_dot = lax.psum(row_dot, "tensor")
        grad_norm = lax.psum_scatter(partial_norm, "tensor", scatter_dimension=2, tiled=True)
        sent = partial_norm
    weight_parts.append(weight_part(2, sent))
    payload = pack(*ring_sum(1, ring(payload, 1), weight_parts[2][1]))
    weight_parts.append(weight_part(3, payload))
    if tensors == 2:
        x_terms, row_terms = after((x_terms, row_terms), weight_parts[3][1])
        row_dot = row_dot + row_terms[..., :1]
        grad_norm = cut_x(partial_norm) + x_terms.astype(jnp.float32) * row_terms[..., 1:]
    unit_rows = (cut_x(own_inputs).astype(jnp.float32) + cut_x(embedded)[:, None, :]) * inverse
    grad_hidden = cut_x(own_upstream).astype(jnp.float32) + inverse * (
        grad_norm * cut_x(gain) - unit_rows * (row_dot / features)
    )
    grad_rows = grad_hidden.astype(jnp.bfloat16)
    gain_term = jnp.sum(grad_norm * unit_rows, (0, 1))
    action_term = jnp.dot(
        onehot.T, jnp.sum(grad_hidden, 1), precision=lax.Precision.HIGHEST
    )
    small = jnp.concatenate([action_term, gain_term[None, :]], 0)
    small = small + swap_core(small)
    bit = 1
    while bit < depth:
        small = small + swap_z(small, bit)
        bit *= 2
    grad_rows, small = lax.optimization_barrier((grad_rows, small))
    returned = [grad_rows[:local_frames]]
    for k in range(1, depth):
        returned.append(
            ring(grad_rows[k * local_frames : (k + 1) * local_frames], depth - k)
        )

    for k in range(2, depth - 1):
        payload = pack(*ring_sum(k, ring(payload, 1), returned[1:]))
        if k + 2 < depth:
            weight_parts.append(weight_part(k + 2, payload))
    grad_inputs = jnp.zeros(inputs.shape, jnp.bfloat16)
    for k in range(depth):
        piece = after(returned[k], payload)
        target, first = place((z + k) % depth)
        grad_inputs = lax.dynamic_update_slice(
            grad_inputs, join_x(piece)[None], (target, 0, first, 0)
        )
    arriving, grad_inputs, small = lax.optimization_barrier(
        (ring(payload, 1), grad_inputs, small)
    )
    small = join_x(small + swap_y(small))
    total = chip_sum(depth - 1, arriving)[0] + unpack(arriving)[0]
    mine = lax.dynamic_slice_in_dim(total, core * shard_rows, shard_rows, 0)
    other = swap_core(lax.dynamic_slice_in_dim(total, (1 - core) * shard_rows, shard_rows, 0))
    first = jnp.where(core == 0, mine, other).reshape(shard_rows, 4, head_width)
    second = jnp.where(core == 0, other, mine).reshape(shard_rows, 4, head_width)
    joined = jnp.concatenate([first, second], 2)
    return (grad_inputs, joined[:, :3], joined[:, 3], small[actions], small[:actions])


def solution(mesh):
    sizes = mesh.shape
    return jax.shard_map(
        functools.partial(on_device, sizes["frame"], sizes["space"], sizes["tensor"]),
        mesh=mesh,
        in_specs=(
            P(None, "frame", "space", None),
            P(None, "frame", "space", None),
            P(None, "frame"),
            P(),
            P(),
            P(),
            P(("frame", "space"), None, "tensor"),
            P(("frame", "space"), "tensor"),
        ),
        out_specs=(
            P(None, "frame", "space", None),
            P(("frame", "space"), None, "tensor"),
            P(("frame", "space"), "tensor"),
            P(),
            P(),
        ),
        check_vma=False,
    )
```

```python
import functools
import math

import jax
import jax.numpy as jnp
from jax import lax
from jax.experimental import pallas as pl
from jax.experimental.pallas import tpu as pltpu
from jax.sharding import PartitionSpec as P

HEAD = 128
NORM_EPSILON = 1e-06
UPSTREAM_TOP = 6.0
WIRE = jnp.float16
WIRE_TOP = 32768.0
MIB = 1024 * 1024


def after(value, *earlier):
    return lax.optimization_barrier((value, earlier))[0]


def dot_nt(a, b):
    return lax.dot_general(a, b, (((1,), (1,)), ((), ())), preferred_element_type=jnp.float32)


def dot_nn(a, b):
    return lax.dot_general(a, b, (((1,), (0,)), ((), ())), preferred_element_type=jnp.float32)


def dot_tn(a, b):
    return lax.dot_general(a, b, (((0,), (0,)), ((), ())), preferred_element_type=jnp.float32)


def attention_kernel(
    late_ref, early_ref, qkv_ref, grad_ref, mixed_ref, merged_ref, peak_ref
):
    frames, group, width = grad_ref.shape
    rows = frames * group
    scale = 1.0 / math.sqrt(HEAD)

    def load(ref, start):
        block = ref[:, :, start : start + HEAD]
        if group % 16:
            return block.astype(jnp.float32).reshape(rows, HEAD).astype(jnp.bfloat16)
        return block.reshape(rows, HEAD)

    def store(ref, start, value):
        if group % 16:
            ref[:, :, start : start + HEAD] = value.reshape(frames, group, HEAD).astype(
                jnp.bfloat16
            )
        else:
            ref[:, :, start : start + HEAD] = value.astype(jnp.bfloat16).reshape(
                frames, group, HEAD
            )

    def peak(value):
        return jnp.max(jnp.abs(value).reshape(rows // 8, 8, HEAD), axis=0)

    @pl.when(pl.program_id(0) == 0)
    def _():
        peak_ref[...] = jnp.zeros_like(peak_ref)

    row_id = lax.broadcasted_iota(jnp.int32, (rows, rows), 0)
    col_id = lax.broadcasted_iota(jnp.int32, (rows, rows), 1)
    allowed = (row_id % group == col_id % group) & (early_ref[...] <= late_ref[...])
    starts = range(0, width, HEAD)
    query = [load(qkv_ref, i) for i in starts]
    key = [load(qkv_ref, width + i) for i in starts]
    value = [load(qkv_ref, 2 * width + i) for i in starts]
    grad = [load(grad_ref, i) for i in starts]
    heads = range(len(query))
    scores = [jnp.where(allowed, dot_nt(query[h], key[h]) * scale, -1e30) for h in heads]
    grad_probs = [dot_nt(grad[h], value[h]) for h in heads]
    exponent = [jnp.exp(scores[h] - jnp.max(scores[h], -1, keepdims=True)) for h in heads]
    probabilities = [exponent[h] / jnp.sum(exponent[h], -1, keepdims=True) for h in heads]
    rounded = [probabilities[h].astype(jnp.bfloat16) for h in heads]
    mean_grad = [jnp.sum(grad_probs[h] * probabilities[h], -1, keepdims=True) for h in heads]
    mixed = [dot_nn(rounded[h], value[h]) for h in heads]
    grad_value = [dot_tn(rounded[h], grad[h]) for h in heads]
    grad_scores = [probabilities[h] * (grad_probs[h] - mean_grad[h]) for h in heads]
    high = [grad_scores[h].astype(jnp.bfloat16) for h in heads]
    low = [(grad_scores[h] - high[h].astype(jnp.float32)).astype(jnp.bfloat16) for h in heads]
    grad_query = [(dot_nn(high[h], key[h]) + dot_nn(low[h], key[h])) * scale for h in heads]
    grad_key = [(dot_tn(high[h], query[h]) + dot_tn(low[h], query[h])) * scale for h in heads]
    top_out, top_qkv = peak_ref[0], peak_ref[1]
    for h, start in enumerate(starts):
        store(mixed_ref, start, mixed[h])
        store(merged_ref, start, grad_query[h])
        store(merged_ref, width + start, grad_key[h])
        store(merged_ref, 2 * width + start, grad_value[h])
        top_out = jnp.maximum(top_out, peak(mixed[h]))
        for term in (grad_query[h], grad_key[h], grad_value[h]):
            top_qkv = jnp.maximum(top_qkv, peak(term))
    peak_ref[0] = top_out
    peak_ref[1] = top_qkv


def temporal_attention(qkv, grad_heads, times):
    frames, pairs, width = grad_heads.shape
    group = 16 if pairs % 16 == 0 else 8
    rows = frames * group
    per_row = jnp.repeat(times.astype(jnp.float32), group)
    work = pairs // group * rows * rows * (width // HEAD)
    fixed = lambda i: (0, 0)
    moving = lambda i: (0, i, 0)
    return pl.pallas_call(
        attention_kernel,
        grid=(pairs // group,),
        in_specs=[
            pl.BlockSpec((rows, 1), fixed),
            pl.BlockSpec((1, rows), fixed),
            pl.BlockSpec((frames, group, 3 * width), moving),
            pl.BlockSpec((frames, group, width), moving),
        ],
        out_specs=[
            pl.BlockSpec((frames, group, width), moving),
            pl.BlockSpec((frames, group, 3 * width), moving),
            pl.BlockSpec((2, 8, HEAD), lambda i: (0, 0, 0)),
        ],
        out_shape=[
            jax.ShapeDtypeStruct((frames, pairs, width), jnp.bfloat16),
            jax.ShapeDtypeStruct((frames, pairs, 3 * width), jnp.bfloat16),
            jax.ShapeDtypeStruct((2, 8, HEAD), jnp.float32),
        ],
        compiler_params=pltpu.CompilerParams(vmem_limit_bytes=16 * MIB),
        cost_estimate=pl.CostEstimate(
            flops=16 * work * HEAD,
            bytes_accessed=16 * frames * pairs * width,
            transcendentals=work,
        ),
        name="temporal_attention",
    )(per_row[:, None], per_row[None, :], qkv, grad_heads)


def turn_kernel(rows_ref, out_ref):
    out_ref[...] = rows_ref[...].T


def turn(rows):
    tokens, features = rows.shape
    tile = features // 8
    return pl.pallas_call(
        turn_kernel,
        grid=(8,),
        in_specs=[pl.BlockSpec((tokens, tile), lambda i: (0, i))],
        out_specs=pl.BlockSpec((tile, tokens), lambda i: (i, 0)),
        out_shape=jax.ShapeDtypeStruct((features, tokens), rows.dtype),
        compiler_params=pltpu.CompilerParams(vmem_limit_bytes=12 * MIB),
        cost_estimate=pl.CostEstimate(flops=1, bytes_accessed=1, transcendentals=0),
        name="turn",
    )(rows)


def weight_kernel(
    place_ref, norm_near, norm_far, up_near, up_far, merged_ref, mixed_ref, near_ref, far_ref
):
    step = pl.program_id(0)

    @pl.when(step < 3)
    def _():
        near_ref[...] = dot_nn(norm_near[...], merged_ref[...])
        far_ref[...] = dot_nn(norm_far[...], merged_ref[...])

    @pl.when(step == 3)
    def _():
        near_ref[...] = dot_nn(up_near[...], mixed_ref[...])
        far_ref[...] = dot_nn(up_far[...], mixed_ref[...])


def weight_product(places, rows, normed, upstream, merged, mixed):
    tokens, width = mixed.shape
    near = pl.BlockSpec((rows, tokens), lambda i, at: (at[0], 0))
    far = pl.BlockSpec((rows, tokens), lambda i, at: (at[1], 0))
    out = pl.BlockSpec((rows, width), lambda i, at: (0, i))
    return pl.pallas_call(
        weight_kernel,
        grid_spec=pltpu.PrefetchScalarGridSpec(
            num_scalar_prefetch=1,
            grid=(4,),
            in_specs=[
                near,
                far,
                near,
                far,
                pl.BlockSpec((tokens, width), lambda i, at: (0, jnp.minimum(i, 2))),
                pl.BlockSpec((tokens, width), lambda i, at: (0, 0)),
            ],
            out_specs=[out, out],
        ),
        out_shape=[jax.ShapeDtypeStruct((rows, 4 * width), jnp.float32)] * 2,
        compiler_params=pltpu.CompilerParams(vmem_limit_bytes=58 * MIB),
        cost_estimate=pl.CostEstimate(flops=1, bytes_accessed=1, transcendentals=0),
        name="weight_product",
    )(places, normed, normed, upstream, upstream, merged, mixed)


def project_kernel(normed_ref, up_ref, weight_ref, qkv_ref, grad_ref):
    @pl.when(pl.program_id(0) < 3)
    def _():
        qkv_ref[...] = dot_nn(normed_ref[...], weight_ref[...]).astype(jnp.bfloat16)

    @pl.when(pl.program_id(0) == 3)
    def _():
        grad_ref[...] = dot_nn(up_ref[...], weight_ref[...]).astype(jnp.bfloat16)


def project(normed, upstream, weights):
    tokens, features = normed.shape
    width = weights.shape[1] // 4
    rows = tokens // 2
    return pl.pallas_call(
        project_kernel,
        grid=(4, 2),
        in_specs=[
            pl.BlockSpec((rows, features), lambda i, j: (jnp.where(i < 3, j, 1), 0)),
            pl.BlockSpec((rows, features), lambda i, j: (jnp.where(i < 3, 0, j), 0)),
            pl.BlockSpec((features, width), lambda i, j: (0, i)),
        ],
        out_specs=[
            pl.BlockSpec(
                (rows, width), lambda i, j: (jnp.where(i < 3, j, 1), jnp.minimum(i, 2))
            ),
            pl.BlockSpec((rows, width), lambda i, j: (jnp.where(i < 3, 0, j), 0)),
        ],
        out_shape=[
            jax.ShapeDtypeStruct((tokens, 3 * width), jnp.bfloat16),
            jax.ShapeDtypeStruct((tokens, width), jnp.bfloat16),
        ],
        compiler_params=pltpu.CompilerParams(vmem_limit_bytes=26 * MIB),
        cost_estimate=pl.CostEstimate(
            flops=2 * tokens * features * 4 * width,
            bytes_accessed=8 * tokens * features,
            transcendentals=0,
        ),
        name="project",
    )(normed, upstream, weights)


def norm_kernel(merged_ref, weight_ref, out_ref):
    out_ref[...] = dot_nt(merged_ref[...], weight_ref[...])


def norm_product(merged, weights):
    rows, depth = merged.shape
    features = weights.shape[0]
    tile = features // 4
    return pl.pallas_call(
        norm_kernel,
        grid=(4,),
        in_specs=[
            pl.BlockSpec((rows, depth), lambda i: (0, 0)),
            pl.BlockSpec((tile, depth), lambda i: (i, 0)),
        ],
        out_specs=pl.BlockSpec((rows, tile), lambda i: (0, i)),
        out_shape=jax.ShapeDtypeStruct((rows, features), jnp.float32),
        compiler_params=pltpu.CompilerParams(vmem_limit_bytes=18 * MIB),
        cost_estimate=pl.CostEstimate(flops=1, bytes_accessed=1, transcendentals=0),
        name="norm_product",
    )(merged, weights)


def on_device(
    depth, spaces, tensors, inputs, upstream, action_ids, frame_time, action_table, gain, w_qkv, w_out
):
    batch, local_frames, local_space, features = inputs.shape
    actions = action_table.shape[0]
    shard_rows, _, channels = w_qkv.shape
    z = lax.axis_index("frame")
    s = lax.axis_index("space")
    x = lax.axis_index("tensor")
    y, core = s // 2, s % 2
    frames = depth * local_frames
    pairs = batch * local_space // depth
    slots = depth // batch
    slice_width = features // tensors
    head_width = channels // 2
    width = 4 * head_width
    tokens = frames * 2 * pairs

    def ring(value, shift):
        return lax.ppermute(value, "frame", [(i, (i + shift) % depth) for i in range(depth)])

    def swap_z(value, bit):
        return lax.ppermute(value, "frame", [(i, i ^ bit) for i in range(depth)])

    def swap_core(value):
        return lax.ppermute(value, "space", [(i, i ^ 1) for i in range(spaces)])

    def swap_y(value):
        return lax.ppermute(value, "space", [(i, i ^ 2) for i in range(spaces)])

    def swap_x(value):
        return lax.ppermute(value, "tensor", [(0, 1), (1, 0)])

    def join_x(own, other=None):
        if tensors == 2:
            other = swap_x(own) if other is None else other
            first = jnp.where(x == 0, own, other)
            second = jnp.where(x == 0, other, own)
            return jnp.concatenate([first, second], -1)
        return lax.all_gather(own, "tensor", axis=own.ndim - 1, tiled=True)

    def cut_x(value, which=None):
        which = x if which is None else which
        return lax.dynamic_slice_in_dim(value, which * slice_width, slice_width, value.ndim - 1)

    def place(j):
        return j // slots, (j % slots) * pairs

    shards = [w_qkv[:, 0], w_qkv[:, 1], w_qkv[:, 2], w_out]

    def core_half(which):
        return jnp.concatenate(
            [jnp.where(which == 0, t[:, :head_width], t[:, head_width:]) for t in shards], 1
        )

    mine, sent = core_half(core), core_half(1 - core)
    other = swap_core(sent)
    block = jnp.concatenate(
        [jnp.where(core == 0, mine, other), jnp.where(core == 0, other, mine)], 0
    )

    def pieces(rows, k, start, size):
        rollout, first = place((z + k) % depth)
        return lax.dynamic_slice(
            rows, (rollout, 0, first, start), (1, local_frames, pairs, size)
        )[0]

    def collect(k, start):
        piece = jnp.stack([pieces(rows, k, start, slice_width) for rows in (inputs, upstream)])
        target, _ = place((z + k) % depth)
        ids = lax.dynamic_index_in_dim(action_ids, target, 0, keepdims=False)
        ids = jnp.broadcast_to(ids.astype(piece.dtype)[:, None], (local_frames, slice_width))
        ids = jnp.pad(ids, ((0, -local_frames % 8), (0, 0)))
        return ring(jnp.concatenate([piece.reshape(-1, slice_width), ids], 0), k)

    piece_shape = (2, local_frames, pairs, slice_width)
    piece_rows = 2 * local_frames * pairs

    def join_piece(own, other):
        ids = own[piece_rows : piece_rows + local_frames, 0].astype(jnp.int32)
        if other is not None:
            other = other[:piece_rows].reshape(piece_shape)
        return join_x(own[:piece_rows].reshape(piece_shape), other), ids

    def settle(weights, k, arrived, row):
        start = (z - k) % depth * (2 * block_rows) + row * block_rows
        return lax.dynamic_update_slice(weights, arrived, (start, 0))

    block_rows = 2 * shard_rows
    arrived = collect(1, x * slice_width)
    blocks, across, joined = [], [], []
    rollout, _ = place(z)
    all_ids = [lax.dynamic_index_in_dim(action_ids, rollout, 0, keepdims=False)]
    weights = after(jnp.zeros((features, width), jnp.bfloat16), arrived)
    for k in range(1, depth):
        blocks.append(block)
        across.append(swap_y(block))
        crossed = swap_x(arrived) if tensors == 2 else None
        piece, ids = join_piece(arrived, crossed)
        joined.append(piece)
        all_ids.append(ids)
        following = ring(block, 1)
        weights = settle(weights, k - 1, block, y)
        if k > 1:
            weights = settle(weights, k - 2, across[k - 2], 1 - y)
        earlier = [across[-1], joined[-1] if crossed is None else crossed]
        if k + 1 < depth:
            arrived = collect(k + 1, after(x * slice_width, block))
            following, arrived, weights, earlier = lax.optimization_barrier(
                (following, arrived, weights, earlier)
            )
        block = following
    locals_ = [pieces(rows, 0, 0, features) for rows in (inputs, upstream)]
    own_inputs = jnp.concatenate([locals_[0]] + [both_rows[0] for both_rows in joined], 0)
    own_upstream = jnp.concatenate([locals_[1]] + [both_rows[1] for both_rows in joined], 0)
    ids = jnp.concatenate(all_ids)
    order = (
        (z - jnp.arange(depth, dtype=jnp.int32)[:, None]) % depth * local_frames
        + jnp.arange(local_frames, dtype=jnp.int32)[None, :]
    ).reshape(frames)
    own_time = lax.dynamic_index_in_dim(frame_time, rollout, 0, keepdims=False)
    times = jnp.sum(
        jnp.where(
            order[:, None] == jnp.arange(frames, dtype=jnp.int32)[None, :], own_time[None, :], 0
        ),
        1,
    )
    onehot = (ids[:, None] == jnp.arange(actions, dtype=jnp.int32)[None, :]).astype(jnp.float32)
    embedded = jnp.dot(onehot, action_table, precision=lax.Precision.HIGHEST)
    hidden = own_inputs.astype(jnp.float32) + embedded[:, None, :]
    inverse = lax.rsqrt(jnp.mean(hidden * hidden, -1, keepdims=True) + NORM_EPSILON)
    normed = (hidden * inverse * gain).astype(jnp.bfloat16)

    block, normed, own_upstream, weights, near = lax.optimization_barrier(
        (block, normed, own_upstream, weights, across[-1])
    )
    far = swap_y(block)

    def both(own):
        return jnp.concatenate([own, swap_core(own)], 1).reshape(tokens, features)

    all_upstream = both(own_upstream)
    all_normed = both(normed)
    normed_t, upstream_t = turn(all_normed), turn(all_upstream)
    weights = settle(weights, depth - 2, near, 1 - y)
    weights = settle(weights, depth - 1, block, y)
    weights = settle(weights, depth - 1, after(far, normed_t, upstream_t), 1 - y)
    qkv, grad_heads = project(all_normed, all_upstream, weights)
    mixed, merged, peaks = temporal_attention(
        qkv.reshape(frames, 2 * pairs, 3 * head_width),
        grad_heads.reshape(frames, 2 * pairs, head_width),
        times,
    )
    flat_mixed = mixed.reshape(tokens, head_width)
    flat_merged = merged.reshape(tokens, 3 * head_width)

    peaks = jnp.max(peaks, (1, 2))
    own_bound = tokens * jnp.where(
        lax.broadcasted_iota(jnp.int32, (1, width), 1) < 3 * head_width,
        math.sqrt(features) * jnp.max(jnp.abs(gain)) * peaks[1],
        UPSTREAM_TOP * peaks[0],
    )
    own_bound = jnp.maximum(own_bound, 1e-20)

    def pack(value, bound):
        exponent = jnp.ceil(jnp.log2(bound / WIRE_TOP))
        return jnp.concatenate(
            [value * jnp.exp2(-exponent), jnp.broadcast_to(exponent, (8, width))], 0
        ).astype(WIRE)

    def unpack(sent):
        scale = jnp.exp2(sent[block_rows : block_rows + 1].astype(jnp.float32))
        return sent[:block_rows].astype(jnp.float32) * scale, scale * WIRE_TOP

    def weight_part(k, earlier):
        block_at = after((z - 1 - k) % depth * 2, earlier)
        places = jnp.stack([block_at + y, block_at + 1 - y])
        near, far = weight_product(
            places, block_rows, normed_t, upstream_t, flat_merged, flat_mixed
        )
        return near, pack(far, own_bound)

    def norm_part(rows):
        flat = rows.reshape(frames * pairs, 3 * head_width)
        return norm_product(flat, weights).reshape(frames, pairs, features)

    def chip_sum(k, earlier):
        term, bound = unpack(after(swap_y(weight_parts[k][1]), earlier))
        return weight_parts[k][0] + term, bound + own_bound

    def ring_sum(k, arriving, earlier):
        total, bound = chip_sum(k, earlier)
        term, ring_bound = unpack(arriving)
        return total + term, bound + ring_bound

    weight_parts = [weight_part(0, flat_merged)]
    norm_away = norm_part(after(merged[:, pairs:], weight_parts[0][1]))
    weight_parts.append(weight_part(1, norm_away))
    payload = pack(*chip_sum(0, weight_parts[1][1]))
    norm_here = norm_part(after(merged[:, :pairs], payload))
    partial_norm = norm_here + swap_core(after(norm_away, payload))
    row_dot = jnp.sum(partial_norm * gain * (hidden * inverse), -1, keepdims=True)
    if tensors == 2:
        x_away = cut_x(partial_norm, 1 - x)
        row_scale = jnp.max(jnp.abs(partial_norm), -1, keepdims=True)
        row_scale = jnp.maximum(row_scale, 1e-20) / WIRE_TOP
        sent = (x_away / row_scale).astype(WIRE)
        row_terms = swap_x(jnp.concatenate([row_dot, row_scale], -1))
        x_terms = swap_x(sent)
    else:
        row_dot = lax.psum(row_dot, "tensor")
        grad_norm = lax.psum_scatter(partial_norm, "tensor", scatter_dimension=2, tiled=True)
        sent = partial_norm
    weight_parts.append(weight_part(2, sent))
    payload = pack(*ring_sum(1, ring(payload, 1), weight_parts[2][1]))
    weight_parts.append(weight_part(3, payload))
    if tensors == 2:
        x_terms, row_terms = after((x_terms, row_terms), weight_parts[3][1])
        row_dot = row_dot + row_terms[..., :1]
        grad_norm = cut_x(partial_norm) + x_terms.astype(jnp.float32) * row_terms[..., 1:]
    unit_rows = (cut_x(own_inputs).astype(jnp.float32) + cut_x(embedded)[:, None, :]) * inverse
    grad_hidden = cut_x(own_upstream).astype(jnp.float32) + inverse * (
        grad_norm * cut_x(gain) - unit_rows * (row_dot / features)
    )
    grad_rows = grad_hidden.astype(jnp.bfloat16)
    gain_term = jnp.sum(grad_norm * unit_rows, (0, 1))
    action_term = jnp.dot(
        onehot.T, jnp.sum(grad_hidden, 1), precision=lax.Precision.HIGHEST
    )
    small = jnp.concatenate([action_term, gain_term[None, :]], 0)
    small = small + swap_core(small)
    small = small + swap_z(small, 1)
    returned = [grad_rows[:local_frames]]
    for k in range(1, depth):
        returned.append(
            ring(grad_rows[k * local_frames : (k + 1) * local_frames], depth - k)
        )

    for k in range(2, depth - 1):
        payload = pack(*ring_sum(k, ring(payload, 1), (returned[1:], small)))
        if k + 2 < depth:
            weight_parts.append(weight_part(k + 2, payload))
    grad_inputs = jnp.zeros(inputs.shape, jnp.bfloat16)
    for k in range(depth):
        piece = after(returned[k], payload)
        target, first = place((z + k) % depth)
        grad_inputs = lax.dynamic_update_slice(
            grad_inputs, join_x(piece)[None], (target, 0, first, 0)
        )
    small = after(small, payload)
    bit = 2
    while bit < depth:
        small = small + swap_z(small, bit)
        bit *= 2
    arriving, grad_inputs, small = lax.optimization_barrier(
        (ring(payload, 1), grad_inputs, small)
    )
    small = join_x(small + swap_y(small))
    total = chip_sum(depth - 1, arriving)[0] + unpack(arriving)[0]
    mine = lax.dynamic_slice_in_dim(total, core * shard_rows, shard_rows, 0)
    other = swap_core(lax.dynamic_slice_in_dim(total, (1 - core) * shard_rows, shard_rows, 0))
    first = jnp.where(core == 0, mine, other).reshape(shard_rows, 4, head_width)
    second = jnp.where(core == 0, other, mine).reshape(shard_rows, 4, head_width)
    joined = jnp.concatenate([first, second], 2)
    return (grad_inputs, joined[:, :3], joined[:, 3], small[actions], small[:actions])


def solution(mesh):
    sizes = mesh.shape
    return jax.shard_map(
        functools.partial(on_device, sizes["frame"], sizes["space"], sizes["tensor"]),
        mesh=mesh,
        in_specs=(
            P(None, "frame", "space", None),
            P(None, "frame", "space", None),
            P(None, "frame"),
            P(),
            P(),
            P(),
            P(("frame", "space"), None, "tensor"),
            P(("frame", "space"), "tensor"),
        ),
        out_specs=(
            P(None, "frame", "space", None),
            P(("frame", "space"), None, "tensor"),
            P(("frame", "space"), "tensor"),
            P(),
            P(),
        ),
        check_vma=False,
    )
```

```python
import functools
import math

import jax
import jax.numpy as jnp
from jax import lax
from jax.experimental import pallas as pl
from jax.experimental.pallas import tpu as pltpu
from jax.sharding import PartitionSpec as P

HEAD = 128
NORM_EPSILON = 1e-06
UPSTREAM_TOP = 6.0
WIRE = jnp.float16
WIRE_TOP = 32768.0
MIB = 1024 * 1024


def after(value, *earlier):
    return lax.optimization_barrier((value, earlier))[0]


def dot_nt(a, b):
    return lax.dot_general(a, b, (((1,), (1,)), ((), ())), preferred_element_type=jnp.float32)


def dot_nn(a, b):
    return lax.dot_general(a, b, (((1,), (0,)), ((), ())), preferred_element_type=jnp.float32)


def dot_tn(a, b):
    return lax.dot_general(a, b, (((0,), (0,)), ((), ())), preferred_element_type=jnp.float32)


def attention_kernel(
    late_ref, early_ref, qkv_ref, grad_ref, mixed_ref, merged_ref, peak_ref
):
    frames, group, width = grad_ref.shape
    rows = frames * group
    scale = 1.0 / math.sqrt(HEAD)

    def load(ref, start):
        block = ref[:, :, start : start + HEAD]
        if group % 16:
            return block.astype(jnp.float32).reshape(rows, HEAD).astype(jnp.bfloat16)
        return block.reshape(rows, HEAD)

    def store(ref, start, value):
        if group % 16:
            ref[:, :, start : start + HEAD] = value.reshape(frames, group, HEAD).astype(
                jnp.bfloat16
            )
        else:
            ref[:, :, start : start + HEAD] = value.astype(jnp.bfloat16).reshape(
                frames, group, HEAD
            )

    def peak(value):
        return jnp.max(jnp.abs(value).reshape(rows // 8, 8, HEAD), axis=0)

    @pl.when(pl.program_id(0) == 0)
    def _():
        peak_ref[...] = jnp.zeros_like(peak_ref)

    row_id = lax.broadcasted_iota(jnp.int32, (rows, rows), 0)
    col_id = lax.broadcasted_iota(jnp.int32, (rows, rows), 1)
    allowed = (row_id % group == col_id % group) & (early_ref[...] <= late_ref[...])
    starts = range(0, width, HEAD)
    query = [load(qkv_ref, i) for i in starts]
    key = [load(qkv_ref, width + i) for i in starts]
    value = [load(qkv_ref, 2 * width + i) for i in starts]
    grad = [load(grad_ref, i) for i in starts]
    heads = range(len(query))
    scores = [jnp.where(allowed, dot_nt(query[h], key[h]) * scale, -1e30) for h in heads]
    grad_probs = [dot_nt(grad[h], value[h]) for h in heads]
    exponent = [jnp.exp(scores[h] - jnp.max(scores[h], -1, keepdims=True)) for h in heads]
    probabilities = [exponent[h] / jnp.sum(exponent[h], -1, keepdims=True) for h in heads]
    rounded = [probabilities[h].astype(jnp.bfloat16) for h in heads]
    mean_grad = [jnp.sum(grad_probs[h] * probabilities[h], -1, keepdims=True) for h in heads]
    mixed = [dot_nn(rounded[h], value[h]) for h in heads]
    grad_value = [dot_tn(rounded[h], grad[h]) for h in heads]
    grad_scores = [probabilities[h] * (grad_probs[h] - mean_grad[h]) for h in heads]
    high = [grad_scores[h].astype(jnp.bfloat16) for h in heads]
    low = [(grad_scores[h] - high[h].astype(jnp.float32)).astype(jnp.bfloat16) for h in heads]
    grad_query = [(dot_nn(high[h], key[h]) + dot_nn(low[h], key[h])) * scale for h in heads]
    grad_key = [(dot_tn(high[h], query[h]) + dot_tn(low[h], query[h])) * scale for h in heads]
    top_out, top_qkv = peak_ref[0], peak_ref[1]
    for h, start in enumerate(starts):
        store(mixed_ref, start, mixed[h])
        store(merged_ref, start, grad_query[h])
        store(merged_ref, width + start, grad_key[h])
        store(merged_ref, 2 * width + start, grad_value[h])
        top_out = jnp.maximum(top_out, peak(mixed[h]))
        for term in (grad_query[h], grad_key[h], grad_value[h]):
            top_qkv = jnp.maximum(top_qkv, peak(term))
    peak_ref[0] = top_out
    peak_ref[1] = top_qkv


def temporal_attention(qkv, grad_heads, times):
    frames, pairs, width = grad_heads.shape
    group = 16 if pairs % 16 == 0 else 8
    rows = frames * group
    per_row = jnp.repeat(times.astype(jnp.float32), group)
    work = pairs // group * rows * rows * (width // HEAD)
    fixed = lambda i: (0, 0)
    moving = lambda i: (0, i, 0)
    return pl.pallas_call(
        attention_kernel,
        grid=(pairs // group,),
        in_specs=[
            pl.BlockSpec((rows, 1), fixed),
            pl.BlockSpec((1, rows), fixed),
            pl.BlockSpec((frames, group, 3 * width), moving),
            pl.BlockSpec((frames, group, width), moving),
        ],
        out_specs=[
            pl.BlockSpec((frames, group, width), moving),
            pl.BlockSpec((frames, group, 3 * width), moving),
            pl.BlockSpec((2, 8, HEAD), lambda i: (0, 0, 0)),
        ],
        out_shape=[
            jax.ShapeDtypeStruct((frames, pairs, width), jnp.bfloat16),
            jax.ShapeDtypeStruct((frames, pairs, 3 * width), jnp.bfloat16),
            jax.ShapeDtypeStruct((2, 8, HEAD), jnp.float32),
        ],
        compiler_params=pltpu.CompilerParams(vmem_limit_bytes=16 * MIB),
        cost_estimate=pl.CostEstimate(
            flops=16 * work * HEAD,
            bytes_accessed=16 * frames * pairs * width,
            transcendentals=work,
        ),
        name="temporal_attention",
    )(per_row[:, None], per_row[None, :], qkv, grad_heads)


def turn_kernel(rows_ref, out_ref):
    out_ref[...] = rows_ref[...].T


def turn(rows):
    tokens, features = rows.shape
    tile = features // 8
    return pl.pallas_call(
        turn_kernel,
        grid=(8,),
        in_specs=[pl.BlockSpec((tokens, tile), lambda i: (0, i))],
        out_specs=pl.BlockSpec((tile, tokens), lambda i: (i, 0)),
        out_shape=jax.ShapeDtypeStruct((features, tokens), rows.dtype),
        compiler_params=pltpu.CompilerParams(vmem_limit_bytes=12 * MIB),
        cost_estimate=pl.CostEstimate(flops=1, bytes_accessed=1, transcendentals=0),
        name="turn",
    )(rows)


def weight_kernel(
    place_ref, norm_near, norm_far, up_near, up_far, merged_ref, mixed_ref, near_ref, far_ref
):
    step = pl.program_id(1)

    @pl.when(step < 3)
    def _():
        near_ref[0] = dot_nn(norm_near[...], merged_ref[...])
        far_ref[0] = dot_nn(norm_far[...], merged_ref[...])

    @pl.when(step == 3)
    def _():
        near_ref[0] = dot_nn(up_near[...], mixed_ref[...])
        far_ref[0] = dot_nn(up_far[...], mixed_ref[...])


def weight_product(places, rows, normed, upstream, merged, mixed):
    tokens, width = mixed.shape
    count = places.shape[0] // 2
    near = pl.BlockSpec((rows, tokens), lambda b, i, at: (at[2 * b], 0))
    far = pl.BlockSpec((rows, tokens), lambda b, i, at: (at[2 * b + 1], 0))
    out = pl.BlockSpec((1, rows, width), lambda b, i, at: (b, 0, i))
    return pl.pallas_call(
        weight_kernel,
        grid_spec=pltpu.PrefetchScalarGridSpec(
            num_scalar_prefetch=1,
            grid=(count, 4),
            in_specs=[
                near,
                far,
                near,
                far,
                pl.BlockSpec((tokens, width), lambda b, i, at: (0, jnp.minimum(i, 2))),
                pl.BlockSpec((tokens, width), lambda b, i, at: (0, 0)),
            ],
            out_specs=[out, out],
        ),
        out_shape=[jax.ShapeDtypeStruct((count, rows, 4 * width), jnp.float32)] * 2,
        compiler_params=pltpu.CompilerParams(vmem_limit_bytes=58 * MIB),
        cost_estimate=pl.CostEstimate(flops=1, bytes_accessed=1, transcendentals=0),
        name="weight_product",
    )(places, normed, normed, upstream, upstream, merged, mixed)


def project_kernel(normed_ref, up_ref, weight_ref, qkv_ref, grad_ref):
    @pl.when(pl.program_id(0) < 3)
    def _():
        qkv_ref[...] = dot_nn(normed_ref[...], weight_ref[...]).astype(jnp.bfloat16)

    @pl.when(pl.program_id(0) == 3)
    def _():
        grad_ref[...] = dot_nn(up_ref[...], weight_ref[...]).astype(jnp.bfloat16)


def project(normed, upstream, weights):
    tokens, features = normed.shape
    width = weights.shape[1] // 4
    rows = tokens // 2
    return pl.pallas_call(
        project_kernel,
        grid=(4, 2),
        in_specs=[
            pl.BlockSpec((rows, features), lambda i, j: (jnp.where(i < 3, j, 1), 0)),
            pl.BlockSpec((rows, features), lambda i, j: (jnp.where(i < 3, 0, j), 0)),
            pl.BlockSpec((features, width), lambda i, j: (0, i)),
        ],
        out_specs=[
            pl.BlockSpec(
                (rows, width), lambda i, j: (jnp.where(i < 3, j, 1), jnp.minimum(i, 2))
            ),
            pl.BlockSpec((rows, width), lambda i, j: (jnp.where(i < 3, 0, j), 0)),
        ],
        out_shape=[
            jax.ShapeDtypeStruct((tokens, 3 * width), jnp.bfloat16),
            jax.ShapeDtypeStruct((tokens, width), jnp.bfloat16),
        ],
        compiler_params=pltpu.CompilerParams(vmem_limit_bytes=26 * MIB),
        cost_estimate=pl.CostEstimate(
            flops=2 * tokens * features * 4 * width,
            bytes_accessed=8 * tokens * features,
            transcendentals=0,
        ),
        name="project",
    )(normed, upstream, weights)


def norm_kernel(merged_ref, weight_ref, own_ref, other_ref):
    frames, pairs, tile = own_ref.shape
    rows = dot_nt(merged_ref[...], weight_ref[...]).reshape(frames, 2 * pairs, tile)
    own_ref[...] = rows[:, :pairs]
    other_ref[...] = rows[:, pairs:]


def norm_product(merged, weights, frames):
    rows, depth = merged.shape
    features = weights.shape[0]
    tile = features // 4
    pairs = rows // frames // 2
    out = pl.BlockSpec((frames, pairs, tile), lambda i: (0, 0, i))
    return pl.pallas_call(
        norm_kernel,
        grid=(4,),
        in_specs=[
            pl.BlockSpec((rows, depth), lambda i: (0, 0)),
            pl.BlockSpec((tile, depth), lambda i: (i, 0)),
        ],
        out_specs=[out, out],
        out_shape=[jax.ShapeDtypeStruct((frames, pairs, features), jnp.float32)] * 2,
        compiler_params=pltpu.CompilerParams(vmem_limit_bytes=26 * MIB),
        cost_estimate=pl.CostEstimate(flops=1, bytes_accessed=1, transcendentals=0),
        name="norm_product",
    )(merged, weights)


def on_device(
    depth, spaces, tensors, inputs, upstream, action_ids, frame_time, action_table, gain, w_qkv, w_out
):
    batch, local_frames, local_space, features = inputs.shape
    actions = action_table.shape[0]
    shard_rows, _, channels = w_qkv.shape
    z = lax.axis_index("frame")
    s = lax.axis_index("space")
    x = lax.axis_index("tensor")
    y, core = s // 2, s % 2
    frames = depth * local_frames
    pairs = batch * local_space // depth
    slots = depth // batch
    slice_width = features // tensors
    head_width = channels // 2
    width = 4 * head_width
    tokens = frames * 2 * pairs

    def ring(value, shift):
        return lax.ppermute(value, "frame", [(i, (i + shift) % depth) for i in range(depth)])

    def swap_z(value, bit):
        return lax.ppermute(value, "frame", [(i, i ^ bit) for i in range(depth)])

    def swap_core(value):
        return lax.ppermute(value, "space", [(i, i ^ 1) for i in range(spaces)])

    def swap_y(value):
        return lax.ppermute(value, "space", [(i, i ^ 2) for i in range(spaces)])

    def swap_x(value):
        return lax.ppermute(value, "tensor", [(0, 1), (1, 0)])

    def join_x(own, other=None):
        if tensors == 2:
            other = swap_x(own) if other is None else other
            first = jnp.where(x == 0, own, other)
            second = jnp.where(x == 0, other, own)
            return jnp.concatenate([first, second], -1)
        return lax.all_gather(own, "tensor", axis=own.ndim - 1, tiled=True)

    def cut_x(value, which=None):
        which = x if which is None else which
        return lax.dynamic_slice_in_dim(value, which * slice_width, slice_width, value.ndim - 1)

    def place(j):
        return j // slots, (j % slots) * pairs

    shards = [w_qkv[:, 0], w_qkv[:, 1], w_qkv[:, 2], w_out]

    def core_half(which):
        return jnp.concatenate(
            [jnp.where(which == 0, t[:, :head_width], t[:, head_width:]) for t in shards], 1
        )

    mine, sent = core_half(core), core_half(1 - core)
    other = swap_core(sent)
    block = jnp.concatenate(
        [jnp.where(core == 0, mine, other), jnp.where(core == 0, other, mine)], 0
    )

    def pieces(rows, k, start, size):
        rollout, first = place((z + k) % depth)
        return lax.dynamic_slice(
            rows, (rollout, 0, first, start), (1, local_frames, pairs, size)
        )[0]

    def collect(k, start):
        piece = jnp.stack([pieces(rows, k, start, slice_width) for rows in (inputs, upstream)])
        target, _ = place((z + k) % depth)
        ids = lax.dynamic_index_in_dim(action_ids, target, 0, keepdims=False)
        ids = jnp.broadcast_to(ids.astype(piece.dtype)[:, None], (local_frames, slice_width))
        ids = jnp.pad(ids, ((0, -local_frames % 8), (0, 0)))
        return ring(jnp.concatenate([piece.reshape(-1, slice_width), ids], 0), k)

    piece_shape = (2, local_frames, pairs, slice_width)
    piece_rows = 2 * local_frames * pairs

    def join_piece(own, other):
        ids = own[piece_rows : piece_rows + local_frames, 0].astype(jnp.int32)
        if other is not None:
            other = other[:piece_rows].reshape(piece_shape)
        return join_x(own[:piece_rows].reshape(piece_shape), other), ids

    def settle(weights, k, arrived, row):
        start = (z - k) % depth * (2 * block_rows) + row * block_rows
        return lax.dynamic_update_slice(weights, arrived, (start, 0))

    block_rows = 2 * shard_rows
    arrived = collect(1, x * slice_width)
    blocks, across, joined = [], [], []
    rollout, _ = place(z)
    all_ids = [lax.dynamic_index_in_dim(action_ids, rollout, 0, keepdims=False)]
    weights = after(jnp.zeros((features, width), jnp.bfloat16), arrived)
    for k in range(1, depth):
        blocks.append(block)
        across.append(swap_y(block))
        crossed = swap_x(arrived) if tensors == 2 else None
        piece, ids = join_piece(arrived, crossed)
        joined.append(piece)
        all_ids.append(ids)
        following = ring(block, 1)
        weights = settle(weights, k - 1, block, y)
        if k > 1:
            weights = settle(weights, k - 2, across[k - 2], 1 - y)
        earlier = [across[-1], joined[-1] if crossed is None else crossed]
        if k + 1 < depth:
            arrived = collect(k + 1, after(x * slice_width, block))
            following, arrived, weights, earlier = lax.optimization_barrier(
                (following, arrived, weights, earlier)
            )
        block = following
    locals_ = [pieces(rows, 0, 0, features) for rows in (inputs, upstream)]
    own_inputs = jnp.concatenate([locals_[0]] + [both_rows[0] for both_rows in joined], 0)
    own_upstream = jnp.concatenate([locals_[1]] + [both_rows[1] for both_rows in joined], 0)
    ids = jnp.concatenate(all_ids)
    order = (
        (z - jnp.arange(depth, dtype=jnp.int32)[:, None]) % depth * local_frames
        + jnp.arange(local_frames, dtype=jnp.int32)[None, :]
    ).reshape(frames)
    own_time = lax.dynamic_index_in_dim(frame_time, rollout, 0, keepdims=False)
    times = jnp.sum(
        jnp.where(
            order[:, None] == jnp.arange(frames, dtype=jnp.int32)[None, :], own_time[None, :], 0
        ),
        1,
    )
    onehot = (ids[:, None] == jnp.arange(actions, dtype=jnp.int32)[None, :]).astype(jnp.float32)
    embedded = jnp.dot(onehot, action_table, precision=lax.Precision.HIGHEST)
    hidden = own_inputs.astype(jnp.float32) + embedded[:, None, :]
    inverse = lax.rsqrt(jnp.mean(hidden * hidden, -1, keepdims=True) + NORM_EPSILON)
    normed = (hidden * inverse * gain).astype(jnp.bfloat16)

    block, normed, own_upstream, weights, near = lax.optimization_barrier(
        (block, normed, own_upstream, weights, across[-1])
    )
    far = swap_y(block)

    def both(own):
        return jnp.concatenate([own, swap_core(own)], 1).reshape(tokens, features)

    all_upstream = both(own_upstream)
    all_normed = both(normed)
    normed_t, upstream_t = turn(all_normed), turn(all_upstream)
    weights = settle(weights, depth - 2, near, 1 - y)
    weights = settle(weights, depth - 1, block, y)
    weights = settle(weights, depth - 1, after(far, normed_t, upstream_t), 1 - y)
    qkv, grad_heads = project(all_normed, all_upstream, weights)
    mixed, merged, peaks = temporal_attention(
        qkv.reshape(frames, 2 * pairs, 3 * head_width),
        grad_heads.reshape(frames, 2 * pairs, head_width),
        times,
    )
    flat_mixed = mixed.reshape(tokens, head_width)
    flat_merged = merged.reshape(tokens, 3 * head_width)

    peaks = jnp.max(peaks, (1, 2))
    own_bound = tokens * jnp.where(
        lax.broadcasted_iota(jnp.int32, (1, width), 1) < 3 * head_width,
        math.sqrt(features) * jnp.max(jnp.abs(gain)) * peaks[1],
        UPSTREAM_TOP * peaks[0],
    )
    own_bound = jnp.maximum(own_bound, 1e-20)

    def pack(value, bound):
        exponent = jnp.ceil(jnp.log2(bound / WIRE_TOP))
        return jnp.concatenate(
            [value * jnp.exp2(-exponent), jnp.broadcast_to(exponent, (8, width))], 0
        ).astype(WIRE)

    def unpack(sent):
        scale = jnp.exp2(sent[block_rows : block_rows + 1].astype(jnp.float32))
        return sent[:block_rows].astype(jnp.float32) * scale, scale * WIRE_TOP

    def weight_parts_of(steps, earlier):
        at = after(z, earlier)
        places = [(at - 1 - k) % depth * 2 + row for k in steps for row in (y, 1 - y)]
        near, far = weight_product(
            jnp.stack(places), block_rows, normed_t, upstream_t, flat_merged, flat_mixed
        )
        return [(near[i], far[i]) for i in range(len(steps))]

    def chip_sum(k, earlier):
        term, bound = unpack(after(swap_y(away[k]), earlier))
        return weight_parts[k][0] + term, bound + own_bound

    def ring_sum(k, arriving, earlier):
        total, bound = chip_sum(k, earlier)
        term, ring_bound = unpack(arriving)
        return total + term, bound + ring_bound

    weight_parts = weight_parts_of([0], flat_merged)
    away = [pack(weight_parts[0][1], own_bound)]
    norm_here, norm_away = norm_product(after(flat_merged, away[0]), weights, frames)
    weight_parts += weight_parts_of(range(1, depth), norm_away)
    away.append(pack(weight_parts[1][1], own_bound))
    payload = pack(*chip_sum(0, away[1]))
    partial_norm = norm_here + swap_core(after(norm_away, payload))
    row_dot = jnp.sum(partial_norm * gain * (hidden * inverse), -1, keepdims=True)
    if tensors == 2:
        x_away = cut_x(partial_norm, 1 - x)
        row_scale = jnp.max(jnp.abs(partial_norm), -1, keepdims=True)
        row_scale = jnp.maximum(row_scale, 1e-20) / WIRE_TOP
        sent = (x_away / row_scale).astype(WIRE)
        row_terms = swap_x(jnp.concatenate([row_dot, row_scale], -1))
        x_terms = swap_x(sent)
    else:
        row_dot = lax.psum(row_dot, "tensor")
        grad_norm = lax.psum_scatter(partial_norm, "tensor", scatter_dimension=2, tiled=True)
        sent = partial_norm
    away.append(pack(after(weight_parts[2][1], sent), own_bound))
    payload = pack(*ring_sum(1, ring(payload, 1), away[2]))
    away.append(pack(after(weight_parts[3][1], payload), own_bound))
    if tensors == 2:
        x_terms, row_terms = after((x_terms, row_terms), away[3])
        row_dot = row_dot + row_terms[..., :1]
        grad_norm = cut_x(partial_norm) + x_terms.astype(jnp.float32) * row_terms[..., 1:]
    unit_rows = (cut_x(own_inputs).astype(jnp.float32) + cut_x(embedded)[:, None, :]) * inverse
    grad_hidden = cut_x(own_upstream).astype(jnp.float32) + inverse * (
        grad_norm * cut_x(gain) - unit_rows * (row_dot / features)
    )
    grad_rows = grad_hidden.astype(jnp.bfloat16)
    gain_term = jnp.sum(grad_norm * unit_rows, (0, 1))
    action_term = jnp.dot(
        onehot.T, jnp.sum(grad_hidden, 1), precision=lax.Precision.HIGHEST
    )
    small = jnp.concatenate([action_term, gain_term[None, :]], 0)
    small = small + swap_core(small)
    small = small + swap_z(small, 1)
    small = join_x(small + swap_y(small))
    returned = [grad_rows[:local_frames]]
    for k in range(1, depth):
        returned.append(
            ring(grad_rows[k * local_frames : (k + 1) * local_frames], depth - k)
        )

    for k in range(2, depth - 1):
        payload = pack(*ring_sum(k, ring(payload, 1), (returned[1:], small)))
        if k + 2 < depth:
            away.append(pack(after(weight_parts[k + 2][1], payload), own_bound))
    grad_inputs = jnp.zeros(inputs.shape, jnp.bfloat16)
    for k in range(depth):
        piece = after(returned[k], payload)
        target, first = place((z + k) % depth)
        grad_inputs = lax.dynamic_update_slice(
            grad_inputs, join_x(piece)[None], (target, 0, first, 0)
        )
    small = after(small, payload)
    bit = 2
    while bit < depth:
        small = small + after(swap_z(small, bit), grad_inputs)
        bit *= 2
    arriving, grad_inputs, small = lax.optimization_barrier(
        (ring(payload, 1), grad_inputs, small)
    )
    total = chip_sum(depth - 1, arriving)[0] + unpack(arriving)[0]
    mine = lax.dynamic_slice_in_dim(total, core * shard_rows, shard_rows, 0)
    other = swap_core(lax.dynamic_slice_in_dim(total, (1 - core) * shard_rows, shard_rows, 0))
    first = jnp.where(core == 0, mine, other).reshape(shard_rows, 4, head_width)
    second = jnp.where(core == 0, other, mine).reshape(shard_rows, 4, head_width)
    joined = jnp.concatenate([first, second], 2)
    return (grad_inputs, joined[:, :3], joined[:, 3], small[actions], small[:actions])


def solution(mesh):
    sizes = mesh.shape
    return jax.shard_map(
        functools.partial(on_device, sizes["frame"], sizes["space"], sizes["tensor"]),
        mesh=mesh,
        in_specs=(
            P(None, "frame", "space", None),
            P(None, "frame", "space", None),
            P(None, "frame"),
            P(),
            P(),
            P(),
            P(("frame", "space"), None, "tensor"),
            P(("frame", "space"), "tensor"),
        ),
        out_specs=(
            P(None, "frame", "space", None),
            P(("frame", "space"), None, "tensor"),
            P(("frame", "space"), "tensor"),
            P(),
            P(),
        ),
        check_vma=False,
    )
```

```python
import functools
import math

import jax
import jax.numpy as jnp
from jax import lax
from jax.experimental import pallas as pl
from jax.experimental.pallas import tpu as pltpu
from jax.sharding import PartitionSpec as P

HEAD = 128
NORM_EPSILON = 1e-06
UPSTREAM_TOP = 6.0
WIRE = jnp.float16
WIRE_TOP = 32768.0
MIB = 1024 * 1024


def after(value, *earlier):
    return lax.optimization_barrier((value, earlier))[0]


def dot_nt(a, b):
    return lax.dot_general(a, b, (((1,), (1,)), ((), ())), preferred_element_type=jnp.float32)


def dot_nn(a, b):
    return lax.dot_general(a, b, (((1,), (0,)), ((), ())), preferred_element_type=jnp.float32)


def dot_tn(a, b):
    return lax.dot_general(a, b, (((0,), (0,)), ((), ())), preferred_element_type=jnp.float32)


def attention_kernel(
    late_ref, early_ref, qkv_ref, grad_ref, mixed_ref, merged_ref, peak_ref
):
    frames, group, width = grad_ref.shape
    rows = frames * group
    scale = 1.0 / math.sqrt(HEAD)

    def load(ref, start):
        block = ref[:, :, start : start + HEAD]
        if group % 16:
            return block.astype(jnp.float32).reshape(rows, HEAD).astype(jnp.bfloat16)
        return block.reshape(rows, HEAD)

    def store(ref, start, value):
        if group % 16:
            ref[:, :, start : start + HEAD] = value.reshape(frames, group, HEAD).astype(
                jnp.bfloat16
            )
        else:
            ref[:, :, start : start + HEAD] = value.astype(jnp.bfloat16).reshape(
                frames, group, HEAD
            )

    def peak(value):
        return jnp.max(jnp.abs(value).reshape(rows // 8, 8, HEAD), axis=0)

    @pl.when(pl.program_id(0) == 0)
    def _():
        peak_ref[...] = jnp.zeros_like(peak_ref)

    row_id = lax.broadcasted_iota(jnp.int32, (rows, rows), 0)
    col_id = lax.broadcasted_iota(jnp.int32, (rows, rows), 1)
    allowed = (row_id % group == col_id % group) & (early_ref[...] <= late_ref[...])
    starts = range(0, width, HEAD)
    query = [load(qkv_ref, i) for i in starts]
    key = [load(qkv_ref, width + i) for i in starts]
    value = [load(qkv_ref, 2 * width + i) for i in starts]
    grad = [load(grad_ref, i) for i in starts]
    heads = range(len(query))
    scores = [jnp.where(allowed, dot_nt(query[h], key[h]) * scale, -1e30) for h in heads]
    grad_probs = [dot_nt(grad[h], value[h]) for h in heads]
    exponent = [jnp.exp(scores[h] - jnp.max(scores[h], -1, keepdims=True)) for h in heads]
    probabilities = [exponent[h] / jnp.sum(exponent[h], -1, keepdims=True) for h in heads]
    rounded = [probabilities[h].astype(jnp.bfloat16) for h in heads]
    mean_grad = [jnp.sum(grad_probs[h] * probabilities[h], -1, keepdims=True) for h in heads]
    mixed = [dot_nn(rounded[h], value[h]) for h in heads]
    grad_value = [dot_tn(rounded[h], grad[h]) for h in heads]
    grad_scores = [probabilities[h] * (grad_probs[h] - mean_grad[h]) for h in heads]
    high = [grad_scores[h].astype(jnp.bfloat16) for h in heads]
    low = [(grad_scores[h] - high[h].astype(jnp.float32)).astype(jnp.bfloat16) for h in heads]
    grad_query = [(dot_nn(high[h], key[h]) + dot_nn(low[h], key[h])) * scale for h in heads]
    grad_key = [(dot_tn(high[h], query[h]) + dot_tn(low[h], query[h])) * scale for h in heads]
    top_out, top_qkv = peak_ref[0], peak_ref[1]
    for h, start in enumerate(starts):
        store(mixed_ref, start, mixed[h])
        store(merged_ref, start, grad_query[h])
        store(merged_ref, width + start, grad_key[h])
        store(merged_ref, 2 * width + start, grad_value[h])
        top_out = jnp.maximum(top_out, peak(mixed[h]))
        for term in (grad_query[h], grad_key[h], grad_value[h]):
            top_qkv = jnp.maximum(top_qkv, peak(term))
    peak_ref[0] = top_out
    peak_ref[1] = top_qkv


def temporal_attention(qkv, grad_heads, times):
    frames, pairs, width = grad_heads.shape
    group = 16 if pairs % 16 == 0 else 8
    rows = frames * group
    per_row = jnp.repeat(times.astype(jnp.float32), group)
    work = pairs // group * rows * rows * (width // HEAD)
    fixed = lambda i: (0, 0)
    moving = lambda i: (0, i, 0)
    return pl.pallas_call(
        attention_kernel,
        grid=(pairs // group,),
        in_specs=[
            pl.BlockSpec((rows, 1), fixed),
            pl.BlockSpec((1, rows), fixed),
            pl.BlockSpec((frames, group, 3 * width), moving),
            pl.BlockSpec((frames, group, width), moving),
        ],
        out_specs=[
            pl.BlockSpec((frames, group, width), moving),
            pl.BlockSpec((frames, group, 3 * width), moving),
            pl.BlockSpec((2, 8, HEAD), lambda i: (0, 0, 0)),
        ],
        out_shape=[
            jax.ShapeDtypeStruct((frames, pairs, width), jnp.bfloat16),
            jax.ShapeDtypeStruct((frames, pairs, 3 * width), jnp.bfloat16),
            jax.ShapeDtypeStruct((2, 8, HEAD), jnp.float32),
        ],
        compiler_params=pltpu.CompilerParams(vmem_limit_bytes=16 * MIB),
        cost_estimate=pl.CostEstimate(
            flops=16 * work * HEAD,
            bytes_accessed=16 * frames * pairs * width,
            transcendentals=work,
        ),
        name="temporal_attention",
    )(per_row[:, None], per_row[None, :], qkv, grad_heads)


def turn_kernel(rows_ref, out_ref):
    out_ref[...] = rows_ref[...].T


def turn(rows):
    tokens, features = rows.shape
    tile = features // 8
    return pl.pallas_call(
        turn_kernel,
        grid=(8,),
        in_specs=[pl.BlockSpec((tokens, tile), lambda i: (0, i))],
        out_specs=pl.BlockSpec((tile, tokens), lambda i: (i, 0)),
        out_shape=jax.ShapeDtypeStruct((features, tokens), rows.dtype),
        compiler_params=pltpu.CompilerParams(vmem_limit_bytes=12 * MIB),
        cost_estimate=pl.CostEstimate(flops=1, bytes_accessed=1, transcendentals=0),
        name="turn",
    )(rows)


def weight_kernel(normed_ref, up_ref, merged_ref, mixed_ref, out_ref):
    @pl.when(pl.program_id(1) < 3)
    def _():
        out_ref[...] = dot_nn(normed_ref[...], merged_ref[...])

    @pl.when(pl.program_id(1) == 3)
    def _():
        out_ref[...] = dot_nn(up_ref[...], mixed_ref[...])


def weight_product(normed, upstream, merged, mixed):
    tokens, width = mixed.shape
    rows = normed.shape[0] // 2
    return pl.pallas_call(
        weight_kernel,
        grid=(2, 4),
        in_specs=[
            pl.BlockSpec((rows, tokens), lambda i, j: (i, 0)),
            pl.BlockSpec((rows, tokens), lambda i, j: (i, 0)),
            pl.BlockSpec((tokens, width), lambda i, j: (0, jnp.minimum(j, 2))),
            pl.BlockSpec((tokens, width), lambda i, j: (0, 0)),
        ],
        out_specs=pl.BlockSpec((rows, width), lambda i, j: (i, j)),
        out_shape=jax.ShapeDtypeStruct((2 * rows, 4 * width), jnp.float32),
        compiler_params=pltpu.CompilerParams(vmem_limit_bytes=58 * MIB),
        cost_estimate=pl.CostEstimate(flops=1, bytes_accessed=1, transcendentals=0),
        name="weight_product",
    )(normed, upstream, merged, mixed)


def project_kernel(normed_ref, up_ref, weight_ref, qkv_ref, grad_ref):
    @pl.when(pl.program_id(0) < 3)
    def _():
        qkv_ref[...] = dot_nn(normed_ref[...], weight_ref[...]).astype(jnp.bfloat16)

    @pl.when(pl.program_id(0) == 3)
    def _():
        grad_ref[...] = dot_nn(up_ref[...], weight_ref[...]).astype(jnp.bfloat16)


def project(normed, upstream, weights):
    tokens, features = normed.shape
    width = weights.shape[1] // 4
    rows = tokens // 2
    return pl.pallas_call(
        project_kernel,
        grid=(4, 2),
        in_specs=[
            pl.BlockSpec((rows, features), lambda i, j: (jnp.where(i < 3, j, 1), 0)),
            pl.BlockSpec((rows, features), lambda i, j: (jnp.where(i < 3, 0, j), 0)),
            pl.BlockSpec((features, width), lambda i, j: (0, i)),
        ],
        out_specs=[
            pl.BlockSpec(
                (rows, width), lambda i, j: (jnp.where(i < 3, j, 1), jnp.minimum(i, 2))
            ),
            pl.BlockSpec((rows, width), lambda i, j: (jnp.where(i < 3, 0, j), 0)),
        ],
        out_shape=[
            jax.ShapeDtypeStruct((tokens, 3 * width), jnp.bfloat16),
            jax.ShapeDtypeStruct((tokens, width), jnp.bfloat16),
        ],
        compiler_params=pltpu.CompilerParams(vmem_limit_bytes=26 * MIB),
        cost_estimate=pl.CostEstimate(
            flops=2 * tokens * features * 4 * width,
            bytes_accessed=8 * tokens * features,
            transcendentals=0,
        ),
        name="project",
    )(normed, upstream, weights)


def norm_kernel(merged_ref, weight_ref, own_ref, other_ref):
    frames, pairs, tile = own_ref.shape
    rows = dot_nt(merged_ref[...], weight_ref[...]).reshape(frames, 2 * pairs, tile)
    own_ref[...] = rows[:, :pairs]
    other_ref[...] = rows[:, pairs:]


def norm_product(merged, weights, frames):
    rows, depth = merged.shape
    features = weights.shape[0]
    tile = features // 4
    pairs = rows // frames // 2
    out = pl.BlockSpec((frames, pairs, tile), lambda i: (0, 0, i))
    return pl.pallas_call(
        norm_kernel,
        grid=(4,),
        in_specs=[
            pl.BlockSpec((rows, depth), lambda i: (0, 0)),
            pl.BlockSpec((tile, depth), lambda i: (i, 0)),
        ],
        out_specs=[out, out],
        out_shape=[jax.ShapeDtypeStruct((frames, pairs, features), jnp.float32)] * 2,
        compiler_params=pltpu.CompilerParams(vmem_limit_bytes=26 * MIB),
        cost_estimate=pl.CostEstimate(flops=1, bytes_accessed=1, transcendentals=0),
        name="norm_product",
    )(merged, weights)


def on_device(
    depth, spaces, tensors, inputs, upstream, action_ids, frame_time, action_table, gain, w_qkv, w_out
):
    batch, local_frames, local_space, features = inputs.shape
    actions = action_table.shape[0]
    shard_rows, _, channels = w_qkv.shape
    z = lax.axis_index("frame")
    s = lax.axis_index("space")
    x = lax.axis_index("tensor")
    y, core = s // 2, s % 2
    frames = depth * local_frames
    pairs = batch * local_space // depth
    slots = depth // batch
    slice_width = features // tensors
    head_width = channels // 2
    width = 4 * head_width
    tokens = frames * 2 * pairs

    def ring(value, shift):
        return lax.ppermute(value, "frame", [(i, (i + shift) % depth) for i in range(depth)])

    def swap_z(value, bit):
        return lax.ppermute(value, "frame", [(i, i ^ bit) for i in range(depth)])

    def swap_core(value):
        return lax.ppermute(value, "space", [(i, i ^ 1) for i in range(spaces)])

    def swap_y(value):
        return lax.ppermute(value, "space", [(i, i ^ 2) for i in range(spaces)])

    def swap_x(value):
        return lax.ppermute(value, "tensor", [(0, 1), (1, 0)])

    def join_x(own, other=None):
        if tensors == 2:
            other = swap_x(own) if other is None else other
            first = jnp.where(x == 0, own, other)
            second = jnp.where(x == 0, other, own)
            return jnp.concatenate([first, second], -1)
        return lax.all_gather(own, "tensor", axis=own.ndim - 1, tiled=True)

    def cut_x(value, which=None):
        which = x if which is None else which
        return lax.dynamic_slice_in_dim(value, which * slice_width, slice_width, value.ndim - 1)

    def place(j):
        return j // slots, (j % slots) * pairs

    shards = [w_qkv[:, 0], w_qkv[:, 1], w_qkv[:, 2], w_out]

    def core_half(which):
        return jnp.concatenate(
            [jnp.where(which == 0, t[:, :head_width], t[:, head_width:]) for t in shards], 1
        )

    mine, sent = core_half(core), core_half(1 - core)
    other = swap_core(sent)
    block = jnp.concatenate(
        [jnp.where(core == 0, mine, other), jnp.where(core == 0, other, mine)], 0
    )

    def pieces(rows, k, start, size):
        rollout, first = place((z + k) % depth)
        return lax.dynamic_slice(
            rows, (rollout, 0, first, start), (1, local_frames, pairs, size)
        )[0]

    def collect(k, start):
        piece = jnp.stack([pieces(rows, k, start, slice_width) for rows in (inputs, upstream)])
        target, _ = place((z + k) % depth)
        ids = lax.dynamic_index_in_dim(action_ids, target, 0, keepdims=False)
        ids = jnp.broadcast_to(ids.astype(piece.dtype)[:, None], (local_frames, slice_width))
        ids = jnp.pad(ids, ((0, -local_frames % 8), (0, 0)))
        return ring(jnp.concatenate([piece.reshape(-1, slice_width), ids], 0), k)

    piece_shape = (2, local_frames, pairs, slice_width)
    piece_rows = 2 * local_frames * pairs

    def join_piece(own, other):
        ids = own[piece_rows : piece_rows + local_frames, 0].astype(jnp.int32)
        if other is not None:
            other = other[:piece_rows].reshape(piece_shape)
        return join_x(own[:piece_rows].reshape(piece_shape), other), ids

    def settle(weights, k, arrived, row):
        start = (z - k) % depth * (2 * block_rows) + row * block_rows
        return lax.dynamic_update_slice(weights, arrived, (start, 0))

    block_rows = 2 * shard_rows
    arrived = collect(1, x * slice_width)
    blocks, across, joined = [], [], []
    rollout, _ = place(z)
    all_ids = [lax.dynamic_index_in_dim(action_ids, rollout, 0, keepdims=False)]
    weights = after(jnp.zeros((features, width), jnp.bfloat16), arrived)
    for k in range(1, depth):
        blocks.append(block)
        across.append(swap_y(block))
        crossed = swap_x(arrived) if tensors == 2 else None
        piece, ids = join_piece(arrived, crossed)
        joined.append(piece)
        all_ids.append(ids)
        following = ring(block, 1)
        weights = settle(weights, k - 1, block, y)
        if k > 1:
            weights = settle(weights, k - 2, across[k - 2], 1 - y)
        earlier = [across[-1], joined[-1] if crossed is None else crossed]
        if k + 1 < depth:
            arrived = collect(k + 1, after(x * slice_width, block))
            following, arrived, weights, earlier = lax.optimization_barrier(
                (following, arrived, weights, earlier)
            )
        block = following
    locals_ = [pieces(rows, 0, 0, features) for rows in (inputs, upstream)]
    own_inputs = jnp.concatenate([locals_[0]] + [both_rows[0] for both_rows in joined], 0)
    own_upstream = jnp.concatenate([locals_[1]] + [both_rows[1] for both_rows in joined], 0)
    ids = jnp.concatenate(all_ids)
    order = (
        (z - jnp.arange(depth, dtype=jnp.int32)[:, None]) % depth * local_frames
        + jnp.arange(local_frames, dtype=jnp.int32)[None, :]
    ).reshape(frames)
    own_time = lax.dynamic_index_in_dim(frame_time, rollout, 0, keepdims=False)
    times = jnp.sum(
        jnp.where(
            order[:, None] == jnp.arange(frames, dtype=jnp.int32)[None, :], own_time[None, :], 0
        ),
        1,
    )
    onehot = (ids[:, None] == jnp.arange(actions, dtype=jnp.int32)[None, :]).astype(jnp.float32)
    embedded = jnp.dot(onehot, action_table, precision=lax.Precision.HIGHEST)
    hidden = own_inputs.astype(jnp.float32) + embedded[:, None, :]
    inverse = lax.rsqrt(jnp.mean(hidden * hidden, -1, keepdims=True) + NORM_EPSILON)
    normed = (hidden * inverse * gain).astype(jnp.bfloat16)

    block, normed, own_upstream, weights, near = lax.optimization_barrier(
        (block, normed, own_upstream, weights, across[-1])
    )
    far = swap_y(block)

    def both(own):
        return jnp.concatenate([own, swap_core(own)], 1).reshape(tokens, features)

    all_upstream = both(own_upstream)
    all_normed = both(normed)
    normed_t, upstream_t = turn(all_normed), turn(all_upstream)
    weights = settle(weights, depth - 2, near, 1 - y)
    weights = settle(weights, depth - 1, block, y)
    weights = settle(weights, depth - 1, after(far, normed_t, upstream_t), 1 - y)
    qkv, grad_heads = project(all_normed, all_upstream, weights)
    mixed, merged, peaks = temporal_attention(
        qkv.reshape(frames, 2 * pairs, 3 * head_width),
        grad_heads.reshape(frames, 2 * pairs, head_width),
        times,
    )
    flat_mixed = mixed.reshape(tokens, head_width)
    flat_merged = merged.reshape(tokens, 3 * head_width)

    peaks = jnp.max(peaks, (1, 2))
    own_bound = tokens * jnp.where(
        lax.broadcasted_iota(jnp.int32, (1, width), 1) < 3 * head_width,
        math.sqrt(features) * jnp.max(jnp.abs(gain)) * peaks[1],
        UPSTREAM_TOP * peaks[0],
    )
    own_bound = jnp.maximum(own_bound, 1e-20)

    def pack(value, bound):
        exponent = jnp.ceil(jnp.log2(bound / WIRE_TOP))
        return jnp.concatenate(
            [value * jnp.exp2(-exponent), jnp.broadcast_to(exponent, (8, width))], 0
        ).astype(WIRE)

    def unpack(sent):
        scale = jnp.exp2(sent[block_rows : block_rows + 1].astype(jnp.float32))
        return sent[:block_rows].astype(jnp.float32) * scale, scale * WIRE_TOP

    weight_terms = weight_product(normed_t, upstream_t, flat_merged, flat_mixed)

    def weight_part(k, row):
        start = ((z - 1 - k) % depth * 2 + row) * block_rows
        return lax.dynamic_slice_in_dim(weight_terms, start, block_rows, 0)

    def chip_sum(k, earlier):
        term, bound = unpack(after(swap_y(away[k]), earlier))
        return weight_part(k, y) + term, bound + own_bound

    def ring_sum(k, arriving, earlier):
        total, bound = chip_sum(k, earlier)
        term, ring_bound = unpack(arriving)
        return total + term, bound + ring_bound

    away = [pack(weight_part(0, 1 - y), own_bound)]
    norm_here, norm_away = norm_product(after(flat_merged, away[0]), weights, frames)
    away.append(pack(after(weight_part(1, 1 - y), norm_away), own_bound))
    payload = pack(*chip_sum(0, away[1]))
    partial_norm = norm_here + swap_core(after(norm_away, payload))
    row_dot = jnp.sum(partial_norm * gain * (hidden * inverse), -1, keepdims=True)
    if tensors == 2:
        x_away = cut_x(partial_norm, 1 - x)
        row_scale = jnp.max(jnp.abs(partial_norm), -1, keepdims=True)
        row_scale = jnp.maximum(row_scale, 1e-20) / WIRE_TOP
        sent = (x_away / row_scale).astype(WIRE)
        row_terms = swap_x(jnp.concatenate([row_dot, row_scale], -1))
        x_terms = swap_x(sent)
    else:
        row_dot = lax.psum(row_dot, "tensor")
        grad_norm = lax.psum_scatter(partial_norm, "tensor", scatter_dimension=2, tiled=True)
        sent = partial_norm
    away.append(pack(after(weight_part(2, 1 - y), sent), own_bound))
    payload = pack(*ring_sum(1, ring(payload, 1), away[2]))
    away.append(pack(after(weight_part(3, 1 - y), payload), own_bound))
    if tensors == 2:
        x_terms, row_terms = after((x_terms, row_terms), away[3])
        row_dot = row_dot + row_terms[..., :1]
        grad_norm = cut_x(partial_norm) + x_terms.astype(jnp.float32) * row_terms[..., 1:]
    unit_rows = (cut_x(own_inputs).astype(jnp.float32) + cut_x(embedded)[:, None, :]) * inverse
    grad_hidden = cut_x(own_upstream).astype(jnp.float32) + inverse * (
        grad_norm * cut_x(gain) - unit_rows * (row_dot / features)
    )
    grad_rows = grad_hidden.astype(jnp.bfloat16)
    gain_term = jnp.sum(grad_norm * unit_rows, (0, 1))
    action_term = jnp.dot(
        onehot.T, jnp.sum(grad_hidden, 1), precision=lax.Precision.HIGHEST
    )
    small = jnp.concatenate([action_term, gain_term[None, :]], 0)
    returned = [grad_rows[:local_frames]]
    for k in range(1, depth):
        returned.append(
            ring(grad_rows[k * local_frames : (k + 1) * local_frames], depth - k)
        )

    small = after(small, returned[1])
    small = small + swap_core(small)
    small = join_x(small + swap_y(small))
    for k in range(2, depth - 1):
        payload = pack(*ring_sum(k, ring(payload, 1), (returned[1:], small)))
        if k + 2 < depth:
            away.append(pack(after(weight_part(k + 2, 1 - y), payload), own_bound))
    grad_inputs = jnp.zeros(inputs.shape, jnp.bfloat16)
    for k in range(depth):
        piece = after(returned[k], payload)
        target, first = place((z + k) % depth)
        grad_inputs = lax.dynamic_update_slice(
            grad_inputs, join_x(piece)[None], (target, 0, first, 0)
        )
    small = small + after(swap_z(small, 1), grad_inputs)
    arriving, grad_inputs, small = lax.optimization_barrier(
        (ring(payload, 1), grad_inputs, small)
    )
    bit = 2
    while bit < depth:
        small = small + swap_z(small, bit)
        bit *= 2
    total = chip_sum(depth - 1, arriving)[0] + unpack(arriving)[0]
    mine = lax.dynamic_slice_in_dim(total, core * shard_rows, shard_rows, 0)
    other = swap_core(lax.dynamic_slice_in_dim(total, (1 - core) * shard_rows, shard_rows, 0))
    first = jnp.where(core == 0, mine, other).reshape(shard_rows, 4, head_width)
    second = jnp.where(core == 0, other, mine).reshape(shard_rows, 4, head_width)
    joined = jnp.concatenate([first, second], 2)
    return (grad_inputs, joined[:, :3], joined[:, 3], small[actions], small[:actions])


def solution(mesh):
    sizes = mesh.shape
    return jax.shard_map(
        functools.partial(on_device, sizes["frame"], sizes["space"], sizes["tensor"]),
        mesh=mesh,
        in_specs=(
            P(None, "frame", "space", None),
            P(None, "frame", "space", None),
            P(None, "frame"),
            P(),
            P(),
            P(),
            P(("frame", "space"), None, "tensor"),
            P(("frame", "space"), "tensor"),
        ),
        out_specs=(
            P(None, "frame", "space", None),
            P(("frame", "space"), None, "tensor"),
            P(("frame", "space"), "tensor"),
            P(),
            P(),
        ),
        check_vma=False,
    )
```

```python
import functools
import math

import jax
import jax.numpy as jnp
from jax import lax
from jax.experimental import pallas as pl
from jax.experimental.pallas import tpu as pltpu
from jax.sharding import PartitionSpec as P

HEAD = 128
NORM_EPSILON = 1e-06
UPSTREAM_TOP = 6.0
WIRE = jnp.float16
WIRE_TOP = 32768.0
MIB = 1024 * 1024


def after(value, *earlier):
    return lax.optimization_barrier((value, earlier))[0]


def dot_nt(a, b):
    return lax.dot_general(a, b, (((1,), (1,)), ((), ())), preferred_element_type=jnp.float32)


def dot_nn(a, b):
    return lax.dot_general(a, b, (((1,), (0,)), ((), ())), preferred_element_type=jnp.float32)


def dot_tn(a, b):
    return lax.dot_general(a, b, (((0,), (0,)), ((), ())), preferred_element_type=jnp.float32)


def attention_kernel(
    late_ref, early_ref, qkv_ref, grad_ref, mixed_ref, merged_ref, peak_ref
):
    frames, group, width = grad_ref.shape
    rows = frames * group
    scale = 1.0 / math.sqrt(HEAD)

    def load(ref, start):
        block = ref[:, :, start : start + HEAD]
        if group % 16:
            return block.astype(jnp.float32).reshape(rows, HEAD).astype(jnp.bfloat16)
        return block.reshape(rows, HEAD)

    def store(ref, start, value):
        if group % 16:
            ref[:, :, start : start + HEAD] = value.reshape(frames, group, HEAD).astype(
                jnp.bfloat16
            )
        else:
            ref[:, :, start : start + HEAD] = value.astype(jnp.bfloat16).reshape(
                frames, group, HEAD
            )

    def peak(value):
        return jnp.max(jnp.abs(value).reshape(rows // 8, 8, HEAD), axis=0)

    @pl.when(pl.program_id(0) == 0)
    def _():
        peak_ref[...] = jnp.zeros_like(peak_ref)

    row_id = lax.broadcasted_iota(jnp.int32, (rows, rows), 0)
    col_id = lax.broadcasted_iota(jnp.int32, (rows, rows), 1)
    allowed = (row_id % group == col_id % group) & (early_ref[...] <= late_ref[...])
    starts = range(0, width, HEAD)
    query = [load(qkv_ref, i) for i in starts]
    key = [load(qkv_ref, width + i) for i in starts]
    value = [load(qkv_ref, 2 * width + i) for i in starts]
    grad = [load(grad_ref, i) for i in starts]
    heads = range(len(query))
    scores = [jnp.where(allowed, dot_nt(query[h], key[h]) * scale, -1e30) for h in heads]
    grad_probs = [dot_nt(grad[h], value[h]) for h in heads]
    exponent = [jnp.exp(scores[h] - jnp.max(scores[h], -1, keepdims=True)) for h in heads]
    probabilities = [exponent[h] / jnp.sum(exponent[h], -1, keepdims=True) for h in heads]
    rounded = [probabilities[h].astype(jnp.bfloat16) for h in heads]
    mean_grad = [jnp.sum(grad_probs[h] * probabilities[h], -1, keepdims=True) for h in heads]
    mixed = [dot_nn(rounded[h], value[h]) for h in heads]
    grad_value = [dot_tn(rounded[h], grad[h]) for h in heads]
    grad_scores = [probabilities[h] * (grad_probs[h] - mean_grad[h]) for h in heads]
    high = [grad_scores[h].astype(jnp.bfloat16) for h in heads]
    low = [(grad_scores[h] - high[h].astype(jnp.float32)).astype(jnp.bfloat16) for h in heads]
    grad_query = [(dot_nn(high[h], key[h]) + dot_nn(low[h], key[h])) * scale for h in heads]
    grad_key = [(dot_tn(high[h], query[h]) + dot_tn(low[h], query[h])) * scale for h in heads]
    top_out, top_qkv = peak_ref[0], peak_ref[1]
    for h, start in enumerate(starts):
        store(mixed_ref, start, mixed[h])
        store(merged_ref, start, grad_query[h])
        store(merged_ref, width + start, grad_key[h])
        store(merged_ref, 2 * width + start, grad_value[h])
        top_out = jnp.maximum(top_out, peak(mixed[h]))
        for term in (grad_query[h], grad_key[h], grad_value[h]):
            top_qkv = jnp.maximum(top_qkv, peak(term))
    peak_ref[0] = top_out
    peak_ref[1] = top_qkv


def temporal_attention(qkv, grad_heads, times):
    frames, pairs, width = grad_heads.shape
    group = 16 if pairs % 16 == 0 else 8
    rows = frames * group
    per_row = jnp.repeat(times.astype(jnp.float32), group)
    work = pairs // group * rows * rows * (width // HEAD)
    fixed = lambda i: (0, 0)
    moving = lambda i: (0, i, 0)
    return pl.pallas_call(
        attention_kernel,
        grid=(pairs // group,),
        in_specs=[
            pl.BlockSpec((rows, 1), fixed),
            pl.BlockSpec((1, rows), fixed),
            pl.BlockSpec((frames, group, 3 * width), moving),
            pl.BlockSpec((frames, group, width), moving),
        ],
        out_specs=[
            pl.BlockSpec((frames, group, width), moving),
            pl.BlockSpec((frames, group, 3 * width), moving),
            pl.BlockSpec((2, 8, HEAD), lambda i: (0, 0, 0)),
        ],
        out_shape=[
            jax.ShapeDtypeStruct((frames, pairs, width), jnp.bfloat16),
            jax.ShapeDtypeStruct((frames, pairs, 3 * width), jnp.bfloat16),
            jax.ShapeDtypeStruct((2, 8, HEAD), jnp.float32),
        ],
        compiler_params=pltpu.CompilerParams(vmem_limit_bytes=16 * MIB),
        cost_estimate=pl.CostEstimate(
            flops=16 * work * HEAD,
            bytes_accessed=16 * frames * pairs * width,
            transcendentals=work,
        ),
        name="temporal_attention",
    )(per_row[:, None], per_row[None, :], qkv, grad_heads)


def turn_kernel(rows_ref, out_ref):
    out_ref[...] = rows_ref[...].T


def turn(rows):
    tokens, features = rows.shape
    tile = features // 8
    return pl.pallas_call(
        turn_kernel,
        grid=(8,),
        in_specs=[pl.BlockSpec((tokens, tile), lambda i: (0, i))],
        out_specs=pl.BlockSpec((tile, tokens), lambda i: (i, 0)),
        out_shape=jax.ShapeDtypeStruct((features, tokens), rows.dtype),
        compiler_params=pltpu.CompilerParams(vmem_limit_bytes=12 * MIB),
        cost_estimate=pl.CostEstimate(flops=1, bytes_accessed=1, transcendentals=0),
        name="turn",
    )(rows)


def weight_kernel(place_ref, norm_ref, up_ref, merged_ref, mixed_ref, near_ref, far_ref):
    step = pl.program_id(0)
    rows = near_ref.shape[0]
    first = place_ref[1] == 0

    def store(both):
        near_ref[...] = jnp.where(first, both[:rows], both[rows:])
        far_ref[...] = jnp.where(first, both[rows:], both[:rows])

    @pl.when(step < 3)
    def _():
        store(dot_nn(norm_ref[...], merged_ref[...]))

    @pl.when(step == 3)
    def _():
        store(dot_nn(up_ref[...], mixed_ref[...]))


def weight_product(places, rows, normed, upstream, merged, mixed):
    tokens, width = mixed.shape
    pair = pl.BlockSpec((2 * rows, tokens), lambda i, at: (at[0], 0))
    out = pl.BlockSpec((rows, width), lambda i, at: (0, i))
    return pl.pallas_call(
        weight_kernel,
        grid_spec=pltpu.PrefetchScalarGridSpec(
            num_scalar_prefetch=1,
            grid=(4,),
            in_specs=[
                pair,
                pair,
                pl.BlockSpec((tokens, width), lambda i, at: (0, jnp.minimum(i, 2))),
                pl.BlockSpec((tokens, width), lambda i, at: (0, 0)),
            ],
            out_specs=[out, out],
        ),
        out_shape=[jax.ShapeDtypeStruct((rows, 4 * width), jnp.float32)] * 2,
        compiler_params=pltpu.CompilerParams(vmem_limit_bytes=58 * MIB),
        cost_estimate=pl.CostEstimate(flops=1, bytes_accessed=1, transcendentals=0),
        name="weight_product",
    )(places, normed, upstream, merged, mixed)


def project_kernel(normed_ref, up_ref, weight_ref, qkv_ref, grad_ref):
    @pl.when(pl.program_id(0) < 3)
    def _():
        qkv_ref[...] = dot_nn(normed_ref[...], weight_ref[...]).astype(jnp.bfloat16)

    @pl.when(pl.program_id(0) == 3)
    def _():
        grad_ref[...] = dot_nn(up_ref[...], weight_ref[...]).astype(jnp.bfloat16)


def project(normed, upstream, weights):
    tokens, features = normed.shape
    width = weights.shape[1] // 4
    rows = tokens // 2
    return pl.pallas_call(
        project_kernel,
        grid=(4, 2),
        in_specs=[
            pl.BlockSpec((rows, features), lambda i, j: (jnp.where(i < 3, j, 1), 0)),
            pl.BlockSpec((rows, features), lambda i, j: (jnp.where(i < 3, 0, j), 0)),
            pl.BlockSpec((features, width), lambda i, j: (0, i)),
        ],
        out_specs=[
            pl.BlockSpec(
                (rows, width), lambda i, j: (jnp.where(i < 3, j, 1), jnp.minimum(i, 2))
            ),
            pl.BlockSpec((rows, width), lambda i, j: (jnp.where(i < 3, 0, j), 0)),
        ],
        out_shape=[
            jax.ShapeDtypeStruct((tokens, 3 * width), jnp.bfloat16),
            jax.ShapeDtypeStruct((tokens, width), jnp.bfloat16),
        ],
        compiler_params=pltpu.CompilerParams(vmem_limit_bytes=26 * MIB),
        cost_estimate=pl.CostEstimate(
            flops=2 * tokens * features * 4 * width,
            bytes_accessed=8 * tokens * features,
            transcendentals=0,
        ),
        name="project",
    )(normed, upstream, weights)


def norm_kernel(merged_ref, weight_ref, own_ref, other_ref):
    frames, pairs, tile = own_ref.shape
    rows = dot_nt(merged_ref[...], weight_ref[...]).reshape(frames, 2 * pairs, tile)
    own_ref[...] = rows[:, :pairs]
    other_ref[...] = rows[:, pairs:]


def norm_product(merged, weights, frames):
    rows, depth = merged.shape
    features = weights.shape[0]
    tile = features // 4
    pairs = rows // frames // 2
    out = pl.BlockSpec((frames, pairs, tile), lambda i: (0, 0, i))
    return pl.pallas_call(
        norm_kernel,
        grid=(4,),
        in_specs=[
            pl.BlockSpec((rows, depth), lambda i: (0, 0)),
            pl.BlockSpec((tile, depth), lambda i: (i, 0)),
        ],
        out_specs=[out, out],
        out_shape=[jax.ShapeDtypeStruct((frames, pairs, features), jnp.float32)] * 2,
        compiler_params=pltpu.CompilerParams(vmem_limit_bytes=26 * MIB),
        cost_estimate=pl.CostEstimate(flops=1, bytes_accessed=1, transcendentals=0),
        name="norm_product",
    )(merged, weights)


def on_device(
    depth, spaces, tensors, inputs, upstream, action_ids, frame_time, action_table, gain, w_qkv, w_out
):
    batch, local_frames, local_space, features = inputs.shape
    actions = action_table.shape[0]
    shard_rows, _, channels = w_qkv.shape
    z = lax.axis_index("frame")
    s = lax.axis_index("space")
    x = lax.axis_index("tensor")
    y, core = s // 2, s % 2
    frames = depth * local_frames
    pairs = batch * local_space // depth
    slots = depth // batch
    slice_width = features // tensors
    head_width = channels // 2
    width = 4 * head_width
    tokens = frames * 2 * pairs

    def ring(value, shift):
        return lax.ppermute(value, "frame", [(i, (i + shift) % depth) for i in range(depth)])

    def swap_z(value, bit):
        return lax.ppermute(value, "frame", [(i, i ^ bit) for i in range(depth)])

    def swap_core(value):
        return lax.ppermute(value, "space", [(i, i ^ 1) for i in range(spaces)])

    def swap_y(value):
        return lax.ppermute(value, "space", [(i, i ^ 2) for i in range(spaces)])

    def swap_x(value):
        return lax.ppermute(value, "tensor", [(0, 1), (1, 0)])

    def join_x(own, other=None):
        if tensors == 2:
            other = swap_x(own) if other is None else other
            first = jnp.where(x == 0, own, other)
            second = jnp.where(x == 0, other, own)
            return jnp.concatenate([first, second], -1)
        return lax.all_gather(own, "tensor", axis=own.ndim - 1, tiled=True)

    def cut_x(value, which=None):
        which = x if which is None else which
        return lax.dynamic_slice_in_dim(value, which * slice_width, slice_width, value.ndim - 1)

    def place(j):
        return j // slots, (j % slots) * pairs

    shards = [w_qkv[:, 0], w_qkv[:, 1], w_qkv[:, 2], w_out]

    def core_half(which):
        return jnp.concatenate(
            [jnp.where(which == 0, t[:, :head_width], t[:, head_width:]) for t in shards], 1
        )

    mine, sent = core_half(core), core_half(1 - core)
    other = swap_core(sent)
    block = jnp.concatenate(
        [jnp.where(core == 0, mine, other), jnp.where(core == 0, other, mine)], 0
    )

    def pieces(rows, k, start, size):
        rollout, first = place((z + k) % depth)
        return lax.dynamic_slice(
            rows, (rollout, 0, first, start), (1, local_frames, pairs, size)
        )[0]

    def collect(k, start):
        piece = jnp.stack([pieces(rows, k, start, slice_width) for rows in (inputs, upstream)])
        target, _ = place((z + k) % depth)
        ids = lax.dynamic_index_in_dim(action_ids, target, 0, keepdims=False)
        ids = jnp.broadcast_to(ids.astype(piece.dtype)[:, None], (local_frames, slice_width))
        ids = jnp.pad(ids, ((0, -local_frames % 8), (0, 0)))
        return ring(jnp.concatenate([piece.reshape(-1, slice_width), ids], 0), k)

    piece_shape = (2, local_frames, pairs, slice_width)
    piece_rows = 2 * local_frames * pairs

    def join_piece(own, other):
        ids = own[piece_rows : piece_rows + local_frames, 0].astype(jnp.int32)
        if other is not None:
            other = other[:piece_rows].reshape(piece_shape)
        return join_x(own[:piece_rows].reshape(piece_shape), other), ids

    def settle(weights, k, arrived, row):
        start = (z - k) % depth * (2 * block_rows) + row * block_rows
        return lax.dynamic_update_slice(weights, arrived, (start, 0))

    block_rows = 2 * shard_rows
    arrived = collect(1, x * slice_width)
    blocks, across, joined = [], [], []
    rollout, _ = place(z)
    all_ids = [lax.dynamic_index_in_dim(action_ids, rollout, 0, keepdims=False)]
    weights = after(jnp.zeros((features, width), jnp.bfloat16), arrived)
    for k in range(1, depth):
        blocks.append(block)
        across.append(swap_y(block))
        crossed = swap_x(arrived) if tensors == 2 else None
        piece, ids = join_piece(arrived, crossed)
        joined.append(piece)
        all_ids.append(ids)
        following = ring(block, 1)
        weights = settle(weights, k - 1, block, y)
        if k > 1:
            weights = settle(weights, k - 2, across[k - 2], 1 - y)
        earlier = [across[-1], joined[-1] if crossed is None else crossed]
        if k + 1 < depth:
            arrived = collect(k + 1, after(x * slice_width, block))
            following, arrived, weights, earlier = lax.optimization_barrier(
                (following, arrived, weights, earlier)
            )
        block = following
    locals_ = [pieces(rows, 0, 0, features) for rows in (inputs, upstream)]
    own_inputs = jnp.concatenate([locals_[0]] + [both_rows[0] for both_rows in joined], 0)
    own_upstream = jnp.concatenate([locals_[1]] + [both_rows[1] for both_rows in joined], 0)
    ids = jnp.concatenate(all_ids)
    order = (
        (z - jnp.arange(depth, dtype=jnp.int32)[:, None]) % depth * local_frames
        + jnp.arange(local_frames, dtype=jnp.int32)[None, :]
    ).reshape(frames)
    own_time = lax.dynamic_index_in_dim(frame_time, rollout, 0, keepdims=False)
    times = jnp.sum(
        jnp.where(
            order[:, None] == jnp.arange(frames, dtype=jnp.int32)[None, :], own_time[None, :], 0
        ),
        1,
    )
    onehot = (ids[:, None] == jnp.arange(actions, dtype=jnp.int32)[None, :]).astype(jnp.float32)
    embedded = jnp.dot(onehot, action_table, precision=lax.Precision.HIGHEST)
    hidden = own_inputs.astype(jnp.float32) + embedded[:, None, :]
    inverse = lax.rsqrt(jnp.mean(hidden * hidden, -1, keepdims=True) + NORM_EPSILON)
    normed = (hidden * inverse * gain).astype(jnp.bfloat16)

    block, normed, own_upstream, weights, near = lax.optimization_barrier(
        (block, normed, own_upstream, weights, across[-1])
    )
    far = swap_y(block)

    def both(own):
        return jnp.concatenate([own, swap_core(own)], 1).reshape(tokens, features)

    all_upstream = both(own_upstream)
    all_normed = both(normed)
    normed_t, upstream_t = turn(all_normed), turn(all_upstream)
    weights = settle(weights, depth - 2, near, 1 - y)
    weights = settle(weights, depth - 1, block, y)
    weights = settle(weights, depth - 1, after(far, normed_t, upstream_t), 1 - y)
    qkv, grad_heads = project(all_normed, all_upstream, weights)
    mixed, merged, peaks = temporal_attention(
        qkv.reshape(frames, 2 * pairs, 3 * head_width),
        grad_heads.reshape(frames, 2 * pairs, head_width),
        times,
    )
    flat_mixed = mixed.reshape(tokens, head_width)
    flat_merged = merged.reshape(tokens, 3 * head_width)

    peaks = jnp.max(peaks, (1, 2))
    own_bound = tokens * jnp.where(
        lax.broadcasted_iota(jnp.int32, (1, width), 1) < 3 * head_width,
        math.sqrt(features) * jnp.max(jnp.abs(gain)) * peaks[1],
        UPSTREAM_TOP * peaks[0],
    )
    own_bound = jnp.maximum(own_bound, 1e-20)

    def pack(value, bound):
        exponent = jnp.ceil(jnp.log2(bound / WIRE_TOP))
        return jnp.concatenate(
            [value * jnp.exp2(-exponent), jnp.broadcast_to(exponent, (8, width))], 0
        ).astype(WIRE)

    def unpack(sent):
        scale = jnp.exp2(sent[block_rows : block_rows + 1].astype(jnp.float32))
        return sent[:block_rows].astype(jnp.float32) * scale, scale * WIRE_TOP

    def weight_part(k, earlier):
        places = jnp.stack([after((z - 1 - k) % depth, earlier), y])
        near, far = weight_product(
            places, block_rows, normed_t, upstream_t, flat_merged, flat_mixed
        )
        return near, pack(far, own_bound)

    def chip_sum(k, earlier):
        term, bound = unpack(after(swap_y(weight_parts[k][1]), earlier))
        return weight_parts[k][0] + term, bound + own_bound

    def ring_sum(k, arriving, earlier):
        total, bound = chip_sum(k, earlier)
        term, ring_bound = unpack(arriving)
        return total + term, bound + ring_bound

    weight_parts = [weight_part(0, flat_merged)]
    norm_here, norm_away = norm_product(
        after(flat_merged, weight_parts[0][1]), weights, frames
    )
    weight_parts.append(weight_part(1, norm_away))
    payload = pack(*chip_sum(0, weight_parts[1][1]))
    partial_norm = norm_here + swap_core(after(norm_away, payload))
    row_dot = jnp.sum(partial_norm * gain * (hidden * inverse), -1, keepdims=True)
    if tensors == 2:
        x_away = cut_x(partial_norm, 1 - x)
        row_scale = jnp.max(jnp.abs(partial_norm), -1, keepdims=True)
        row_scale = jnp.maximum(row_scale, 1e-20) / WIRE_TOP
        sent = (x_away / row_scale).astype(WIRE)
        row_terms = swap_x(jnp.concatenate([row_dot, row_scale], -1))
        x_terms = swap_x(sent)
    else:
        row_dot = lax.psum(row_dot, "tensor")
        grad_norm = lax.psum_scatter(partial_norm, "tensor", scatter_dimension=2, tiled=True)
        sent = partial_norm
    weight_parts.append(weight_part(2, sent))
    payload = pack(*ring_sum(1, ring(payload, 1), weight_parts[2][1]))
    weight_parts.append(weight_part(3, payload))
    if tensors == 2:
        x_terms, row_terms = after((x_terms, row_terms), weight_parts[3][1])
        row_dot = row_dot + row_terms[..., :1]
        grad_norm = cut_x(partial_norm) + x_terms.astype(jnp.float32) * row_terms[..., 1:]
    unit_rows = (cut_x(own_inputs).astype(jnp.float32) + cut_x(embedded)[:, None, :]) * inverse
    grad_hidden = cut_x(own_upstream).astype(jnp.float32) + inverse * (
        grad_norm * cut_x(gain) - unit_rows * (row_dot / features)
    )
    grad_rows = grad_hidden.astype(jnp.bfloat16)
    gain_term = jnp.sum(grad_norm * unit_rows, (0, 1))
    action_term = jnp.dot(
        onehot.T, jnp.sum(grad_hidden, 1), precision=lax.Precision.HIGHEST
    )
    small = jnp.concatenate([action_term, gain_term[None, :]], 0)
    small = small + swap_core(small)
    small = small + swap_z(small, 1)
    returned = [grad_rows[:local_frames]]
    for k in range(1, depth):
        returned.append(
            ring(grad_rows[k * local_frames : (k + 1) * local_frames], depth - k)
        )

    for k in range(2, depth - 1):
        payload = pack(*ring_sum(k, ring(payload, 1), (returned[1:], small)))
        if k + 2 < depth:
            weight_parts.append(weight_part(k + 2, payload))
    grad_inputs = jnp.zeros(inputs.shape, jnp.bfloat16)
    for k in range(depth):
        piece = after(returned[k], payload)
        target, first = place((z + k) % depth)
        grad_inputs = lax.dynamic_update_slice(
            grad_inputs, join_x(piece)[None], (target, 0, first, 0)
        )
    small = after(small, payload)
    bit = 2
    while bit < depth:
        small = small + after(swap_z(small, bit), grad_inputs)
        bit *= 2
    arriving, grad_inputs, small = lax.optimization_barrier(
        (ring(payload, 1), grad_inputs, small)
    )
    small = join_x(small + swap_y(small))
    total = chip_sum(depth - 1, arriving)[0] + unpack(arriving)[0]
    mine = lax.dynamic_slice_in_dim(total, core * shard_rows, shard_rows, 0)
    other = swap_core(lax.dynamic_slice_in_dim(total, (1 - core) * shard_rows, shard_rows, 0))
    first = jnp.where(core == 0, mine, other).reshape(shard_rows, 4, head_width)
    second = jnp.where(core == 0, other, mine).reshape(shard_rows, 4, head_width)
    joined = jnp.concatenate([first, second], 2)
    return (grad_inputs, joined[:, :3], joined[:, 3], small[actions], small[:actions])


def solution(mesh):
    sizes = mesh.shape
    return jax.shard_map(
        functools.partial(on_device, sizes["frame"], sizes["space"], sizes["tensor"]),
        mesh=mesh,
        in_specs=(
            P(None, "frame", "space", None),
            P(None, "frame", "space", None),
            P(None, "frame"),
            P(),
            P(),
            P(),
            P(("frame", "space"), None, "tensor"),
            P(("frame", "space"), "tensor"),
        ),
        out_specs=(
            P(None, "frame", "space", None),
            P(("frame", "space"), None, "tensor"),
            P(("frame", "space"), "tensor"),
            P(),
            P(),
        ),
        check_vma=False,
    )
```

```python
import functools
import math

import jax
import jax.numpy as jnp
from jax import lax
from jax.experimental import pallas as pl
from jax.experimental.pallas import tpu as pltpu
from jax.sharding import PartitionSpec as P

HEAD = 128
NORM_EPSILON = 1e-06
UPSTREAM_TOP = 6.0
WIRE = jnp.float16
WIRE_TOP = 32768.0
MIB = 1024 * 1024


def after(value, *earlier):
    return lax.optimization_barrier((value, earlier))[0]


def dot_nt(a, b):
    return lax.dot_general(a, b, (((1,), (1,)), ((), ())), preferred_element_type=jnp.float32)


def dot_nn(a, b):
    return lax.dot_general(a, b, (((1,), (0,)), ((), ())), preferred_element_type=jnp.float32)


def dot_tn(a, b):
    return lax.dot_general(a, b, (((0,), (0,)), ((), ())), preferred_element_type=jnp.float32)


def attention_kernel(
    late_ref, early_ref, qkv_ref, grad_ref, mixed_ref, merged_ref, peak_ref
):
    frames, group, width = grad_ref.shape
    rows = frames * group
    scale = 1.0 / math.sqrt(HEAD)

    def load(ref, start):
        block = ref[:, :, start : start + HEAD]
        if group % 16:
            return block.astype(jnp.float32).reshape(rows, HEAD).astype(jnp.bfloat16)
        return block.reshape(rows, HEAD)

    def store(ref, start, value):
        if group % 16:
            ref[:, :, start : start + HEAD] = value.reshape(frames, group, HEAD).astype(
                jnp.bfloat16
            )
        else:
            ref[:, :, start : start + HEAD] = value.astype(jnp.bfloat16).reshape(
                frames, group, HEAD
            )

    def peak(value):
        return jnp.max(jnp.abs(value).reshape(rows // 8, 8, HEAD), axis=0)

    @pl.when(pl.program_id(0) == 0)
    def _():
        peak_ref[...] = jnp.zeros_like(peak_ref)

    row_id = lax.broadcasted_iota(jnp.int32, (rows, rows), 0)
    col_id = lax.broadcasted_iota(jnp.int32, (rows, rows), 1)
    allowed = (row_id % group == col_id % group) & (early_ref[...] <= late_ref[...])
    starts = range(0, width, HEAD)
    query = [load(qkv_ref, i) for i in starts]
    key = [load(qkv_ref, width + i) for i in starts]
    value = [load(qkv_ref, 2 * width + i) for i in starts]
    grad = [load(grad_ref, i) for i in starts]
    heads = range(len(query))
    scores = [jnp.where(allowed, dot_nt(query[h], key[h]) * scale, -1e30) for h in heads]
    grad_probs = [dot_nt(grad[h], value[h]) for h in heads]
    exponent = [jnp.exp(scores[h] - jnp.max(scores[h], -1, keepdims=True)) for h in heads]
    probabilities = [exponent[h] / jnp.sum(exponent[h], -1, keepdims=True) for h in heads]
    rounded = [probabilities[h].astype(jnp.bfloat16) for h in heads]
    mean_grad = [jnp.sum(grad_probs[h] * probabilities[h], -1, keepdims=True) for h in heads]
    mixed = [dot_nn(rounded[h], value[h]) for h in heads]
    grad_value = [dot_tn(rounded[h], grad[h]) for h in heads]
    grad_scores = [probabilities[h] * (grad_probs[h] - mean_grad[h]) for h in heads]
    high = [grad_scores[h].astype(jnp.bfloat16) for h in heads]
    low = [(grad_scores[h] - high[h].astype(jnp.float32)).astype(jnp.bfloat16) for h in heads]
    grad_query = [(dot_nn(high[h], key[h]) + dot_nn(low[h], key[h])) * scale for h in heads]
    grad_key = [(dot_tn(high[h], query[h]) + dot_tn(low[h], query[h])) * scale for h in heads]
    top_out, top_qkv = peak_ref[0], peak_ref[1]
    for h, start in enumerate(starts):
        store(mixed_ref, start, mixed[h])
        store(merged_ref, start, grad_query[h])
        store(merged_ref, width + start, grad_key[h])
        store(merged_ref, 2 * width + start, grad_value[h])
        top_out = jnp.maximum(top_out, peak(mixed[h]))
        for term in (grad_query[h], grad_key[h], grad_value[h]):
            top_qkv = jnp.maximum(top_qkv, peak(term))
    peak_ref[0] = top_out
    peak_ref[1] = top_qkv


def temporal_attention(qkv, grad_heads, times):
    frames, pairs, width = grad_heads.shape
    group = 16 if pairs % 16 == 0 else 8
    rows = frames * group
    per_row = jnp.repeat(times.astype(jnp.float32), group)
    work = pairs // group * rows * rows * (width // HEAD)
    fixed = lambda i: (0, 0)
    moving = lambda i: (0, i, 0)
    return pl.pallas_call(
        attention_kernel,
        grid=(pairs // group,),
        in_specs=[
            pl.BlockSpec((rows, 1), fixed),
            pl.BlockSpec((1, rows), fixed),
            pl.BlockSpec((frames, group, 3 * width), moving),
            pl.BlockSpec((frames, group, width), moving),
        ],
        out_specs=[
            pl.BlockSpec((frames, group, width), moving),
            pl.BlockSpec((frames, group, 3 * width), moving),
            pl.BlockSpec((2, 8, HEAD), lambda i: (0, 0, 0)),
        ],
        out_shape=[
            jax.ShapeDtypeStruct((frames, pairs, width), jnp.bfloat16),
            jax.ShapeDtypeStruct((frames, pairs, 3 * width), jnp.bfloat16),
            jax.ShapeDtypeStruct((2, 8, HEAD), jnp.float32),
        ],
        compiler_params=pltpu.CompilerParams(vmem_limit_bytes=16 * MIB),
        cost_estimate=pl.CostEstimate(
            flops=16 * work * HEAD,
            bytes_accessed=16 * frames * pairs * width,
            transcendentals=work,
        ),
        name="temporal_attention",
    )(per_row[:, None], per_row[None, :], qkv, grad_heads)


def turn_kernel(rows_ref, out_ref):
    out_ref[...] = rows_ref[...].T


def turn(rows):
    tokens, features = rows.shape
    tile = features // 8
    return pl.pallas_call(
        turn_kernel,
        grid=(8,),
        in_specs=[pl.BlockSpec((tokens, tile), lambda i: (0, i))],
        out_specs=pl.BlockSpec((tile, tokens), lambda i: (i, 0)),
        out_shape=jax.ShapeDtypeStruct((features, tokens), rows.dtype),
        compiler_params=pltpu.CompilerParams(vmem_limit_bytes=12 * MIB),
        cost_estimate=pl.CostEstimate(flops=1, bytes_accessed=1, transcendentals=0),
        name="turn",
    )(rows)


def weight_kernel(place_ref, norm_ref, up_ref, merged_ref, mixed_ref, near_ref, far_ref):
    step = pl.program_id(0)
    rows = near_ref.shape[0]
    first = place_ref[1] == 0

    def store(both):
        near_ref[...] = jnp.where(first, both[:rows], both[rows:])
        far_ref[...] = jnp.where(first, both[rows:], both[:rows])

    @pl.when(step < 3)
    def _():
        store(dot_nn(norm_ref[...], merged_ref[...]))

    @pl.when(step == 3)
    def _():
        store(dot_nn(up_ref[...], mixed_ref[...]))


def weight_product(places, rows, normed, upstream, merged, mixed):
    tokens, width = mixed.shape
    pair = pl.BlockSpec((2 * rows, tokens), lambda i, at: (at[0], 0))
    out = pl.BlockSpec((rows, width), lambda i, at: (0, i))
    return pl.pallas_call(
        weight_kernel,
        grid_spec=pltpu.PrefetchScalarGridSpec(
            num_scalar_prefetch=1,
            grid=(4,),
            in_specs=[
                pair,
                pair,
                pl.BlockSpec((tokens, width), lambda i, at: (0, jnp.minimum(i, 2))),
                pl.BlockSpec((tokens, width), lambda i, at: (0, 0)),
            ],
            out_specs=[out, out],
        ),
        out_shape=[jax.ShapeDtypeStruct((rows, 4 * width), jnp.float32)] * 2,
        compiler_params=pltpu.CompilerParams(vmem_limit_bytes=58 * MIB),
        cost_estimate=pl.CostEstimate(flops=1, bytes_accessed=1, transcendentals=0),
        name="weight_product",
    )(places, normed, upstream, merged, mixed)


def project_kernel(normed_ref, up_ref, weight_ref, qkv_ref, grad_ref):
    @pl.when(pl.program_id(0) < 3)
    def _():
        qkv_ref[...] = dot_nn(normed_ref[...], weight_ref[...]).astype(jnp.bfloat16)

    @pl.when(pl.program_id(0) == 3)
    def _():
        grad_ref[...] = dot_nn(up_ref[...], weight_ref[...]).astype(jnp.bfloat16)


def project(normed, upstream, weights):
    tokens, features = normed.shape
    width = weights.shape[1] // 4
    rows = tokens // 2
    return pl.pallas_call(
        project_kernel,
        grid=(4, 2),
        in_specs=[
            pl.BlockSpec((rows, features), lambda i, j: (jnp.where(i < 3, j, 1), 0)),
            pl.BlockSpec((rows, features), lambda i, j: (jnp.where(i < 3, 0, j), 0)),
            pl.BlockSpec((features, width), lambda i, j: (0, i)),
        ],
        out_specs=[
            pl.BlockSpec(
                (rows, width), lambda i, j: (jnp.where(i < 3, j, 1), jnp.minimum(i, 2))
            ),
            pl.BlockSpec((rows, width), lambda i, j: (jnp.where(i < 3, 0, j), 0)),
        ],
        out_shape=[
            jax.ShapeDtypeStruct((tokens, 3 * width), jnp.bfloat16),
            jax.ShapeDtypeStruct((tokens, width), jnp.bfloat16),
        ],
        compiler_params=pltpu.CompilerParams(vmem_limit_bytes=26 * MIB),
        cost_estimate=pl.CostEstimate(
            flops=2 * tokens * features * 4 * width,
            bytes_accessed=8 * tokens * features,
            transcendentals=0,
        ),
        name="project",
    )(normed, upstream, weights)


def norm_kernel(merged_ref, weight_ref, own_ref, other_ref):
    frames, pairs, tile = own_ref.shape
    rows = dot_nt(merged_ref[...], weight_ref[...]).reshape(frames, 2 * pairs, tile)
    own_ref[...] = rows[:, :pairs]
    other_ref[...] = rows[:, pairs:]


def norm_product(merged, weights, frames):
    rows, depth = merged.shape
    features = weights.shape[0]
    tile = features // 4
    pairs = rows // frames // 2
    out = pl.BlockSpec((frames, pairs, tile), lambda i: (0, 0, i))
    return pl.pallas_call(
        norm_kernel,
        grid=(4,),
        in_specs=[
            pl.BlockSpec((rows, depth), lambda i: (0, 0)),
            pl.BlockSpec((tile, depth), lambda i: (i, 0)),
        ],
        out_specs=[out, out],
        out_shape=[jax.ShapeDtypeStruct((frames, pairs, features), jnp.float32)] * 2,
        compiler_params=pltpu.CompilerParams(vmem_limit_bytes=26 * MIB),
        cost_estimate=pl.CostEstimate(flops=1, bytes_accessed=1, transcendentals=0),
        name="norm_product",
    )(merged, weights)


def on_device(
    depth, spaces, tensors, inputs, upstream, action_ids, frame_time, action_table, gain, w_qkv, w_out
):
    batch, local_frames, local_space, features = inputs.shape
    actions = action_table.shape[0]
    shard_rows, _, channels = w_qkv.shape
    z = lax.axis_index("frame")
    s = lax.axis_index("space")
    x = lax.axis_index("tensor")
    y, core = s // 2, s % 2
    frames = depth * local_frames
    pairs = batch * local_space // depth
    slots = depth // batch
    slice_width = features // tensors
    head_width = channels // 2
    width = 4 * head_width
    tokens = frames * 2 * pairs

    def ring(value, shift):
        return lax.ppermute(value, "frame", [(i, (i + shift) % depth) for i in range(depth)])

    def swap_z(value, bit):
        return lax.ppermute(value, "frame", [(i, i ^ bit) for i in range(depth)])

    def swap_core(value):
        return lax.ppermute(value, "space", [(i, i ^ 1) for i in range(spaces)])

    def swap_y(value):
        return lax.ppermute(value, "space", [(i, i ^ 2) for i in range(spaces)])

    def swap_xy(value):
        pairs_xy = [(i, ((i // 2) ^ 2) * 2 + (i % 2 ^ 1)) for i in range(2 * spaces)]
        return lax.ppermute(value, ("space", "tensor"), pairs_xy)

    def swap_x(value):
        return lax.ppermute(value, "tensor", [(0, 1), (1, 0)])

    def join_x(own, other=None):
        if tensors == 2:
            other = swap_x(own) if other is None else other
            first = jnp.where(x == 0, own, other)
            second = jnp.where(x == 0, other, own)
            return jnp.concatenate([first, second], -1)
        return lax.all_gather(own, "tensor", axis=own.ndim - 1, tiled=True)

    def cut_x(value, which=None):
        which = x if which is None else which
        return lax.dynamic_slice_in_dim(value, which * slice_width, slice_width, value.ndim - 1)

    def place(j):
        return j // slots, (j % slots) * pairs

    shards = [w_qkv[:, 0], w_qkv[:, 1], w_qkv[:, 2], w_out]

    def core_half(which):
        return jnp.concatenate(
            [jnp.where(which == 0, t[:, :head_width], t[:, head_width:]) for t in shards], 1
        )

    mine, sent = core_half(core), core_half(1 - core)
    other = swap_core(sent)
    block = jnp.concatenate(
        [jnp.where(core == 0, mine, other), jnp.where(core == 0, other, mine)], 0
    )

    def pieces(rows, k, start, size):
        rollout, first = place((z + k) % depth)
        return lax.dynamic_slice(
            rows, (rollout, 0, first, start), (1, local_frames, pairs, size)
        )[0]

    def collect(k, start):
        piece = jnp.stack([pieces(rows, k, start, slice_width) for rows in (inputs, upstream)])
        target, _ = place((z + k) % depth)
        ids = lax.dynamic_index_in_dim(action_ids, target, 0, keepdims=False)
        ids = jnp.broadcast_to(ids.astype(piece.dtype)[:, None], (local_frames, slice_width))
        ids = jnp.pad(ids, ((0, -local_frames % 8), (0, 0)))
        return ring(jnp.concatenate([piece.reshape(-1, slice_width), ids], 0), k)

    piece_shape = (2, local_frames, pairs, slice_width)
    piece_rows = 2 * local_frames * pairs

    def join_piece(own, other):
        ids = own[piece_rows : piece_rows + local_frames, 0].astype(jnp.int32)
        if other is not None:
            other = other[:piece_rows].reshape(piece_shape)
        return join_x(own[:piece_rows].reshape(piece_shape), other), ids

    def settle(weights, k, arrived, row):
        start = (z - k) % depth * (2 * block_rows) + row * block_rows
        return lax.dynamic_update_slice(weights, arrived, (start, 0))

    block_rows = 2 * shard_rows
    arrived = collect(1, x * slice_width)
    blocks, across, joined = [], [], []
    rollout, _ = place(z)
    all_ids = [lax.dynamic_index_in_dim(action_ids, rollout, 0, keepdims=False)]
    weights = after(jnp.zeros((features, width), jnp.bfloat16), arrived)
    for k in range(1, depth):
        blocks.append(block)
        across.append(swap_y(block))
        crossed = swap_x(arrived) if tensors == 2 else None
        piece, ids = join_piece(arrived, crossed)
        joined.append(piece)
        all_ids.append(ids)
        following = ring(block, 1)
        weights = settle(weights, k - 1, block, y)
        if k > 1:
            weights = settle(weights, k - 2, across[k - 2], 1 - y)
        earlier = [across[-1], joined[-1] if crossed is None else crossed]
        if k + 1 < depth:
            arrived = collect(k + 1, after(x * slice_width, block))
            following, arrived, weights, earlier = lax.optimization_barrier(
                (following, arrived, weights, earlier)
            )
        block = following
    locals_ = [pieces(rows, 0, 0, features) for rows in (inputs, upstream)]
    own_inputs = jnp.concatenate([locals_[0]] + [both_rows[0] for both_rows in joined], 0)
    own_upstream = jnp.concatenate([locals_[1]] + [both_rows[1] for both_rows in joined], 0)
    ids = jnp.concatenate(all_ids)
    order = (
        (z - jnp.arange(depth, dtype=jnp.int32)[:, None]) % depth * local_frames
        + jnp.arange(local_frames, dtype=jnp.int32)[None, :]
    ).reshape(frames)
    own_time = lax.dynamic_index_in_dim(frame_time, rollout, 0, keepdims=False)
    times = jnp.sum(
        jnp.where(
            order[:, None] == jnp.arange(frames, dtype=jnp.int32)[None, :], own_time[None, :], 0
        ),
        1,
    )
    onehot = (ids[:, None] == jnp.arange(actions, dtype=jnp.int32)[None, :]).astype(jnp.float32)
    embedded = jnp.dot(onehot, action_table, precision=lax.Precision.HIGHEST)
    hidden = own_inputs.astype(jnp.float32) + embedded[:, None, :]
    inverse = lax.rsqrt(jnp.mean(hidden * hidden, -1, keepdims=True) + NORM_EPSILON)
    normed = (hidden * inverse * gain).astype(jnp.bfloat16)

    block, normed, own_upstream, weights, near = lax.optimization_barrier(
        (block, normed, own_upstream, weights, across[-1])
    )
    far = swap_y(block)

    def both(own):
        return jnp.concatenate([own, swap_core(own)], 1).reshape(tokens, features)

    all_upstream = both(own_upstream)
    all_normed = both(normed)
    normed_t, upstream_t = turn(all_normed), turn(all_upstream)
    weights = settle(weights, depth - 2, near, 1 - y)
    weights = settle(weights, depth - 1, block, y)
    weights = settle(weights, depth - 1, after(far, normed_t, upstream_t), 1 - y)
    qkv, grad_heads = project(all_normed, all_upstream, weights)
    mixed, merged, peaks = temporal_attention(
        qkv.reshape(frames, 2 * pairs, 3 * head_width),
        grad_heads.reshape(frames, 2 * pairs, head_width),
        times,
    )
    flat_mixed = mixed.reshape(tokens, head_width)
    flat_merged = merged.reshape(tokens, 3 * head_width)

    peaks = jnp.max(peaks, (1, 2))
    own_bound = tokens * jnp.where(
        lax.broadcasted_iota(jnp.int32, (1, width), 1) < 3 * head_width,
        math.sqrt(features) * jnp.max(jnp.abs(gain)) * peaks[1],
        UPSTREAM_TOP * peaks[0],
    )
    own_bound = jnp.maximum(own_bound, 1e-20)

    def pack(value, bound):
        exponent = jnp.ceil(jnp.log2(bound / WIRE_TOP))
        return jnp.concatenate(
            [value * jnp.exp2(-exponent), jnp.broadcast_to(exponent, (8, width))], 0
        ).astype(WIRE)

    def unpack(sent):
        scale = jnp.exp2(sent[block_rows : block_rows + 1].astype(jnp.float32))
        return sent[:block_rows].astype(jnp.float32) * scale, scale * WIRE_TOP

    def weight_part(k, earlier):
        places = jnp.stack([after((z - 1 - k) % depth, earlier), y])
        near, far = weight_product(
            places, block_rows, normed_t, upstream_t, flat_merged, flat_mixed
        )
        return near, far

    def chip_sum(k, earlier):
        term, bound = unpack(after(swap_y(away[k]), earlier))
        return weight_parts[k][0] + term, bound + own_bound

    def ring_sum(k, arriving, earlier):
        total, bound = chip_sum(k, earlier)
        term, ring_bound = unpack(arriving)
        return total + term, bound + ring_bound

    weight_parts = [weight_part(0, flat_merged)]
    away = [pack(weight_parts[0][1], own_bound)]
    norm_here, norm_away = norm_product(
        after(flat_merged, away[0]), weights, frames
    )
    weight_parts.append(weight_part(1, norm_away))
    away.append(pack(weight_parts[1][1], own_bound))
    payload = pack(*chip_sum(0, away[1]))
    partial_norm = norm_here + swap_core(after(norm_away, payload))
    row_dot = jnp.sum(partial_norm * gain * (hidden * inverse), -1, keepdims=True)
    if tensors == 2:
        x_away = cut_x(partial_norm, 1 - x)
        row_scale = jnp.max(jnp.abs(partial_norm), -1, keepdims=True)
        row_scale = jnp.maximum(row_scale, 1e-20) / WIRE_TOP
        sent = (x_away / row_scale).astype(WIRE)
        row_terms = swap_x(jnp.concatenate([row_dot, row_scale], -1))
        x_terms = swap_x(sent)
    else:
        row_dot = lax.psum(row_dot, "tensor")
        grad_norm = lax.psum_scatter(partial_norm, "tensor", scatter_dimension=2, tiled=True)
        sent = partial_norm
    weight_parts.append(weight_part(2, sent))
    payload = pack(*ring_sum(1, ring(payload, 1), weight_parts[2][1]))
    away.append(pack(after(weight_parts[2][1], payload), own_bound))
    weight_parts.append(weight_part(3, away[2]))
    if tensors == 2:
        x_terms, row_terms = after((x_terms, row_terms), weight_parts[3][1])
        row_dot = row_dot + row_terms[..., :1]
        grad_norm = cut_x(partial_norm) + x_terms.astype(jnp.float32) * row_terms[..., 1:]
    unit_rows = (cut_x(own_inputs).astype(jnp.float32) + cut_x(embedded)[:, None, :]) * inverse
    grad_hidden = cut_x(own_upstream).astype(jnp.float32) + inverse * (
        grad_norm * cut_x(gain) - unit_rows * (row_dot / features)
    )
    grad_rows = grad_hidden.astype(jnp.bfloat16)
    gain_term = jnp.sum(grad_norm * unit_rows, (0, 1))
    action_term = jnp.dot(
        onehot.T, jnp.sum(grad_hidden, 1), precision=lax.Precision.HIGHEST
    )
    small = jnp.concatenate([action_term, gain_term[None, :]], 0)
    small = small + swap_core(small)
    small = small + swap_z(small, 1)
    away.append(pack(after(weight_parts[3][1], grad_rows), own_bound))
    returned = [grad_rows[:local_frames]]
    for k in range(1, depth):
        returned.append(
            ring(grad_rows[k * local_frames : (k + 1) * local_frames], depth - k)
        )

    for k in range(2, depth - 1):
        payload = pack(*ring_sum(k, ring(payload, 1), (returned[1:], small, away[-1])))
        if k + 2 < depth:
            weight_parts.append(weight_part(k + 2, payload))
            away.append(pack(weight_parts[-1][1], own_bound))
    grad_inputs = jnp.zeros(inputs.shape, jnp.bfloat16)
    for k in range(depth):
        piece = after(returned[k], payload)
        target, first = place((z + k) % depth)
        grad_inputs = lax.dynamic_update_slice(
            grad_inputs, join_x(piece)[None], (target, 0, first, 0)
        )
    small = after(small, payload)
    bit = 2
    while bit < depth:
        small = small + after(swap_z(small, bit), grad_inputs)
        bit *= 2
    arriving, grad_inputs, small = lax.optimization_barrier(
        (ring(payload, 1), grad_inputs, small)
    )
    if tensors == 2:
        small = join_x(small + swap_y(small), swap_x(small) + swap_xy(small))
    else:
        small = join_x(small + swap_y(small))
    total = chip_sum(depth - 1, arriving)[0] + unpack(arriving)[0]
    mine = lax.dynamic_slice_in_dim(total, core * shard_rows, shard_rows, 0)
    other = swap_core(lax.dynamic_slice_in_dim(total, (1 - core) * shard_rows, shard_rows, 0))
    first = jnp.where(core == 0, mine, other).reshape(shard_rows, 4, head_width)
    second = jnp.where(core == 0, other, mine).reshape(shard_rows, 4, head_width)
    joined = jnp.concatenate([first, second], 2)
    return (grad_inputs, joined[:, :3], joined[:, 3], small[actions], small[:actions])


def solution(mesh):
    sizes = mesh.shape
    return jax.shard_map(
        functools.partial(on_device, sizes["frame"], sizes["space"], sizes["tensor"]),
        mesh=mesh,
        in_specs=(
            P(None, "frame", "space", None),
            P(None, "frame", "space", None),
            P(None, "frame"),
            P(),
            P(),
            P(),
            P(("frame", "space"), None, "tensor"),
            P(("frame", "space"), "tensor"),
        ),
        out_specs=(
            P(None, "frame", "space", None),
            P(("frame", "space"), None, "tensor"),
            P(("frame", "space"), "tensor"),
            P(),
            P(),
        ),
        check_vma=False,
    )
```

```python
import functools
import math

import jax
import jax.numpy as jnp
from jax import lax
from jax.experimental import pallas as pl
from jax.experimental.pallas import tpu as pltpu
from jax.sharding import PartitionSpec as P

HEAD = 128
NORM_EPSILON = 1e-06
UPSTREAM_TOP = 6.0
WIRE = jnp.float16
WIRE_TOP = 32768.0
MIB = 1024 * 1024


def after(value, *earlier):
    return lax.optimization_barrier((value, earlier))[0]


def dot_nt(a, b):
    return lax.dot_general(a, b, (((1,), (1,)), ((), ())), preferred_element_type=jnp.float32)


def dot_nn(a, b):
    return lax.dot_general(a, b, (((1,), (0,)), ((), ())), preferred_element_type=jnp.float32)


def dot_tn(a, b):
    return lax.dot_general(a, b, (((0,), (0,)), ((), ())), preferred_element_type=jnp.float32)


def attention_kernel(
    late_ref, early_ref, qkv_ref, grad_ref, mixed_ref, merged_ref, peak_ref
):
    frames, group, width = grad_ref.shape
    rows = frames * group
    scale = 1.0 / math.sqrt(HEAD)

    def load(ref, start):
        block = ref[:, :, start : start + HEAD]
        if group % 16:
            return block.astype(jnp.float32).reshape(rows, HEAD).astype(jnp.bfloat16)
        return block.reshape(rows, HEAD)

    def store(ref, start, value):
        if group % 16:
            ref[:, :, start : start + HEAD] = value.reshape(frames, group, HEAD).astype(
                jnp.bfloat16
            )
        else:
            ref[:, :, start : start + HEAD] = value.astype(jnp.bfloat16).reshape(
                frames, group, HEAD
            )

    def peak(value):
        return jnp.max(jnp.abs(value).reshape(rows // 8, 8, HEAD), axis=0)

    @pl.when(pl.program_id(0) == 0)
    def _():
        peak_ref[...] = jnp.zeros_like(peak_ref)

    row_id = lax.broadcasted_iota(jnp.int32, (rows, rows), 0)
    col_id = lax.broadcasted_iota(jnp.int32, (rows, rows), 1)
    allowed = (row_id % group == col_id % group) & (early_ref[...] <= late_ref[...])
    starts = range(0, width, HEAD)
    query = [load(qkv_ref, i) for i in starts]
    key = [load(qkv_ref, width + i) for i in starts]
    value = [load(qkv_ref, 2 * width + i) for i in starts]
    grad = [load(grad_ref, i) for i in starts]
    heads = range(len(query))
    scores = [jnp.where(allowed, dot_nt(query[h], key[h]) * scale, -1e30) for h in heads]
    grad_probs = [dot_nt(grad[h], value[h]) for h in heads]
    exponent = [jnp.exp(scores[h] - jnp.max(scores[h], -1, keepdims=True)) for h in heads]
    probabilities = [exponent[h] / jnp.sum(exponent[h], -1, keepdims=True) for h in heads]
    rounded = [probabilities[h].astype(jnp.bfloat16) for h in heads]
    mean_grad = [jnp.sum(grad_probs[h] * probabilities[h], -1, keepdims=True) for h in heads]
    mixed = [dot_nn(rounded[h], value[h]) for h in heads]
    grad_value = [dot_tn(rounded[h], grad[h]) for h in heads]
    grad_scores = [probabilities[h] * (grad_probs[h] - mean_grad[h]) for h in heads]
    high = [grad_scores[h].astype(jnp.bfloat16) for h in heads]
    low = [(grad_scores[h] - high[h].astype(jnp.float32)).astype(jnp.bfloat16) for h in heads]
    grad_query = [(dot_nn(high[h], key[h]) + dot_nn(low[h], key[h])) * scale for h in heads]
    grad_key = [(dot_tn(high[h], query[h]) + dot_tn(low[h], query[h])) * scale for h in heads]
    top_out, top_qkv = peak_ref[0], peak_ref[1]
    for h, start in enumerate(starts):
        store(mixed_ref, start, mixed[h])
        store(merged_ref, start, grad_query[h])
        store(merged_ref, width + start, grad_key[h])
        store(merged_ref, 2 * width + start, grad_value[h])
        top_out = jnp.maximum(top_out, peak(mixed[h]))
        for term in (grad_query[h], grad_key[h], grad_value[h]):
            top_qkv = jnp.maximum(top_qkv, peak(term))
    peak_ref[0] = top_out
    peak_ref[1] = top_qkv


def temporal_attention(qkv, grad_heads, times):
    frames, pairs, width = grad_heads.shape
    group = 16 if pairs % 16 == 0 else 8
    rows = frames * group
    per_row = jnp.repeat(times.astype(jnp.float32), group)
    work = pairs // group * rows * rows * (width // HEAD)
    fixed = lambda i: (0, 0)
    moving = lambda i: (0, i, 0)
    return pl.pallas_call(
        attention_kernel,
        grid=(pairs // group,),
        in_specs=[
            pl.BlockSpec((rows, 1), fixed),
            pl.BlockSpec((1, rows), fixed),
            pl.BlockSpec((frames, group, 3 * width), moving),
            pl.BlockSpec((frames, group, width), moving),
        ],
        out_specs=[
            pl.BlockSpec((frames, group, width), moving),
            pl.BlockSpec((frames, group, 3 * width), moving),
            pl.BlockSpec((2, 8, HEAD), lambda i: (0, 0, 0)),
        ],
        out_shape=[
            jax.ShapeDtypeStruct((frames, pairs, width), jnp.bfloat16),
            jax.ShapeDtypeStruct((frames, pairs, 3 * width), jnp.bfloat16),
            jax.ShapeDtypeStruct((2, 8, HEAD), jnp.float32),
        ],
        compiler_params=pltpu.CompilerParams(vmem_limit_bytes=16 * MIB),
        cost_estimate=pl.CostEstimate(
            flops=16 * work * HEAD,
            bytes_accessed=16 * frames * pairs * width,
            transcendentals=work,
        ),
        name="temporal_attention",
    )(per_row[:, None], per_row[None, :], qkv, grad_heads)


def turn_kernel(rows_ref, out_ref):
    out_ref[...] = rows_ref[...].T


def turn(rows):
    tokens, features = rows.shape
    tile = features // 8
    return pl.pallas_call(
        turn_kernel,
        grid=(8,),
        in_specs=[pl.BlockSpec((tokens, tile), lambda i: (0, i))],
        out_specs=pl.BlockSpec((tile, tokens), lambda i: (i, 0)),
        out_shape=jax.ShapeDtypeStruct((features, tokens), rows.dtype),
        compiler_params=pltpu.CompilerParams(vmem_limit_bytes=12 * MIB),
        cost_estimate=pl.CostEstimate(flops=1, bytes_accessed=1, transcendentals=0),
        name="turn",
    )(rows)


def weight_kernel(place_ref, norm_ref, up_ref, merged_ref, mixed_ref, near_ref, far_ref):
    step = pl.program_id(0)
    rows = near_ref.shape[0]
    first = place_ref[1] == 0

    def store(both):
        near_ref[...] = jnp.where(first, both[:rows], both[rows:])
        far_ref[...] = jnp.where(first, both[rows:], both[:rows])

    @pl.when(step < 3)
    def _():
        store(dot_nn(norm_ref[...], merged_ref[...]))

    @pl.when(step == 3)
    def _():
        store(dot_nn(up_ref[...], mixed_ref[...]))


def weight_product(places, rows, normed, upstream, merged, mixed):
    tokens, width = mixed.shape
    pair = pl.BlockSpec((2 * rows, tokens), lambda i, at: (at[0], 0))
    out = pl.BlockSpec((rows, width), lambda i, at: (0, i))
    return pl.pallas_call(
        weight_kernel,
        grid_spec=pltpu.PrefetchScalarGridSpec(
            num_scalar_prefetch=1,
            grid=(4,),
            in_specs=[
                pair,
                pair,
                pl.BlockSpec((tokens, width), lambda i, at: (0, jnp.minimum(i, 2))),
                pl.BlockSpec((tokens, width), lambda i, at: (0, 0)),
            ],
            out_specs=[out, out],
        ),
        out_shape=[jax.ShapeDtypeStruct((rows, 4 * width), jnp.float32)] * 2,
        compiler_params=pltpu.CompilerParams(vmem_limit_bytes=58 * MIB),
        cost_estimate=pl.CostEstimate(flops=1, bytes_accessed=1, transcendentals=0),
        name="weight_product",
    )(places, normed, upstream, merged, mixed)


def project_kernel(normed_ref, up_ref, weight_ref, qkv_ref, grad_ref):
    @pl.when(pl.program_id(0) < 3)
    def _():
        qkv_ref[...] = dot_nn(normed_ref[...], weight_ref[...]).astype(jnp.bfloat16)

    @pl.when(pl.program_id(0) == 3)
    def _():
        grad_ref[...] = dot_nn(up_ref[...], weight_ref[...]).astype(jnp.bfloat16)


def project(normed, upstream, weights):
    tokens, features = normed.shape
    width = weights.shape[1] // 4
    rows = tokens // 2
    return pl.pallas_call(
        project_kernel,
        grid=(4, 2),
        in_specs=[
            pl.BlockSpec((rows, features), lambda i, j: (jnp.where(i < 3, j, 1), 0)),
            pl.BlockSpec((rows, features), lambda i, j: (jnp.where(i < 3, 0, j), 0)),
            pl.BlockSpec((features, width), lambda i, j: (0, i)),
        ],
        out_specs=[
            pl.BlockSpec(
                (rows, width), lambda i, j: (jnp.where(i < 3, j, 1), jnp.minimum(i, 2))
            ),
            pl.BlockSpec((rows, width), lambda i, j: (jnp.where(i < 3, 0, j), 0)),
        ],
        out_shape=[
            jax.ShapeDtypeStruct((tokens, 3 * width), jnp.bfloat16),
            jax.ShapeDtypeStruct((tokens, width), jnp.bfloat16),
        ],
        compiler_params=pltpu.CompilerParams(vmem_limit_bytes=26 * MIB),
        cost_estimate=pl.CostEstimate(
            flops=2 * tokens * features * 4 * width,
            bytes_accessed=8 * tokens * features,
            transcendentals=0,
        ),
        name="project",
    )(normed, upstream, weights)


def norm_kernel(merged_ref, weight_ref, own_ref, other_ref):
    frames, pairs, tile = own_ref.shape
    rows = dot_nt(merged_ref[...], weight_ref[...]).reshape(frames, 2 * pairs, tile)
    own_ref[...] = rows[:, :pairs]
    other_ref[...] = rows[:, pairs:]


def norm_product(merged, weights, frames):
    rows, depth = merged.shape
    features = weights.shape[0]
    tile = features // 4
    pairs = rows // frames // 2
    out = pl.BlockSpec((frames, pairs, tile), lambda i: (0, 0, i))
    return pl.pallas_call(
        norm_kernel,
        grid=(4,),
        in_specs=[
            pl.BlockSpec((rows, depth), lambda i: (0, 0)),
            pl.BlockSpec((tile, depth), lambda i: (i, 0)),
        ],
        out_specs=[out, out],
        out_shape=[jax.ShapeDtypeStruct((frames, pairs, features), jnp.float32)] * 2,
        compiler_params=pltpu.CompilerParams(vmem_limit_bytes=26 * MIB),
        cost_estimate=pl.CostEstimate(flops=1, bytes_accessed=1, transcendentals=0),
        name="norm_product",
    )(merged, weights)


def on_device(
    depth, spaces, tensors, inputs, upstream, action_ids, frame_time, action_table, gain, w_qkv, w_out
):
    batch, local_frames, local_space, features = inputs.shape
    actions = action_table.shape[0]
    shard_rows, _, channels = w_qkv.shape
    z = lax.axis_index("frame")
    s = lax.axis_index("space")
    x = lax.axis_index("tensor")
    y, core = s // 2, s % 2
    frames = depth * local_frames
    pairs = batch * local_space // depth
    slots = depth // batch
    slice_width = features // tensors
    head_width = channels // 2
    width = 4 * head_width
    tokens = frames * 2 * pairs

    def ring(value, shift):
        return lax.ppermute(value, "frame", [(i, (i + shift) % depth) for i in range(depth)])

    def swap_z(value, bit):
        return lax.ppermute(value, "frame", [(i, i ^ bit) for i in range(depth)])

    def swap_core(value):
        return lax.ppermute(value, "space", [(i, i ^ 1) for i in range(spaces)])

    def swap_y(value):
        return lax.ppermute(value, "space", [(i, i ^ 2) for i in range(spaces)])

    def swap_xy(value):
        pairs_xy = [(i, ((i // 2) ^ 2) * 2 + (i % 2 ^ 1)) for i in range(2 * spaces)]
        return lax.ppermute(value, ("space", "tensor"), pairs_xy)

    def swap_x(value):
        return lax.ppermute(value, "tensor", [(0, 1), (1, 0)])

    def join_x(own, other=None):
        if tensors == 2:
            other = swap_x(own) if other is None else other
            first = jnp.where(x == 0, own, other)
            second = jnp.where(x == 0, other, own)
            return jnp.concatenate([first, second], -1)
        return lax.all_gather(own, "tensor", axis=own.ndim - 1, tiled=True)

    def cut_x(value, which=None):
        which = x if which is None else which
        return lax.dynamic_slice_in_dim(value, which * slice_width, slice_width, value.ndim - 1)

    def place(j):
        return j // slots, (j % slots) * pairs

    shards = [w_qkv[:, 0], w_qkv[:, 1], w_qkv[:, 2], w_out]

    def core_half(which):
        return jnp.concatenate(
            [jnp.where(which == 0, t[:, :head_width], t[:, head_width:]) for t in shards], 1
        )

    mine, sent = core_half(core), core_half(1 - core)
    other = swap_core(sent)
    block = jnp.concatenate(
        [jnp.where(core == 0, mine, other), jnp.where(core == 0, other, mine)], 0
    )

    def pieces(rows, k, start, size):
        rollout, first = place((z + k) % depth)
        return lax.dynamic_slice(
            rows, (rollout, 0, first, start), (1, local_frames, pairs, size)
        )[0]

    def collect(k, start):
        piece = jnp.stack([pieces(rows, k, start, slice_width) for rows in (inputs, upstream)])
        target, _ = place((z + k) % depth)
        ids = lax.dynamic_index_in_dim(action_ids, target, 0, keepdims=False)
        ids = jnp.broadcast_to(ids.astype(piece.dtype)[:, None], (local_frames, slice_width))
        ids = jnp.pad(ids, ((0, -local_frames % 8), (0, 0)))
        return ring(jnp.concatenate([piece.reshape(-1, slice_width), ids], 0), k)

    piece_shape = (2, local_frames, pairs, slice_width)
    piece_rows = 2 * local_frames * pairs

    def join_piece(own, other):
        ids = own[piece_rows : piece_rows + local_frames, 0].astype(jnp.int32)
        if other is not None:
            other = other[:piece_rows].reshape(piece_shape)
        return join_x(own[:piece_rows].reshape(piece_shape), other), ids

    def settle(weights, k, arrived, row):
        start = (z - k) % depth * (2 * block_rows) + row * block_rows
        return lax.dynamic_update_slice(weights, arrived, (start, 0))

    block_rows = 2 * shard_rows
    arrived = collect(1, x * slice_width)
    blocks, across, joined = [], [], []
    rollout, _ = place(z)
    all_ids = [lax.dynamic_index_in_dim(action_ids, rollout, 0, keepdims=False)]
    weights = after(jnp.zeros((features, width), jnp.bfloat16), arrived)
    for k in range(1, depth):
        blocks.append(block)
        across.append(swap_y(block))
        crossed = swap_x(arrived) if tensors == 2 else None
        piece, ids = join_piece(arrived, crossed)
        joined.append(piece)
        all_ids.append(ids)
        following = ring(block, 1)
        weights = settle(weights, k - 1, block, y)
        if k > 1:
            weights = settle(weights, k - 2, across[k - 2], 1 - y)
        earlier = [across[-1], joined[-1] if crossed is None else crossed]
        if k + 1 < depth:
            arrived = collect(k + 1, after(x * slice_width, block))
            following, arrived, weights, earlier = lax.optimization_barrier(
                (following, arrived, weights, earlier)
            )
        block = following
    locals_ = [pieces(rows, 0, 0, features) for rows in (inputs, upstream)]
    own_inputs = jnp.concatenate([locals_[0]] + [both_rows[0] for both_rows in joined], 0)
    own_upstream = jnp.concatenate([locals_[1]] + [both_rows[1] for both_rows in joined], 0)
    ids = jnp.concatenate(all_ids)
    order = (
        (z - jnp.arange(depth, dtype=jnp.int32)[:, None]) % depth * local_frames
        + jnp.arange(local_frames, dtype=jnp.int32)[None, :]
    ).reshape(frames)
    own_time = lax.dynamic_index_in_dim(frame_time, rollout, 0, keepdims=False)
    times = jnp.sum(
        jnp.where(
            order[:, None] == jnp.arange(frames, dtype=jnp.int32)[None, :], own_time[None, :], 0
        ),
        1,
    )
    onehot = (ids[:, None] == jnp.arange(actions, dtype=jnp.int32)[None, :]).astype(jnp.float32)
    embedded = jnp.dot(onehot, action_table, precision=lax.Precision.HIGHEST)
    hidden = own_inputs.astype(jnp.float32) + embedded[:, None, :]
    inverse = lax.rsqrt(jnp.mean(hidden * hidden, -1, keepdims=True) + NORM_EPSILON)
    normed = (hidden * inverse * gain).astype(jnp.bfloat16)

    block, normed, own_upstream, weights, near = lax.optimization_barrier(
        (block, normed, own_upstream, weights, across[-1])
    )
    far = swap_y(block)

    def both(own):
        return jnp.concatenate([own, swap_core(own)], 1).reshape(tokens, features)

    all_upstream = both(own_upstream)
    all_normed = both(normed)
    normed_t, upstream_t = turn(all_normed), turn(all_upstream)
    weights = settle(weights, depth - 2, near, 1 - y)
    weights = settle(weights, depth - 1, block, y)
    weights = settle(weights, depth - 1, after(far, normed_t, upstream_t), 1 - y)
    qkv, grad_heads = project(all_normed, all_upstream, weights)
    mixed, merged, peaks = temporal_attention(
        qkv.reshape(frames, 2 * pairs, 3 * head_width),
        grad_heads.reshape(frames, 2 * pairs, head_width),
        times,
    )
    flat_mixed = mixed.reshape(tokens, head_width)
    flat_merged = merged.reshape(tokens, 3 * head_width)

    peaks = jnp.max(peaks, (1, 2))
    own_bound = tokens * jnp.where(
        lax.broadcasted_iota(jnp.int32, (1, width), 1) < 3 * head_width,
        math.sqrt(features) * jnp.max(jnp.abs(gain)) * peaks[1],
        UPSTREAM_TOP * peaks[0],
    )
    own_bound = jnp.maximum(own_bound, 1e-20)

    def pack(value, bound):
        exponent = jnp.ceil(jnp.log2(bound / WIRE_TOP))
        return jnp.concatenate(
            [value * jnp.exp2(-exponent), jnp.broadcast_to(exponent, (8, width))], 0
        ).astype(WIRE)

    def unpack(sent):
        scale = jnp.exp2(sent[block_rows : block_rows + 1].astype(jnp.float32))
        return sent[:block_rows].astype(jnp.float32) * scale, scale * WIRE_TOP

    def weight_part(k, earlier):
        places = jnp.stack([after((z - 1 - k) % depth, earlier), y])
        near, far = weight_product(
            places, block_rows, normed_t, upstream_t, flat_merged, flat_mixed
        )
        return near, pack(far, own_bound)

    def chip_sum(k, earlier):
        term, bound = unpack(after(swap_y(weight_parts[k][1]), earlier))
        return weight_parts[k][0] + term, bound + own_bound

    def ring_sum(k, arriving, earlier):
        total, bound = chip_sum(k, earlier)
        term, ring_bound = unpack(arriving)
        return total + term, bound + ring_bound

    weight_parts = [weight_part(0, flat_merged)]
    norm_here, norm_away = norm_product(
        after(flat_merged, weight_parts[0][1]), weights, frames
    )
    weight_parts.append(weight_part(1, norm_away))
    payload = pack(*chip_sum(0, weight_parts[1][1]))
    partial_norm = norm_here + swap_core(after(norm_away, payload))
    row_dot = jnp.sum(partial_norm * gain * (hidden * inverse), -1, keepdims=True)
    if tensors == 2:
        x_away = cut_x(partial_norm, 1 - x)
        row_scale = jnp.max(jnp.abs(partial_norm), -1, keepdims=True)
        row_scale = jnp.maximum(row_scale, 1e-20) / WIRE_TOP
        sent = (x_away / row_scale).astype(WIRE)
        row_terms = swap_x(jnp.concatenate([row_dot, row_scale], -1))
        x_terms = swap_x(sent)
    else:
        row_dot = lax.psum(row_dot, "tensor")
        grad_norm = lax.psum_scatter(partial_norm, "tensor", scatter_dimension=2, tiled=True)
        sent = partial_norm
    weight_parts.append(weight_part(2, sent))
    payload = pack(*ring_sum(1, ring(payload, 1), weight_parts[2][1]))
    weight_parts.append(weight_part(3, payload))
    if tensors == 2:
        x_terms, row_terms = after((x_terms, row_terms), weight_parts[3][1])
        row_dot = row_dot + row_terms[..., :1]
        grad_norm = cut_x(partial_norm) + x_terms.astype(jnp.float32) * row_terms[..., 1:]
    unit_rows = (cut_x(own_inputs).astype(jnp.float32) + cut_x(embedded)[:, None, :]) * inverse
    grad_hidden = cut_x(own_upstream).astype(jnp.float32) + inverse * (
        grad_norm * cut_x(gain) - unit_rows * (row_dot / features)
    )
    grad_rows = grad_hidden.astype(jnp.bfloat16)
    gain_term = jnp.sum(grad_norm * unit_rows, (0, 1))
    action_term = jnp.dot(
        onehot.T, jnp.sum(grad_hidden, 1), precision=lax.Precision.HIGHEST
    )
    small = jnp.concatenate([action_term, gain_term[None, :]], 0)
    small = small + swap_core(small)
    small = small + swap_z(small, 1)
    returned = [grad_rows[:local_frames]]
    for k in range(1, depth):
        returned.append(
            ring(grad_rows[k * local_frames : (k + 1) * local_frames], depth - k)
        )

    for k in range(2, depth - 1):
        payload = pack(*ring_sum(k, ring(payload, 1), (returned[1:], small)))
        if k + 2 < depth:
            weight_parts.append(weight_part(k + 2, payload))
    grad_inputs = jnp.zeros(inputs.shape, jnp.bfloat16)
    for k in range(depth):
        piece = after(returned[k], payload)
        target, first = place((z + k) % depth)
        grad_inputs = lax.dynamic_update_slice(
            grad_inputs, join_x(piece)[None], (target, 0, first, 0)
        )
    small = after(small, payload)
    bit = 2
    while bit < depth:
        small = small + after(swap_z(small, bit), grad_inputs)
        bit *= 2
    arriving, grad_inputs, small = lax.optimization_barrier(
        (ring(payload, 1), grad_inputs, small)
    )
    if tensors == 2:
        small = join_x(small + swap_y(small), swap_x(small) + swap_xy(small))
    else:
        small = join_x(small + swap_y(small))
    total = chip_sum(depth - 1, arriving)[0] + unpack(arriving)[0]
    mine = lax.dynamic_slice_in_dim(total, core * shard_rows, shard_rows, 0)
    other = swap_core(lax.dynamic_slice_in_dim(total, (1 - core) * shard_rows, shard_rows, 0))
    first = jnp.where(core == 0, mine, other).reshape(shard_rows, 4, head_width)
    second = jnp.where(core == 0, other, mine).reshape(shard_rows, 4, head_width)
    joined = jnp.concatenate([first, second], 2)
    return (grad_inputs, joined[:, :3], joined[:, 3], small[actions], small[:actions])


def solution(mesh):
    sizes = mesh.shape
    return jax.shard_map(
        functools.partial(on_device, sizes["frame"], sizes["space"], sizes["tensor"]),
        mesh=mesh,
        in_specs=(
            P(None, "frame", "space", None),
            P(None, "frame", "space", None),
            P(None, "frame"),
            P(),
            P(),
            P(),
            P(("frame", "space"), None, "tensor"),
            P(("frame", "space"), "tensor"),
        ),
        out_specs=(
            P(None, "frame", "space", None),
            P(("frame", "space"), None, "tensor"),
            P(("frame", "space"), "tensor"),
            P(),
            P(),
        ),
        check_vma=False,
    )
```

```python
import functools
import math

import jax
import jax.numpy as jnp
from jax import lax
from jax.experimental import pallas as pl
from jax.experimental.pallas import tpu as pltpu
from jax.sharding import PartitionSpec as P

HEAD = 128
NORM_EPSILON = 1e-06
UPSTREAM_TOP = 6.0
WIRE = jnp.float16
WIRE_TOP = 32768.0
MIB = 1024 * 1024


def after(value, *earlier):
    return lax.optimization_barrier((value, earlier))[0]


def dot_nt(a, b):
    return lax.dot_general(a, b, (((1,), (1,)), ((), ())), preferred_element_type=jnp.float32)


def dot_nn(a, b):
    return lax.dot_general(a, b, (((1,), (0,)), ((), ())), preferred_element_type=jnp.float32)


def dot_tn(a, b):
    return lax.dot_general(a, b, (((0,), (0,)), ((), ())), preferred_element_type=jnp.float32)


def attention_kernel(
    late_ref, early_ref, qkv_ref, grad_ref, mixed_ref, merged_ref, peak_ref
):
    frames, group, width = grad_ref.shape
    rows = frames * group
    scale = 1.0 / math.sqrt(HEAD)

    def load(ref, start):
        block = ref[:, :, start : start + HEAD]
        if group % 16:
            return block.astype(jnp.float32).reshape(rows, HEAD).astype(jnp.bfloat16)
        return block.reshape(rows, HEAD)

    def store(ref, start, value):
        if group % 16:
            ref[:, :, start : start + HEAD] = value.reshape(frames, group, HEAD).astype(
                jnp.bfloat16
            )
        else:
            ref[:, :, start : start + HEAD] = value.astype(jnp.bfloat16).reshape(
                frames, group, HEAD
            )

    def peak(value):
        return jnp.max(jnp.abs(value).reshape(rows // 8, 8, HEAD), axis=0)

    @pl.when(pl.program_id(0) == 0)
    def _():
        peak_ref[...] = jnp.zeros_like(peak_ref)

    row_id = lax.broadcasted_iota(jnp.int32, (rows, rows), 0)
    col_id = lax.broadcasted_iota(jnp.int32, (rows, rows), 1)
    allowed = (row_id % group == col_id % group) & (early_ref[...] <= late_ref[...])
    starts = range(0, width, HEAD)
    query = [load(qkv_ref, i) for i in starts]
    key = [load(qkv_ref, width + i) for i in starts]
    value = [load(qkv_ref, 2 * width + i) for i in starts]
    grad = [load(grad_ref, i) for i in starts]
    heads = range(len(query))
    scores = [jnp.where(allowed, dot_nt(query[h], key[h]) * scale, -1e30) for h in heads]
    grad_probs = [dot_nt(grad[h], value[h]) for h in heads]
    exponent = [jnp.exp(scores[h] - jnp.max(scores[h], -1, keepdims=True)) for h in heads]
    probabilities = [exponent[h] / jnp.sum(exponent[h], -1, keepdims=True) for h in heads]
    rounded = [probabilities[h].astype(jnp.bfloat16) for h in heads]
    mean_grad = [jnp.sum(grad_probs[h] * probabilities[h], -1, keepdims=True) for h in heads]
    mixed = [dot_nn(rounded[h], value[h]) for h in heads]
    grad_value = [dot_tn(rounded[h], grad[h]) for h in heads]
    grad_scores = [probabilities[h] * (grad_probs[h] - mean_grad[h]) for h in heads]
    high = [grad_scores[h].astype(jnp.bfloat16) for h in heads]
    low = [(grad_scores[h] - high[h].astype(jnp.float32)).astype(jnp.bfloat16) for h in heads]
    grad_query = [(dot_nn(high[h], key[h]) + dot_nn(low[h], key[h])) * scale for h in heads]
    grad_key = [(dot_tn(high[h], query[h]) + dot_tn(low[h], query[h])) * scale for h in heads]
    top_out, top_qkv = peak_ref[0], peak_ref[1]
    for h, start in enumerate(starts):
        store(mixed_ref, start, mixed[h])
        store(merged_ref, start, grad_query[h])
        store(merged_ref, width + start, grad_key[h])
        store(merged_ref, 2 * width + start, grad_value[h])
        top_out = jnp.maximum(top_out, peak(mixed[h]))
        for term in (grad_query[h], grad_key[h], grad_value[h]):
            top_qkv = jnp.maximum(top_qkv, peak(term))
    peak_ref[0] = top_out
    peak_ref[1] = top_qkv


def temporal_attention(qkv, grad_heads, times):
    frames, pairs, width = grad_heads.shape
    group = 16 if pairs % 16 == 0 else 8
    rows = frames * group
    per_row = jnp.repeat(times.astype(jnp.float32), group)
    work = pairs // group * rows * rows * (width // HEAD)
    fixed = lambda i: (0, 0)
    moving = lambda i: (0, i, 0)
    return pl.pallas_call(
        attention_kernel,
        grid=(pairs // group,),
        in_specs=[
            pl.BlockSpec((rows, 1), fixed),
            pl.BlockSpec((1, rows), fixed),
            pl.BlockSpec((frames, group, 3 * width), moving),
            pl.BlockSpec((frames, group, width), moving),
        ],
        out_specs=[
            pl.BlockSpec((frames, group, width), moving),
            pl.BlockSpec((frames, group, 3 * width), moving),
            pl.BlockSpec((2, 8, HEAD), lambda i: (0, 0, 0)),
        ],
        out_shape=[
            jax.ShapeDtypeStruct((frames, pairs, width), jnp.bfloat16),
            jax.ShapeDtypeStruct((frames, pairs, 3 * width), jnp.bfloat16),
            jax.ShapeDtypeStruct((2, 8, HEAD), jnp.float32),
        ],
        compiler_params=pltpu.CompilerParams(vmem_limit_bytes=16 * MIB),
        cost_estimate=pl.CostEstimate(
            flops=16 * work * HEAD,
            bytes_accessed=16 * frames * pairs * width,
            transcendentals=work,
        ),
        name="temporal_attention",
    )(per_row[:, None], per_row[None, :], qkv, grad_heads)


def turn_kernel(rows_ref, out_ref):
    out_ref[...] = rows_ref[...].T


def turn(rows):
    tokens, features = rows.shape
    tile = features // 8
    return pl.pallas_call(
        turn_kernel,
        grid=(8,),
        in_specs=[pl.BlockSpec((tokens, tile), lambda i: (0, i))],
        out_specs=pl.BlockSpec((tile, tokens), lambda i: (i, 0)),
        out_shape=jax.ShapeDtypeStruct((features, tokens), rows.dtype),
        compiler_params=pltpu.CompilerParams(vmem_limit_bytes=12 * MIB),
        cost_estimate=pl.CostEstimate(flops=1, bytes_accessed=1, transcendentals=0),
        name="turn",
    )(rows)


def weight_kernel(place_ref, norm_ref, up_ref, merged_ref, mixed_ref, near_ref, far_ref):
    step = pl.program_id(0)
    rows = near_ref.shape[0]
    first = place_ref[1] == 0

    def store(both):
        near_ref[...] = jnp.where(first, both[:rows], both[rows:])
        far_ref[...] = jnp.where(first, both[rows:], both[:rows])

    @pl.when(step < 3)
    def _():
        store(dot_nn(norm_ref[...], merged_ref[...]))

    @pl.when(step == 3)
    def _():
        store(dot_nn(up_ref[...], mixed_ref[...]))


def weight_product(places, rows, normed, upstream, merged, mixed):
    tokens, width = mixed.shape
    pair = pl.BlockSpec((2 * rows, tokens), lambda i, at: (at[0], 0))
    out = pl.BlockSpec((rows, width), lambda i, at: (0, i))
    return pl.pallas_call(
        weight_kernel,
        grid_spec=pltpu.PrefetchScalarGridSpec(
            num_scalar_prefetch=1,
            grid=(4,),
            in_specs=[
                pair,
                pair,
                pl.BlockSpec((tokens, width), lambda i, at: (0, jnp.minimum(i, 2))),
                pl.BlockSpec((tokens, width), lambda i, at: (0, 0)),
            ],
            out_specs=[out, out],
        ),
        out_shape=[jax.ShapeDtypeStruct((rows, 4 * width), jnp.float32)] * 2,
        compiler_params=pltpu.CompilerParams(vmem_limit_bytes=58 * MIB),
        cost_estimate=pl.CostEstimate(flops=1, bytes_accessed=1, transcendentals=0),
        name="weight_product",
    )(places, normed, upstream, merged, mixed)


def project_kernel(normed_ref, up_ref, weight_ref, qkv_ref, grad_ref):
    @pl.when(pl.program_id(0) < 3)
    def _():
        qkv_ref[...] = dot_nn(normed_ref[...], weight_ref[...]).astype(jnp.bfloat16)

    @pl.when(pl.program_id(0) == 3)
    def _():
        grad_ref[...] = dot_nn(up_ref[...], weight_ref[...]).astype(jnp.bfloat16)


def project(normed, upstream, weights):
    tokens, features = normed.shape
    width = weights.shape[1] // 4
    rows = tokens // 2
    return pl.pallas_call(
        project_kernel,
        grid=(4, 2),
        in_specs=[
            pl.BlockSpec((rows, features), lambda i, j: (jnp.where(i < 3, j, 1), 0)),
            pl.BlockSpec((rows, features), lambda i, j: (jnp.where(i < 3, 0, j), 0)),
            pl.BlockSpec((features, width), lambda i, j: (0, i)),
        ],
        out_specs=[
            pl.BlockSpec(
                (rows, width), lambda i, j: (jnp.where(i < 3, j, 1), jnp.minimum(i, 2))
            ),
            pl.BlockSpec((rows, width), lambda i, j: (jnp.where(i < 3, 0, j), 0)),
        ],
        out_shape=[
            jax.ShapeDtypeStruct((tokens, 3 * width), jnp.bfloat16),
            jax.ShapeDtypeStruct((tokens, width), jnp.bfloat16),
        ],
        compiler_params=pltpu.CompilerParams(vmem_limit_bytes=26 * MIB),
        cost_estimate=pl.CostEstimate(
            flops=2 * tokens * features * 4 * width,
            bytes_accessed=8 * tokens * features,
            transcendentals=0,
        ),
        name="project",
    )(normed, upstream, weights)


def norm_kernel(merged_ref, weight_ref, own_ref, other_ref):
    frames, pairs, tile = own_ref.shape
    rows = dot_nt(merged_ref[...], weight_ref[...]).reshape(frames, 2 * pairs, tile)
    own_ref[...] = rows[:, :pairs]
    other_ref[...] = rows[:, pairs:]


def norm_product(merged, weights, frames):
    rows, depth = merged.shape
    features = weights.shape[0]
    tile = features // 4
    pairs = rows // frames // 2
    out = pl.BlockSpec((frames, pairs, tile), lambda i: (0, 0, i))
    return pl.pallas_call(
        norm_kernel,
        grid=(4,),
        in_specs=[
            pl.BlockSpec((rows, depth), lambda i: (0, 0)),
            pl.BlockSpec((tile, depth), lambda i: (i, 0)),
        ],
        out_specs=[out, out],
        out_shape=[jax.ShapeDtypeStruct((frames, pairs, features), jnp.float32)] * 2,
        compiler_params=pltpu.CompilerParams(vmem_limit_bytes=26 * MIB),
        cost_estimate=pl.CostEstimate(flops=1, bytes_accessed=1, transcendentals=0),
        name="norm_product",
    )(merged, weights)


def on_device(
    depth, spaces, tensors, inputs, upstream, action_ids, frame_time, action_table, gain, w_qkv, w_out
):
    batch, local_frames, local_space, features = inputs.shape
    actions = action_table.shape[0]
    shard_rows, _, channels = w_qkv.shape
    z = lax.axis_index("frame")
    s = lax.axis_index("space")
    x = lax.axis_index("tensor")
    y, core = s // 2, s % 2
    frames = depth * local_frames
    pairs = batch * local_space // depth
    slots = depth // batch
    slice_width = features // tensors
    head_width = channels // 2
    width = 4 * head_width
    tokens = frames * 2 * pairs

    def ring(value, shift):
        return lax.ppermute(value, "frame", [(i, (i + shift) % depth) for i in range(depth)])

    def swap_z(value, bit):
        return lax.ppermute(value, "frame", [(i, i ^ bit) for i in range(depth)])

    def swap_core(value):
        return lax.ppermute(value, "space", [(i, i ^ 1) for i in range(spaces)])

    def swap_y(value):
        return lax.ppermute(value, "space", [(i, i ^ 2) for i in range(spaces)])

    def swap_x(value):
        return lax.ppermute(value, "tensor", [(0, 1), (1, 0)])

    def join_x(own, other=None):
        if tensors == 2:
            other = swap_x(own) if other is None else other
            first = jnp.where(x == 0, own, other)
            second = jnp.where(x == 0, other, own)
            return jnp.concatenate([first, second], -1)
        return lax.all_gather(own, "tensor", axis=own.ndim - 1, tiled=True)

    def cut_x(value, which=None):
        which = x if which is None else which
        return lax.dynamic_slice_in_dim(value, which * slice_width, slice_width, value.ndim - 1)

    def place(j):
        return j // slots, (j % slots) * pairs

    shards = [w_qkv[:, 0], w_qkv[:, 1], w_qkv[:, 2], w_out]

    def core_half(which):
        return jnp.concatenate(
            [jnp.where(which == 0, t[:, :head_width], t[:, head_width:]) for t in shards], 1
        )

    mine, sent = core_half(core), core_half(1 - core)
    other = swap_core(sent)
    block = jnp.concatenate(
        [jnp.where(core == 0, mine, other), jnp.where(core == 0, other, mine)], 0
    )

    def pieces(rows, k, start, size):
        rollout, first = place((z + k) % depth)
        return lax.dynamic_slice(
            rows, (rollout, 0, first, start), (1, local_frames, pairs, size)
        )[0]

    def collect(k, start):
        piece = jnp.stack([pieces(rows, k, start, slice_width) for rows in (inputs, upstream)])
        target, _ = place((z + k) % depth)
        ids = lax.dynamic_index_in_dim(action_ids, target, 0, keepdims=False)
        ids = jnp.broadcast_to(ids.astype(piece.dtype)[:, None], (local_frames, slice_width))
        ids = jnp.pad(ids, ((0, -local_frames % 8), (0, 0)))
        return ring(jnp.concatenate([piece.reshape(-1, slice_width), ids], 0), k)

    piece_shape = (2, local_frames, pairs, slice_width)
    piece_rows = 2 * local_frames * pairs

    def join_piece(own, other):
        ids = own[piece_rows : piece_rows + local_frames, 0].astype(jnp.int32)
        if other is not None:
            other = other[:piece_rows].reshape(piece_shape)
        return join_x(own[:piece_rows].reshape(piece_shape), other), ids

    def settle(weights, k, arrived, row):
        start = (z - k) % depth * (2 * block_rows) + row * block_rows
        return lax.dynamic_update_slice(weights, arrived, (start, 0))

    block_rows = 2 * shard_rows
    arrived = collect(1, x * slice_width)
    blocks, across, joined = [], [], []
    rollout, _ = place(z)
    all_ids = [lax.dynamic_index_in_dim(action_ids, rollout, 0, keepdims=False)]
    weights = after(jnp.zeros((features, width), jnp.bfloat16), arrived)
    for k in range(1, depth):
        blocks.append(block)
        across.append(swap_y(block))
        crossed = swap_x(arrived) if tensors == 2 else None
        piece, ids = join_piece(arrived, crossed)
        joined.append(piece)
        all_ids.append(ids)
        following = ring(block, 1)
        weights = settle(weights, k - 1, block, y)
        if k > 1:
            weights = settle(weights, k - 2, across[k - 2], 1 - y)
        earlier = [across[-1], joined[-1] if crossed is None else crossed]
        if k + 1 < depth:
            arrived = collect(k + 1, after(x * slice_width, block))
            following, arrived, weights, earlier = lax.optimization_barrier(
                (following, arrived, weights, earlier)
            )
        block = following
    locals_ = [pieces(rows, 0, 0, features) for rows in (inputs, upstream)]
    own_inputs = jnp.concatenate([locals_[0]] + [both_rows[0] for both_rows in joined], 0)
    own_upstream = jnp.concatenate([locals_[1]] + [both_rows[1] for both_rows in joined], 0)
    ids = jnp.concatenate(all_ids)
    order = (
        (z - jnp.arange(depth, dtype=jnp.int32)[:, None]) % depth * local_frames
        + jnp.arange(local_frames, dtype=jnp.int32)[None, :]
    ).reshape(frames)
    own_time = lax.dynamic_index_in_dim(frame_time, rollout, 0, keepdims=False)
    times = jnp.sum(
        jnp.where(
            order[:, None] == jnp.arange(frames, dtype=jnp.int32)[None, :], own_time[None, :], 0
        ),
        1,
    )
    onehot = (ids[:, None] == jnp.arange(actions, dtype=jnp.int32)[None, :]).astype(jnp.float32)
    embedded = jnp.dot(onehot, action_table, precision=lax.Precision.HIGHEST)
    hidden = own_inputs.astype(jnp.float32) + embedded[:, None, :]
    inverse = lax.rsqrt(jnp.mean(hidden * hidden, -1, keepdims=True) + NORM_EPSILON)
    normed = (hidden * inverse * gain).astype(jnp.bfloat16)

    block, normed, own_upstream, weights, near = lax.optimization_barrier(
        (block, normed, own_upstream, weights, across[-1])
    )
    far = swap_y(block)

    def both(own):
        return jnp.concatenate([own, swap_core(own)], 1).reshape(tokens, features)

    all_upstream = both(own_upstream)
    all_normed = both(normed)
    normed_t, upstream_t = turn(all_normed), turn(all_upstream)
    weights = settle(weights, depth - 2, near, 1 - y)
    weights = settle(weights, depth - 1, block, y)
    weights = settle(weights, depth - 1, after(far, normed_t, upstream_t), 1 - y)
    qkv, grad_heads = project(all_normed, all_upstream, weights)
    mixed, merged, peaks = temporal_attention(
        qkv.reshape(frames, 2 * pairs, 3 * head_width),
        grad_heads.reshape(frames, 2 * pairs, head_width),
        times,
    )
    flat_mixed = mixed.reshape(tokens, head_width)
    flat_merged = merged.reshape(tokens, 3 * head_width)

    peaks = jnp.max(peaks, (1, 2))
    own_bound = tokens * jnp.where(
        lax.broadcasted_iota(jnp.int32, (1, width), 1) < 3 * head_width,
        math.sqrt(features) * jnp.max(jnp.abs(gain)) * peaks[1],
        UPSTREAM_TOP * peaks[0],
    )
    own_bound = jnp.maximum(own_bound, 1e-20)

    def pack(value, bound):
        exponent = jnp.ceil(jnp.log2(bound / WIRE_TOP))
        row = lax.broadcasted_iota(jnp.int32, (block_rows + 8, 1), 0)
        padded = jnp.pad(value * jnp.exp2(-exponent), ((0, 8), (0, 0)))
        return jnp.where(row < block_rows, padded, exponent).astype(WIRE)

    def unpack(sent):
        scale = jnp.exp2(sent[block_rows : block_rows + 1].astype(jnp.float32))
        return sent[:block_rows].astype(jnp.float32) * scale, scale * WIRE_TOP

    def weight_part(k, earlier):
        places = jnp.stack([after((z - 1 - k) % depth, earlier), y])
        near, far = weight_product(
            places, block_rows, normed_t, upstream_t, flat_merged, flat_mixed
        )
        return near, pack(far, own_bound)

    def chip_sum(k, earlier):
        term, bound = unpack(after(swap_y(weight_parts[k][1]), earlier))
        return weight_parts[k][0] + term, bound + own_bound

    def ring_sum(k, arriving, earlier):
        total, bound = chip_sum(k, earlier)
        term, ring_bound = unpack(arriving)
        return total + term, bound + ring_bound

    weight_parts = [weight_part(0, flat_merged)]
    norm_here, norm_away = norm_product(
        after(flat_merged, weight_parts[0][1]), weights, frames
    )
    weight_parts.append(weight_part(1, norm_away))
    payload = pack(*chip_sum(0, weight_parts[1][1]))
    partial_norm = norm_here + swap_core(after(norm_away, payload))
    row_dot = jnp.sum(partial_norm * gain * (hidden * inverse), -1, keepdims=True)
    if tensors == 2:
        x_away = cut_x(partial_norm, 1 - x)
        row_scale = jnp.max(jnp.abs(partial_norm), -1, keepdims=True)
        row_scale = jnp.maximum(row_scale, 1e-20) / WIRE_TOP
        sent = (x_away / row_scale).astype(WIRE)
        row_terms = swap_x(jnp.concatenate([row_dot, row_scale], -1))
        x_terms = swap_x(sent)
    else:
        row_dot = lax.psum(row_dot, "tensor")
        grad_norm = lax.psum_scatter(partial_norm, "tensor", scatter_dimension=2, tiled=True)
        sent = partial_norm
    weight_parts.append(weight_part(2, sent))
    payload = pack(*ring_sum(1, ring(payload, 1), weight_parts[2][1]))
    weight_parts.append(weight_part(3, payload))
    if tensors == 2:
        x_terms, row_terms = after((x_terms, row_terms), weight_parts[3][1])
        row_dot = row_dot + row_terms[..., :1]
        grad_norm = cut_x(partial_norm) + x_terms.astype(jnp.float32) * row_terms[..., 1:]
    unit_rows = (cut_x(own_inputs).astype(jnp.float32) + cut_x(embedded)[:, None, :]) * inverse
    grad_hidden = cut_x(own_upstream).astype(jnp.float32) + inverse * (
        grad_norm * cut_x(gain) - unit_rows * (row_dot / features)
    )
    grad_rows = grad_hidden.astype(jnp.bfloat16)
    gain_term = jnp.sum(grad_norm * unit_rows, (0, 1))
    action_term = jnp.dot(
        onehot.T, jnp.sum(grad_hidden, 1), precision=lax.Precision.HIGHEST
    )
    small = jnp.concatenate([action_term, gain_term[None, :]], 0)
    small = small + swap_core(small)
    small = small + swap_z(small, 1)
    returned = [grad_rows[:local_frames]]
    for k in range(1, depth):
        returned.append(
            ring(grad_rows[k * local_frames : (k + 1) * local_frames], depth - k)
        )

    for k in range(2, depth - 1):
        payload = pack(*ring_sum(k, ring(payload, 1), (returned[1:], small)))
        if k + 2 < depth:
            weight_parts.append(weight_part(k + 2, payload))
    grad_inputs = jnp.zeros(inputs.shape, jnp.bfloat16)
    for k in range(depth):
        piece = after(returned[k], payload)
        target, first = place((z + k) % depth)
        grad_inputs = lax.dynamic_update_slice(
            grad_inputs, join_x(piece)[None], (target, 0, first, 0)
        )
    small = after(small, payload)
    bit = 2
    while bit < depth:
        small = small + after(swap_z(small, bit), grad_inputs)
        bit *= 2
    arriving, grad_inputs, small = lax.optimization_barrier(
        (ring(payload, 1), grad_inputs, small)
    )
    small = join_x(small + swap_y(small))
    total = chip_sum(depth - 1, arriving)[0] + unpack(arriving)[0]
    mine = lax.dynamic_slice_in_dim(total, core * shard_rows, shard_rows, 0)
    other = swap_core(lax.dynamic_slice_in_dim(total, (1 - core) * shard_rows, shard_rows, 0))
    first = jnp.where(core == 0, mine, other).reshape(shard_rows, 4, head_width)
    second = jnp.where(core == 0, other, mine).reshape(shard_rows, 4, head_width)
    joined = jnp.concatenate([first, second], 2)
    return (grad_inputs, joined[:, :3], joined[:, 3], small[actions], small[:actions])


def solution(mesh):
    sizes = mesh.shape
    return jax.shard_map(
        functools.partial(on_device, sizes["frame"], sizes["space"], sizes["tensor"]),
        mesh=mesh,
        in_specs=(
            P(None, "frame", "space", None),
            P(None, "frame", "space", None),
            P(None, "frame"),
            P(),
            P(),
            P(),
            P(("frame", "space"), None, "tensor"),
            P(("frame", "space"), "tensor"),
        ),
        out_specs=(
            P(None, "frame", "space", None),
            P(("frame", "space"), None, "tensor"),
            P(("frame", "space"), "tensor"),
            P(),
            P(),
        ),
        check_vma=False,
    )
```
